32 devices in a mesh: tm: 8 (over y, x, core), row: 4 (over z).
Axes of the slice: x: 2, y: 2, z: 4, core: 2. Of those that a mesh axis runs over, the one named last changes fastest.
Arguments:
- right_side: float32 [8, 256, 1024], P('tm', 'row'), may hold values from -6 to 6
- kappa: float32 [256, 1024], P('row'), may hold values from 0.5 to 8
Outputs:
- solution: float32 [8, 256, 1024], P('tm', 'row')
The draws below stay inside these ranges and needn't reach their ends.
All inputs are finite; a program needn't handle non-finite values.
Results may differ from the reference program's by a relative error of at most 0.0003.
Values sent between devices are 32-bit elements; how exact they have to be, the bound alone decides.
A program may use at most 64 MiB of HBM per device.

```python
import math
import jax
import jax.numpy as jnp
from jax import lax

NY = 1024
SWEEPS = 2
DEGREE = 4
NT = 8
NX = 256


def block_levels(key, dims, cuts, least, largest):
    def one(dim, parts):
        steps = jax.random.uniform(jax.random.fold_in(jax.random.fold_in(key, 6), dim), (parts,), jnp.float32, least / len(cuts), largest / len(cuts))
        return jnp.repeat(jnp.exp(steps), dims[dim] // parts).reshape((-1,) + (1,) * (len(dims) - dim - 1))

    loudness = one(*cuts[0])
    for cut in cuts[1:]:
        loudness = loudness * one(*cut)
    return loudness


def normal_values(own_key, shape, spread, bound, cuts=(), kind=jnp.bfloat16):
    values = spread * jax.random.normal(own_key, shape, jnp.float32)
    if cuts:
        values = values * block_levels(own_key, shape, cuts, -0.22, 0.18)
    return jnp.clip(values, -bound, bound).astype(kind)


def setup_inputs(seed: int = 0) -> dict:
    key_list = jax.random.split(jax.random.key(seed), 3)
    right_side = normal_values(key_list[0], (NT, NX, NY), 1.0, 6.0, ((0, 8), (1, 4)), jnp.float32)
    kappa = jnp.clip(jnp.exp(math.log(8.0) - 2.7725887 * jax.random.uniform(key_list[1], (NX, NY), jnp.float32) ** block_levels(key_list[1], (NX, NY), ((0, 4),), -0.2, 0.2)), 0.5, 8.0)
    return dict(right_side=right_side, kappa=kappa)


circulant_alpha = 0.05
courant_rows = 0.5
courant_cols = 0.25
cheb_centre = 1.0
cheb_half = 0.7


def step_weights(count):
    return [1.0 / (cheb_centre + cheb_half * math.cos(math.pi * (2 * number + 1) / (2 * count))) for number in range(count)]


def face_terms(kappa):
    padded = jnp.pad(kappa, 1)
    centre = padded[1:-1, 1:-1]
    north = 0.5 * (centre + padded[2:, 1:-1])
    south = 0.5 * (centre + padded[:-2, 1:-1])
    east = 0.5 * (centre + padded[1:-1, 2:])
    west = 0.5 * (centre + padded[1:-1, :-2])
    diagonal = north + south + east + west + (courant_rows + courant_cols)
    return north, south, east, west, diagonal


def spatial(field, faces):
    north, south, east, west, diagonal = faces
    padded = jnp.pad(field, ((0, 0), (1, 1), (1, 1)))
    centre = padded[:, 1:-1, 1:-1]
    above = padded[:, 2:, 1:-1]
    below = padded[:, :-2, 1:-1]
    after = padded[:, 1:-1, 2:]
    before = padded[:, 1:-1, :-2]
    coupled = north * above + south * below + east * after + west * before
    return diagonal * centre - coupled - courant_rows * below - courant_cols * before


def reference(right_side, kappa):
    faces = face_terms(kappa)
    diagonal = faces[4]
    steps = jnp.arange(NT, dtype=jnp.int32).astype(jnp.float32)
    log_alpha = math.log(circulant_alpha)
    scaled = right_side * jnp.exp(log_alpha * steps / NT)[:, None, None]
    spectrum = jnp.fft.fft(scaled, axis=0)
    spec_real = jnp.real(spectrum)
    spec_imag = jnp.imag(spectrum)
    decay = circulant_alpha ** (1.0 / NT)
    weights = step_weights(DEGREE)

    def solve_one(item):
        rhs_real, rhs_imag, frequency = item
        theta = (2.0 * math.pi / NT) * frequency.astype(jnp.float32)
        shift_real = 1.0 - decay * jnp.cos(theta)
        shift_imag = decay * jnp.sin(theta)
        diag_real = shift_real + diagonal
        magnitude = diag_real * diag_real + shift_imag * shift_imag
        inv_real = diag_real / magnitude
        inv_imag = -shift_imag / magnitude
        rhs = jnp.stack([rhs_real, rhs_imag])
        state = jnp.zeros_like(rhs)
        first = True
        for sweep in range(SWEEPS):
            for weight in weights:
                if first:
                    residual = rhs
                    first = False
                else:
                    image = spatial(state, faces)
                    image_real = shift_real * state[0] - shift_imag * state[1] + image[0]
                    image_imag = shift_real * state[1] + shift_imag * state[0] + image[1]
                    residual = rhs - jnp.stack([image_real, image_imag])
                corr_real = inv_real * residual[0] - inv_imag * residual[1]
                corr_imag = inv_real * residual[1] + inv_imag * residual[0]
                state = state + weight * jnp.stack([corr_real, corr_imag])
        return state[0], state[1]

    frequencies = jnp.arange(NT, dtype=jnp.int32)
    sol_real, sol_imag = lax.map(solve_one, (spec_real, spec_imag, frequencies))
    signal = jnp.real(jnp.fft.ifft(sol_real + 1j * sol_imag, axis=0))
    return signal * jnp.exp(-log_alpha * steps / NT)[:, None, None]
```

```python
import functools
import math

import jax
import jax.numpy as jnp
from jax import lax
from jax.experimental import pallas as pl
from jax.experimental.pallas import tpu as pltpu
from jax.sharding import PartitionSpec as P

SWEEPS = 2
DEGREE = 4


circulant_alpha = 0.05
courant_rows = 0.5
courant_cols = 0.25
cheb_centre = 1.0
cheb_half = 0.7


def from_partner(value, axis, bit):
    mask = 2**bit
    pairs = [(source, source ^ mask) for source in range(lax.axis_size(axis))]
    return lax.ppermute(value, axis, pairs)


def padded_2(block, sides, width):
    for axis, dim in sides:
        count = lax.axis_size(axis)
        forward = [(i, i + 1) for i in range(count - 1)]
        backward = [(target, source) for source, target in forward]
        low = lax.ppermute(
            lax.slice_in_dim(block, block.shape[dim] - width, None, axis=dim), axis, forward
        )
        high = lax.ppermute(lax.slice_in_dim(block, 0, width, axis=dim), axis, backward)
        block = jnp.concatenate([low, block, high], axis=dim)
    return block


def step_weights(count):
    return [
        1.0 / (cheb_centre + cheb_half * math.cos(math.pi * (2 * number + 1) / (2 * count)))
        for number in range(count)
    ]


def face_terms(kappa_rows):
    padded = jnp.pad(kappa_rows, ((0, 0), (1, 1)))
    centre = padded[1:-1, 1:-1]
    north = 0.5 * (centre + padded[2:, 1:-1])
    south = 0.5 * (centre + padded[:-2, 1:-1])
    east = 0.5 * (centre + padded[1:-1, 2:])
    west = 0.5 * (centre + padded[1:-1, :-2])
    diagonal = north + south + east + west + (courant_rows + courant_cols)
    return (north, south, east, west, diagonal)


def spatial(extended, faces):
    north, south, east, west, diagonal = faces
    padded = jnp.pad(extended, ((0, 0), (0, 0), (0, 0), (1, 1)))
    centre = padded[:, :, 1:-1, 1:-1]
    above = padded[:, :, 2:, 1:-1]
    below = padded[:, :, :-2, 1:-1]
    after = padded[:, :, 1:-1, 2:]
    before = padded[:, :, 1:-1, :-2]
    coupled = north * above + south * below + east * after + west * before
    return diagonal * centre - coupled - courant_rows * below - courant_cols * before


def rotate(pair, cosine, sine):
    return jnp.stack([pair[0] * cosine - pair[1] * sine, pair[0] * sine + pair[1] * cosine])


def short_transform(pair, sign):
    count = pair.shape[1]
    index = jnp.arange(count, dtype=jnp.int32)
    angles = 2.0 * math.pi / count * (index[:, None] * index[None, :] % count).astype(jnp.float32)
    cosine = jnp.cos(angles)
    sine = sign * jnp.sin(angles)
    highest = lax.Precision.HIGHEST
    real = jnp.einsum("kj,jrc->krc", cosine, pair[0], precision=highest) - jnp.einsum(
        "kj,jrc->krc", sine, pair[1], precision=highest
    )
    imag = jnp.einsum("kj,jrc->krc", cosine, pair[1], precision=highest) + jnp.einsum(
        "kj,jrc->krc", sine, pair[0], precision=highest
    )
    return jnp.stack([real, imag])


def bit_reversed(device, levels):
    total = jnp.zeros((), jnp.int32)
    for place in range(levels):
        total = total + device // 2**place % 2 * 2 ** (levels - 1 - place)
    return total


def forward_pairs(scaled, device, levels, tm_size, total_steps):
    place = levels - 1
    half = 2**place
    lower = device // half % 2 == 1
    angle = -math.pi / half * (device % half).astype(jnp.float32)
    partner = from_partner(scaled, "tm", place)
    summed = scaled + partner
    differ = partner - scaled
    real = jnp.where(lower, differ * jnp.cos(angle), summed)
    imag = jnp.where(lower, differ * jnp.sin(angle), jnp.zeros_like(summed))
    state = jnp.stack([real, imag])
    for place in range(levels - 2, -1, -1):
        half = 2**place
        lower = device // half % 2 == 1
        angle = -math.pi / half * (device % half).astype(jnp.float32)
        partner = from_partner(state, "tm", place)
        summed = state + partner
        rotated = rotate(partner - state, jnp.cos(angle), jnp.sin(angle))
        state = jnp.where(lower, rotated, summed)
    first_index = bit_reversed(device, levels)
    steps_dev = scaled.shape[0]
    local_steps = jnp.arange(steps_dev, dtype=jnp.int32)
    twist = (
        -2.0 * math.pi / total_steps * (local_steps * first_index % total_steps).astype(jnp.float32)
    )
    state = rotate(state, jnp.cos(twist)[:, None, None], jnp.sin(twist)[:, None, None])
    spectrum = short_transform(state, -1.0)
    frequencies = first_index + tm_size * local_steps
    return (spectrum, frequencies)


def backward_pairs(solved, device, levels, total_steps):
    steps_dev = solved.shape[1]
    first_index = bit_reversed(device, levels)
    state = short_transform(solved, 1.0) * (1.0 / steps_dev)
    local_steps = jnp.arange(steps_dev, dtype=jnp.int32)
    twist = (
        2.0 * math.pi / total_steps * (local_steps * first_index % total_steps).astype(jnp.float32)
    )
    state = rotate(state, jnp.cos(twist)[:, None, None], jnp.sin(twist)[:, None, None])
    for place in range(0, levels - 1):
        half = 2**place
        lower = device // half % 2 == 1
        angle = math.pi / half * (device % half).astype(jnp.float32)
        cosine = jnp.cos(angle)
        sine = jnp.sin(angle)
        partner = from_partner(state, "tm", place)
        upper_value = (state + rotate(partner, cosine, sine)) * 0.5
        lower_value = (partner - rotate(state, cosine, sine)) * 0.5
        state = jnp.where(lower, lower_value, upper_value)
    place = levels - 1
    half = 2**place
    lower = device // half % 2 == 1
    angle = math.pi / half * (device % half).astype(jnp.float32)
    own_turned = state[0] * jnp.cos(angle) - state[1] * jnp.sin(angle)
    outgoing = jnp.where(lower, own_turned, state[0])
    received = from_partner(outgoing, "tm", place)
    return jnp.where(lower, (received - own_turned) * 0.5, (state[0] + received) * 0.5)


def shift_terms(frequencies, faces, total_steps):
    decay = circulant_alpha ** (1.0 / total_steps)
    theta = 2.0 * math.pi / total_steps * frequencies.astype(jnp.float32)
    shift_real = (1.0 - decay * jnp.cos(theta))[:, None, None]
    shift_imag = (decay * jnp.sin(theta))[:, None, None]
    diag_real = shift_real + faces[4]
    magnitude = diag_real * diag_real + shift_imag * shift_imag
    return (shift_real, shift_imag, diag_real / magnitude, -shift_imag / magnitude)


def solve_each(spectrum, frequencies, kappa):
    total_steps = spectrum.shape[1] * lax.axis_size("tm")
    kappa_rows = padded_2(kappa, (("row", 0),), 1)
    faces = face_terms(kappa_rows)
    shift_real, shift_imag, inv_real, inv_imag = shift_terms(frequencies, faces, total_steps)
    state = jnp.zeros_like(spectrum)
    first = True
    for sweep in range(SWEEPS):
        for weight in step_weights(DEGREE):
            if first:
                residual = spectrum
                first = False
            else:
                extended = padded_2(state, (("row", 2),), 1)
                image = spatial(extended, faces)
                image_real = shift_real * state[0] - shift_imag * state[1] + image[0]
                image_imag = shift_real * state[1] + shift_imag * state[0] + image[1]
                residual = spectrum - jnp.stack([image_real, image_imag])
            corr_real = inv_real * residual[0] - inv_imag * residual[1]
            corr_imag = inv_real * residual[1] + inv_imag * residual[0]
            state = state + weight * jnp.stack([corr_real, corr_imag])
    return state


def solve_block(spectrum, frequencies, kappa):
    return solve_each(spectrum, frequencies, kappa)


def body(right_side, kappa):
    steps_dev = right_side.shape[0]
    tm_size = lax.axis_size("tm")
    total_steps = steps_dev * tm_size
    device = lax.axis_index("tm")
    local_steps = jnp.arange(steps_dev, dtype=jnp.int32)
    global_steps = device * steps_dev + local_steps
    log_alpha = math.log(circulant_alpha)
    step_float = global_steps.astype(jnp.float32)
    scaled = right_side * jnp.exp(log_alpha * step_float / total_steps)[:, None, None]
    levels = tm_size.bit_length() - 1
    spectrum, frequencies = forward_pairs(scaled, device, levels, tm_size, total_steps)
    solved = solve_block(spectrum, frequencies, kappa)
    signal = backward_pairs(solved, device, levels, total_steps)
    return signal * jnp.exp(-log_alpha * step_float / total_steps)[:, None, None]


LANES = 128
HALO = 8
SIDES = [(0, -1), (0, 1), (-1, 0), (-1, -1), (-1, 1), (1, 0), (1, -1), (1, 1)]


def patch_place(index):
    chip = index // 2
    return 2 * (chip + chip // 2 * (5 - 2 * chip)) + index % 2


def sublane_constants():
    field = lax.broadcasted_iota(jnp.int32, (8, LANES), 0)
    decay = circulant_alpha ** (1.0 / 8)
    real = jnp.full((8, LANES), 1.0 - decay, jnp.float32)
    turn = jnp.zeros((8, LANES), jnp.float32)
    real = jnp.where(field == 4, 1.0 + decay, real)
    for k in (1, 2, 3):
        theta = 2.0 * math.pi * k / 8
        both = field % 4 == k
        real = jnp.where(both, 1.0 - decay * math.cos(theta), real)
        sine = decay * math.sin(theta)
        turn = jnp.where(field == k, sine, jnp.where(field == k + 4, -sine, turn))
    return real, turn


def forward_eight(x):
    root = math.sqrt(0.5)
    s = [x[t] + x[t + 4] for t in range(4)]
    d = [x[t] - x[t + 4] for t in range(4)]
    even, odd = s[0] + s[2], s[1] + s[3]
    less, more = root * (d[1] - d[3]), root * (d[1] + d[3])
    return [
        even + odd, d[0] + less, s[0] - s[2], d[0] - less,
        even - odd, -d[2] - more, s[3] - s[1], d[2] - more,
    ]


def backward_eight(f):
    root = math.sqrt(0.5)
    x0, r1, r2, r3, x4, i1, i2, i3 = f
    plus, minus = x0 + x4, x0 - x4
    even = [plus + 2.0 * r2, minus - 2.0 * i2, plus - 2.0 * r2, minus + 2.0 * i2]
    less, total = r1 - r3, i1 + i3
    odd = [
        2.0 * (r1 + r3), 2.0 * root * (less - total),
        2.0 * (i3 - i1), -2.0 * root * (less + total),
    ]
    return [even[t] + odd[t] for t in range(4)] + [even[t] - odd[t] for t in range(4)]


def patch_kernel(
    rows, row_count, rhs, kappa, out,
    arrived, leaving, kap, b_m, b_s, v_a, v_b, u_a,
    coef, inv_r, inv_t, packed, from_left, from_right,
    go_s, go_r, back_s, back_r, halo_s, halo_r, kap_s, kap_r, local,
):
    mesh_id = pl.DeviceIdType.MESH
    me, z = lax.axis_index("tm"), lax.axis_index("row")
    p = patch_place(me)
    ext = rows + 2 * HALO
    groups = rows // 8

    def there(dp, dz):
        ok = None
        for delta, at, count in ((dp, p, 8), (dz, z, row_count)):
            if delta:
                good = at > 0 if delta < 0 else at < count - 1
                ok = good if ok is None else jnp.logical_and(ok, good)
        return ok

    def neighbour(dp, dz):
        return (patch_place((p + dp + 8) % 8), z + dz)

    barrier = pltpu.get_barrier_semaphore()
    for d in range(1, 8):
        pl.semaphore_signal(barrier, inc=1, device_id=((me + d) % 8, z), device_id_type=mesh_id)
    expected = jnp.int32(7)
    for dp, dz in SIDES:
        if dz == 0:
            continue
        ok = there(dp, dz)
        expected = expected + ok.astype(jnp.int32)

        @pl.when(ok)
        def _():
            pl.semaphore_signal(
                barrier, inc=1, device_id=neighbour(dp, dz), device_id_type=mesh_id
            )

    own_rhs = pltpu.make_async_copy(
        rhs.at[:, pl.ds(pl.multiple_of(p * LANES, LANES), LANES)], arrived.at[me], local.at[0]
    )
    own_kap = pltpu.make_async_copy(kappa, kap.at[pl.ds(HALO, rows)], local.at[1])
    own_rhs.start()
    own_kap.start()
    pl.semaphore_wait(barrier, expected)

    def go_copy(d):
        peer = (me + d) % 8
        columns = pl.ds(pl.multiple_of(patch_place(peer) * LANES, LANES), LANES)
        return pltpu.make_async_remote_copy(
            src_ref=rhs.at[:, columns], dst_ref=arrived.at[me],
            send_sem=go_s.at[d], recv_sem=go_r.at[d],
            device_id=(peer, z), device_id_type=mesh_id,
        )

    def go_arrival(d):
        peer = (me + 8 - d) % 8
        return pltpu.make_async_remote_copy(
            src_ref=rhs.at[:, pl.ds(0, LANES)], dst_ref=arrived.at[peer],
            send_sem=go_s.at[d], recv_sem=go_r.at[d],
            device_id=(peer, z), device_id_type=mesh_id,
        )

    def kap_copy(dz):
        first, last = (0, HALO + rows) if dz < 0 else (rows - HALO, 0)
        which = (dz + 1) // 2
        return pltpu.make_async_remote_copy(
            src_ref=kappa.at[pl.ds(first, HALO)], dst_ref=kap.at[pl.ds(last, HALO)],
            send_sem=kap_s.at[which], recv_sem=kap_r.at[which],
            device_id=(me, z + dz), device_id_type=mesh_id,
        )

    for dz in (-1, 1):
        @pl.when(there(0, dz))
        def _():
            kap_copy(dz).start()

    for d in range(1, 8):
        go_copy(d).start()

    own_kap.wait()
    for dz in (-1, 1):
        lost = HALO + rows if dz < 0 else 0

        @pl.when(there(0, -dz))
        def _():
            kap_copy(dz).wait_recv()

        @pl.when(jnp.logical_not(there(0, -dz)))
        def _():
            kap[pl.ds(lost, HALO), :] = jnp.zeros((HALO, kap.shape[1]), jnp.float32)

    lane = lax.broadcasted_iota(jnp.int32, (8, LANES), 1)
    lane_all = lax.broadcasted_iota(jnp.int32, (ext, LANES), 1)

    def kap_block(which):
        return kap[:, pl.ds(pl.multiple_of(which * LANES, LANES), LANES)]

    right_in = (p < 7).astype(jnp.float32)
    left_in = (p > 0).astype(jnp.float32)
    side_in = jnp.where(lane_all < 64, right_in, left_in)
    row_at = lax.broadcasted_iota(jnp.int32, (ext, LANES), 0)
    top_in = (z > 0).astype(jnp.float32)
    low_in = (z < row_count - 1).astype(jnp.float32)
    row_in = jnp.where(row_at < HALO, top_in, jnp.where(row_at >= HALO + rows, low_in, 1.0))
    k_m = kap_block(p)
    k_s = jnp.where(lane_all < 64, kap_block((p + 1) % 8), kap_block((p + 7) % 8)) * side_in
    turned = [pltpu.roll(k, 1, 1) for k in (k_m, k_s)]
    turned_up = [pltpu.roll(k, LANES - 1, 1) for k in (k_m, k_s)]
    for side, k in enumerate((k_m, k_s)):
        north = 0.5 * (k + pltpu.roll(k, ext - 1, 0))
        south = 0.5 * (k + pltpu.roll(k, 1, 0))
        east = 0.5 * (k + jnp.where(lane_all == LANES - 1, turned_up[1 - side], turned_up[side]))
        west = 0.5 * (k + jnp.where(lane_all == 0, turned[1 - side], turned[side]))
        diagonal = north + south + east + west + (courant_rows + courant_cols)
        inside = row_in if side == 0 else row_in * side_in
        parts = (north, south + courant_rows, east, west + courant_cols, diagonal, inside)
        for number, part in enumerate(parts):
            u_a[pl.ds((side * 6 + number) * ext, ext), :] = part

    shift_real, shift_turn = sublane_constants()
    shift_square = shift_turn * shift_turn

    def spread(g, carry):
        for side in range(2):
            tiles = [
                u_a[pl.ds(pl.multiple_of((side * 6 + number) * ext + 8 * g, 8), 8), :]
                for number in range(6)
            ]
            for i in range(8):
                at = pl.ds(pl.multiple_of(64 * g + 8 * i, 8), 8)
                wide = [jnp.broadcast_to(tile[i : i + 1, :], (8, LANES)) for tile in tiles]
                for number in range(4):
                    coef[side * 4 + number, at, :] = wide[number]
                diag_real = wide[4] + shift_real
                scale = wide[5] / (diag_real * diag_real + shift_square)
                inv_r[side, at, :] = diag_real * scale
                inv_t[side, at, :] = shift_turn * scale
        return carry

    lax.fori_loop(0, ext // 8, spread, 0)

    own_rhs.wait()
    for d in range(1, 8):
        go_arrival(d).wait_recv()

    log_alpha = math.log(circulant_alpha)

    def transform(g, carry):
        tile = pl.ds(pl.multiple_of(8 * g, 8), 8)
        steps = [arrived[t, tile, :] * math.exp(log_alpha * t / 8) for t in range(8)]
        for f, value in enumerate(forward_eight(steps)):
            b_m[pl.ds(64 * (g + 1) + f, 8, stride=8), :] = value
        edges = jnp.zeros((8, LANES), jnp.float32)
        for i in range(8):
            line = b_m[pl.ds(pl.multiple_of(64 * (g + 1) + 8 * i, 8), 8), :]
            edges = jnp.where(lane // 16 == i, pltpu.roll(line, 8 + 16 * i, 1), edges)
        packed[tile, :] = edges
        return carry

    lax.fori_loop(0, groups, transform, 0)

    def halo_copy(number):
        dp, dz = SIDES[number]
        if dp == 0:
            first = HALO if dz < 0 else rows
            source = b_m.at[pl.ds(8 * first, 8 * HALO)]
        else:
            first, count = {0: (0, groups), -1: (0, 1), 1: (groups - 1, 1)}[dz]
            source = packed.at[pl.ds(8 * first, 8 * count)]
        copy = pltpu.make_async_remote_copy(
            src_ref=source, dst_ref=halo_target(number),
            send_sem=halo_s.at[number], recv_sem=halo_r.at[number],
            device_id=neighbour(dp, dz), device_id_type=mesh_id,
        )
        return copy

    def halo_target(number):
        dp, dz = SIDES[number]
        if dp == 0:
            return b_m.at[pl.ds(8 * (HALO + rows if dz < 0 else 0), 8 * HALO)]
        last, count = {0: (1, groups), -1: (groups + 1, 1), 1: (0, 1)}[dz]
        return (from_right if dp < 0 else from_left).at[pl.ds(8 * last, 8 * count)]

    for number, (dp, dz) in enumerate(SIDES):
        @pl.when(there(dp, dz))
        def _():
            halo_copy(number).start()

    for number, (dp, dz) in enumerate(SIDES):
        @pl.when(there(-dp, -dz))
        def _():
            halo_copy(number).wait_recv()

        @pl.when(jnp.logical_not(there(-dp, -dz)))
        def _():
            target = halo_target(number)
            target[...] = jnp.zeros(target.shape, jnp.float32)

    weights = step_weights(DEGREE) * SWEEPS
    edge = jnp.zeros((8, LANES), jnp.float32)
    for ref in (v_a, v_b):
        for side in range(2):
            ref[side, pl.ds(0, 8), :] = edge
            ref[side, pl.ds(8 * (ext + 1), 8), :] = edge

    def begin(g, carry):
        tile = pl.ds(pl.multiple_of(8 * g, 8), 8)
        both = jnp.where(lane % 16 < 8, from_left[tile, :], from_right[tile, :])
        for i in range(8):
            at = pl.ds(pl.multiple_of(64 * g + 8 * i, 8), 8)
            after = pl.ds(pl.multiple_of(64 * g + 8 * i + 8, 8), 8)
            line = pltpu.roll(both, 120 - 16 * i, 1)
            b_s[at, :] = line
            for side, value in enumerate((b_m[at, :], line)):
                v_a[side, after, :] = weights[0] * (
                    inv_r[side, at, :] * value + inv_t[side, at, :] * pltpu.roll(value, 4, 0)
                )
        return carry

    lax.fori_loop(0, ext // 8, begin, 0)

    def step(old, new, weight, last):
        def body(g, carry):
            for i in range(8):
                at = pl.ds(pl.multiple_of(64 * g + 8 * i, 8), 8)
                mid = pl.ds(pl.multiple_of(64 * g + 8 * i + 8, 8), 8)
                above = pl.ds(pl.multiple_of(64 * g + 8 * i + 16, 8), 8)
                here = [old[side, mid, :] for side in range(2)]
                ups = [pltpu.roll(x, LANES - 1, 1) for x in here]
                downs = [pltpu.roll(x, 1, 1) for x in here]
                for side in range(1 if last else 2):
                    total = (b_m if side == 0 else b_s)[at, :]
                    total = total + coef[4 * side, at, :] * old[side, above, :]
                    total = total + coef[4 * side + 1, at, :] * old[side, at, :]
                    total = total + coef[4 * side + 2, at, :] * jnp.where(
                        lane == LANES - 1, ups[1 - side], ups[side]
                    )
                    total = total + coef[4 * side + 3, at, :] * jnp.where(
                        lane == 0, downs[1 - side], downs[side]
                    )
                    change = inv_r[side, at, :] * total + inv_t[side, at, :] * pltpu.roll(
                        total, 4, 0
                    )
                    new[side, mid, :] = (1.0 - weight) * here[side] + weight * change
            return carry

        if last:
            lax.fori_loop(1, groups + 1, body, 0)
        else:
            lax.fori_loop(0, ext // 8, body, 0)

    old, new = v_a, v_b
    for number in range(1, len(weights)):
        step(old, new, weights[number], number == len(weights) - 1)
        old, new = new, old

    def inverse(g, carry):
        tile = pl.ds(pl.multiple_of(8 * g, 8), 8)
        fields = [old[0, pl.ds(64 * (g + 1) + 8 + f, 8, stride=8), :] for f in range(8)]
        for t, value in enumerate(backward_eight(fields)):
            leaving[t, tile, :] = value * (math.exp(-log_alpha * t / 8) / 8)
        return carry

    lax.fori_loop(0, groups, inverse, 0)

    columns = pl.ds(pl.multiple_of(p * LANES, LANES), LANES)

    def back_copy(d):
        peer = (me + d) % 8
        return pltpu.make_async_remote_copy(
            src_ref=leaving.at[peer], dst_ref=out.at[:, columns],
            send_sem=back_s.at[d], recv_sem=back_r.at[d],
            device_id=(peer, z), device_id_type=mesh_id,
        )

    def back_arrival(d):
        peer = (me + 8 - d) % 8
        theirs = pl.ds(pl.multiple_of(patch_place(peer) * LANES, LANES), LANES)
        return pltpu.make_async_remote_copy(
            src_ref=leaving.at[peer], dst_ref=out.at[:, theirs],
            send_sem=back_s.at[d], recv_sem=back_r.at[d],
            device_id=(peer, z), device_id_type=mesh_id,
        )

    for d in range(1, 8):
        back_copy(d).start()
    own_out = pltpu.make_async_copy(leaving.at[me], out.at[:, columns], local.at[2])
    own_out.start()

    for dz in (-1, 1):
        @pl.when(there(0, dz))
        def _():
            kap_copy(dz).wait_send()

    for d in range(1, 8):
        go_copy(d).wait_send()
    for number, (dp, dz) in enumerate(SIDES):
        @pl.when(there(dp, dz))
        def _():
            halo_copy(number).wait_send()

    own_out.wait()
    for d in range(1, 8):
        back_arrival(d).wait_recv()
    for d in range(1, 8):
        back_copy(d).wait_send()


def patch_body(row_count, right_side, kappa):
    rows, width = kappa.shape
    ext = rows + 2 * HALO
    f32 = jnp.float32
    dma = pltpu.SemaphoreType.DMA
    result = pl.pallas_call(
        functools.partial(patch_kernel, rows, row_count),
        out_shape=jax.ShapeDtypeStruct((rows, width), f32),
        in_specs=[pl.BlockSpec(memory_space=pl.ANY)] * 2,
        out_specs=pl.BlockSpec(memory_space=pltpu.VMEM),
        scratch_shapes=[
            pltpu.VMEM((8, rows, LANES), f32),
            pltpu.VMEM((8, rows, LANES), f32),
            pltpu.VMEM((ext, width), f32),
            pltpu.VMEM((8 * ext, LANES), f32),
            pltpu.VMEM((8 * ext, LANES), f32),
            pltpu.VMEM((2, 8 * (ext + 2), LANES), f32),
            pltpu.VMEM((2, 8 * (ext + 2), LANES), f32),
            pltpu.VMEM((12 * ext, LANES), f32),
            pltpu.VMEM((8, 8 * ext, LANES), f32),
            pltpu.VMEM((2, 8 * ext, LANES), f32),
            pltpu.VMEM((2, 8 * ext, LANES), f32),
            pltpu.VMEM((rows, LANES), f32),
            pltpu.VMEM((ext, LANES), f32),
            pltpu.VMEM((ext, LANES), f32),
            dma((8,)), dma((8,)), dma((8,)), dma((8,)), dma((8,)), dma((8,)),
            dma((2,)), dma((2,)), dma((3,)),
        ],
        compiler_params=pltpu.CompilerParams(
            collective_id=0, has_side_effects=True, vmem_limit_bytes=24 * 2**20
        ),
        name="patch_solve",
    )(right_side.reshape(rows, width), kappa)
    return result.reshape(right_side.shape)


def solution(mesh):
    placed = (P("tm", "row", None), P("row", None))
    tm_size, row_count = mesh.shape["tm"], mesh.shape["row"]

    def local(right_side, kappa):
        fits = (
            tm_size == 8 and right_side.shape[0] == 1
            and kappa.shape[1] == tm_size * LANES and kappa.shape[0] % 8 == 0
        )
        if fits:
            return patch_body(row_count, right_side, kappa)
        return body(right_side, kappa)

    return jax.shard_map(
        local, mesh=mesh, in_specs=placed, out_specs=P("tm", "row", None), check_vma=False
    )
```

```python
import functools
import math

import jax
import jax.numpy as jnp
from jax import lax
from jax.experimental import pallas as pl
from jax.experimental.pallas import tpu as pltpu
from jax.sharding import PartitionSpec as P

SWEEPS = 2
DEGREE = 4


circulant_alpha = 0.05
courant_rows = 0.5
courant_cols = 0.25
cheb_centre = 1.0
cheb_half = 0.7


def from_partner(value, axis, bit):
    mask = 2**bit
    pairs = [(source, source ^ mask) for source in range(lax.axis_size(axis))]
    return lax.ppermute(value, axis, pairs)


def padded_2(block, sides, width):
    for axis, dim in sides:
        count = lax.axis_size(axis)
        forward = [(i, i + 1) for i in range(count - 1)]
        backward = [(target, source) for source, target in forward]
        low = lax.ppermute(
            lax.slice_in_dim(block, block.shape[dim] - width, None, axis=dim), axis, forward
        )
        high = lax.ppermute(lax.slice_in_dim(block, 0, width, axis=dim), axis, backward)
        block = jnp.concatenate([low, block, high], axis=dim)
    return block


def step_weights(count):
    return [
        1.0 / (cheb_centre + cheb_half * math.cos(math.pi * (2 * number + 1) / (2 * count)))
        for number in range(count)
    ]


def face_terms(kappa_rows):
    padded = jnp.pad(kappa_rows, ((0, 0), (1, 1)))
    centre = padded[1:-1, 1:-1]
    north = 0.5 * (centre + padded[2:, 1:-1])
    south = 0.5 * (centre + padded[:-2, 1:-1])
    east = 0.5 * (centre + padded[1:-1, 2:])
    west = 0.5 * (centre + padded[1:-1, :-2])
    diagonal = north + south + east + west + (courant_rows + courant_cols)
    return (north, south, east, west, diagonal)


def spatial(extended, faces):
    north, south, east, west, diagonal = faces
    padded = jnp.pad(extended, ((0, 0), (0, 0), (0, 0), (1, 1)))
    centre = padded[:, :, 1:-1, 1:-1]
    above = padded[:, :, 2:, 1:-1]
    below = padded[:, :, :-2, 1:-1]
    after = padded[:, :, 1:-1, 2:]
    before = padded[:, :, 1:-1, :-2]
    coupled = north * above + south * below + east * after + west * before
    return diagonal * centre - coupled - courant_rows * below - courant_cols * before


def rotate(pair, cosine, sine):
    return jnp.stack([pair[0] * cosine - pair[1] * sine, pair[0] * sine + pair[1] * cosine])


def short_transform(pair, sign):
    count = pair.shape[1]
    index = jnp.arange(count, dtype=jnp.int32)
    angles = 2.0 * math.pi / count * (index[:, None] * index[None, :] % count).astype(jnp.float32)
    cosine = jnp.cos(angles)
    sine = sign * jnp.sin(angles)
    highest = lax.Precision.HIGHEST
    real = jnp.einsum("kj,jrc->krc", cosine, pair[0], precision=highest) - jnp.einsum(
        "kj,jrc->krc", sine, pair[1], precision=highest
    )
    imag = jnp.einsum("kj,jrc->krc", cosine, pair[1], precision=highest) + jnp.einsum(
        "kj,jrc->krc", sine, pair[0], precision=highest
    )
    return jnp.stack([real, imag])


def bit_reversed(device, levels):
    total = jnp.zeros((), jnp.int32)
    for place in range(levels):
        total = total + device // 2**place % 2 * 2 ** (levels - 1 - place)
    return total


def forward_pairs(scaled, device, levels, tm_size, total_steps):
    place = levels - 1
    half = 2**place
    lower = device // half % 2 == 1
    angle = -math.pi / half * (device % half).astype(jnp.float32)
    partner = from_partner(scaled, "tm", place)
    summed = scaled + partner
    differ = partner - scaled
    real = jnp.where(lower, differ * jnp.cos(angle), summed)
    imag = jnp.where(lower, differ * jnp.sin(angle), jnp.zeros_like(summed))
    state = jnp.stack([real, imag])
    for place in range(levels - 2, -1, -1):
        half = 2**place
        lower = device // half % 2 == 1
        angle = -math.pi / half * (device % half).astype(jnp.float32)
        partner = from_partner(state, "tm", place)
        summed = state + partner
        rotated = rotate(partner - state, jnp.cos(angle), jnp.sin(angle))
        state = jnp.where(lower, rotated, summed)
    first_index = bit_reversed(device, levels)
    steps_dev = scaled.shape[0]
    local_steps = jnp.arange(steps_dev, dtype=jnp.int32)
    twist = (
        -2.0 * math.pi / total_steps * (local_steps * first_index % total_steps).astype(jnp.float32)
    )
    state = rotate(state, jnp.cos(twist)[:, None, None], jnp.sin(twist)[:, None, None])
    spectrum = short_transform(state, -1.0)
    frequencies = first_index + tm_size * local_steps
    return (spectrum, frequencies)


def backward_pairs(solved, device, levels, total_steps):
    steps_dev = solved.shape[1]
    first_index = bit_reversed(device, levels)
    state = short_transform(solved, 1.0) * (1.0 / steps_dev)
    local_steps = jnp.arange(steps_dev, dtype=jnp.int32)
    twist = (
        2.0 * math.pi / total_steps * (local_steps * first_index % total_steps).astype(jnp.float32)
    )
    state = rotate(state, jnp.cos(twist)[:, None, None], jnp.sin(twist)[:, None, None])
    for place in range(0, levels - 1):
        half = 2**place
        lower = device // half % 2 == 1
        angle = math.pi / half * (device % half).astype(jnp.float32)
        cosine = jnp.cos(angle)
        sine = jnp.sin(angle)
        partner = from_partner(state, "tm", place)
        upper_value = (state + rotate(partner, cosine, sine)) * 0.5
        lower_value = (partner - rotate(state, cosine, sine)) * 0.5
        state = jnp.where(lower, lower_value, upper_value)
    place = levels - 1
    half = 2**place
    lower = device // half % 2 == 1
    angle = math.pi / half * (device % half).astype(jnp.float32)
    own_turned = state[0] * jnp.cos(angle) - state[1] * jnp.sin(angle)
    outgoing = jnp.where(lower, own_turned, state[0])
    received = from_partner(outgoing, "tm", place)
    return jnp.where(lower, (received - own_turned) * 0.5, (state[0] + received) * 0.5)


def shift_terms(frequencies, faces, total_steps):
    decay = circulant_alpha ** (1.0 / total_steps)
    theta = 2.0 * math.pi / total_steps * frequencies.astype(jnp.float32)
    shift_real = (1.0 - decay * jnp.cos(theta))[:, None, None]
    shift_imag = (decay * jnp.sin(theta))[:, None, None]
    diag_real = shift_real + faces[4]
    magnitude = diag_real * diag_real + shift_imag * shift_imag
    return (shift_real, shift_imag, diag_real / magnitude, -shift_imag / magnitude)


def solve_each(spectrum, frequencies, kappa):
    total_steps = spectrum.shape[1] * lax.axis_size("tm")
    kappa_rows = padded_2(kappa, (("row", 0),), 1)
    faces = face_terms(kappa_rows)
    shift_real, shift_imag, inv_real, inv_imag = shift_terms(frequencies, faces, total_steps)
    state = jnp.zeros_like(spectrum)
    first = True
    for sweep in range(SWEEPS):
        for weight in step_weights(DEGREE):
            if first:
                residual = spectrum
                first = False
            else:
                extended = padded_2(state, (("row", 2),), 1)
                image = spatial(extended, faces)
                image_real = shift_real * state[0] - shift_imag * state[1] + image[0]
                image_imag = shift_real * state[1] + shift_imag * state[0] + image[1]
                residual = spectrum - jnp.stack([image_real, image_imag])
            corr_real = inv_real * residual[0] - inv_imag * residual[1]
            corr_imag = inv_real * residual[1] + inv_imag * residual[0]
            state = state + weight * jnp.stack([corr_real, corr_imag])
    return state


def solve_block(spectrum, frequencies, kappa):
    return solve_each(spectrum, frequencies, kappa)


def body(right_side, kappa):
    steps_dev = right_side.shape[0]
    tm_size = lax.axis_size("tm")
    total_steps = steps_dev * tm_size
    device = lax.axis_index("tm")
    local_steps = jnp.arange(steps_dev, dtype=jnp.int32)
    global_steps = device * steps_dev + local_steps
    log_alpha = math.log(circulant_alpha)
    step_float = global_steps.astype(jnp.float32)
    scaled = right_side * jnp.exp(log_alpha * step_float / total_steps)[:, None, None]
    levels = tm_size.bit_length() - 1
    spectrum, frequencies = forward_pairs(scaled, device, levels, tm_size, total_steps)
    solved = solve_block(spectrum, frequencies, kappa)
    signal = backward_pairs(solved, device, levels, total_steps)
    return signal * jnp.exp(-log_alpha * step_float / total_steps)[:, None, None]


LANES = 128
HALO = 8
SIDES = [(0, -1), (0, 1), (-1, 0), (-1, -1), (-1, 1), (1, 0), (1, -1), (1, 1)]


def patch_place(index):
    chip = index // 2
    return 2 * (chip + chip // 2 * (5 - 2 * chip)) + index % 2


def sublane_constants():
    field = lax.broadcasted_iota(jnp.int32, (8, LANES), 0) % 4
    decay = circulant_alpha ** (1.0 / 8)
    real = jnp.zeros((8, LANES), jnp.float32)
    turn = jnp.zeros((8, LANES), jnp.float32)
    for k in (1, 2, 3):
        theta = 2.0 * math.pi * k / 8
        real = jnp.where(field == k, 1.0 - decay * math.cos(theta), real)
        turn = jnp.where(field == k, decay * math.sin(theta), turn)
    real_a = jnp.where(field == 0, 1.0 - decay, real)
    real_b = jnp.where(field == 0, 1.0 + decay, real)
    return real_a, real_b, turn


def forward_eight(x):
    root = math.sqrt(0.5)
    s = [x[t] + x[t + 4] for t in range(4)]
    d = [x[t] - x[t + 4] for t in range(4)]
    even, odd = s[0] + s[2], s[1] + s[3]
    less, more = root * (d[1] - d[3]), root * (d[1] + d[3])
    return [
        even + odd, d[0] + less, s[0] - s[2], d[0] - less,
        even - odd, -d[2] - more, s[3] - s[1], d[2] - more,
    ]


def backward_eight(f):
    root = math.sqrt(0.5)
    x0, r1, r2, r3, x4, i1, i2, i3 = f
    plus, minus = x0 + x4, x0 - x4
    even = [plus + 2.0 * r2, minus - 2.0 * i2, plus - 2.0 * r2, minus + 2.0 * i2]
    less, total = r1 - r3, i1 + i3
    odd = [
        2.0 * (r1 + r3), 2.0 * root * (less - total),
        2.0 * (i3 - i1), -2.0 * root * (less + total),
    ]
    return [even[t] + odd[t] for t in range(4)] + [even[t] - odd[t] for t in range(4)]


def patch_kernel(
    rows, row_count, rhs, kappa, out,
    arrived, leaving, kap, rhs_f, v_a, v_b, u_a,
    coef, inv, packed, from_left, from_right, row_out, row_in_f,
    go_s, go_r, back_s, back_r, halo_s, halo_r, kap_s, kap_r, local,
):
    mesh_id = pl.DeviceIdType.MESH
    me, z = lax.axis_index("tm"), lax.axis_index("row")
    p = patch_place(me)
    ext = rows + 2 * HALO
    groups = rows // 8
    pairs = ext // 2

    def there(dp, dz):
        ok = None
        for delta, at, count in ((dp, p, 8), (dz, z, row_count)):
            if delta:
                good = at > 0 if delta < 0 else at < count - 1
                ok = good if ok is None else jnp.logical_and(ok, good)
        return ok

    def neighbour(dp, dz):
        return (patch_place((p + dp + 8) % 8), z + dz)

    barrier = pltpu.get_barrier_semaphore()
    for d in range(1, 8):
        pl.semaphore_signal(barrier, inc=1, device_id=((me + d) % 8, z), device_id_type=mesh_id)
    expected = jnp.int32(7)
    for dp, dz in SIDES:
        if dz == 0:
            continue
        ok = there(dp, dz)
        expected = expected + ok.astype(jnp.int32)

        @pl.when(ok)
        def _():
            pl.semaphore_signal(
                barrier, inc=1, device_id=neighbour(dp, dz), device_id_type=mesh_id
            )

    own_rhs = pltpu.make_async_copy(
        rhs.at[:, pl.ds(pl.multiple_of(p * LANES, LANES), LANES)], arrived.at[me], local.at[0]
    )
    own_kap = pltpu.make_async_copy(kappa, kap.at[pl.ds(HALO, rows)], local.at[1])
    own_rhs.start()
    own_kap.start()
    pl.semaphore_wait(barrier, expected)

    def go_copy(d):
        peer = (me + d) % 8
        columns = pl.ds(pl.multiple_of(patch_place(peer) * LANES, LANES), LANES)
        return pltpu.make_async_remote_copy(
            src_ref=rhs.at[:, columns], dst_ref=arrived.at[me],
            send_sem=go_s.at[d], recv_sem=go_r.at[d],
            device_id=(peer, z), device_id_type=mesh_id,
        )

    def go_arrival(d):
        peer = (me + 8 - d) % 8
        return pltpu.make_async_remote_copy(
            src_ref=rhs.at[:, pl.ds(0, LANES)], dst_ref=arrived.at[peer],
            send_sem=go_s.at[d], recv_sem=go_r.at[d],
            device_id=(peer, z), device_id_type=mesh_id,
        )

    def kap_copy(dz):
        first, last = (0, HALO + rows) if dz < 0 else (rows - HALO, 0)
        which = (dz + 1) // 2
        return pltpu.make_async_remote_copy(
            src_ref=kappa.at[pl.ds(first, HALO)], dst_ref=kap.at[pl.ds(last, HALO)],
            send_sem=kap_s.at[which], recv_sem=kap_r.at[which],
            device_id=(me, z + dz), device_id_type=mesh_id,
        )

    for dz in (-1, 1):
        @pl.when(there(0, dz))
        def _():
            kap_copy(dz).start()

    for d in range(1, 8):
        go_copy(d).start()

    own_kap.wait()
    for dz in (-1, 1):
        lost = HALO + rows if dz < 0 else 0

        @pl.when(there(0, -dz))
        def _():
            kap_copy(dz).wait_recv()

        @pl.when(jnp.logical_not(there(0, -dz)))
        def _():
            kap[pl.ds(lost, HALO), :] = jnp.zeros((HALO, kap.shape[1]), jnp.float32)

    lane = lax.broadcasted_iota(jnp.int32, (8, LANES), 1)
    lane_all = lax.broadcasted_iota(jnp.int32, (ext, LANES), 1)

    def kap_block(which):
        return kap[:, pl.ds(pl.multiple_of(which * LANES, LANES), LANES)]

    right_in = (p < 7).astype(jnp.float32)
    left_in = (p > 0).astype(jnp.float32)
    side_in = jnp.where(lane_all < 64, right_in, left_in)
    row_at = lax.broadcasted_iota(jnp.int32, (ext, LANES), 0)
    top_in = (z > 0).astype(jnp.float32)
    low_in = (z < row_count - 1).astype(jnp.float32)
    row_in = jnp.where(row_at < HALO, top_in, jnp.where(row_at >= HALO + rows, low_in, 1.0))
    k_m = kap_block(p)
    k_s = jnp.where(lane_all < 64, kap_block((p + 1) % 8), kap_block((p + 7) % 8)) * side_in
    turned = [pltpu.roll(k, 1, 1) for k in (k_m, k_s)]
    turned_up = [pltpu.roll(k, LANES - 1, 1) for k in (k_m, k_s)]
    for side, k in enumerate((k_m, k_s)):
        north = 0.5 * (k + pltpu.roll(k, ext - 1, 0))
        south = 0.5 * (k + pltpu.roll(k, 1, 0))
        east = 0.5 * (k + jnp.where(lane_all == LANES - 1, turned_up[1 - side], turned_up[side]))
        west = 0.5 * (k + jnp.where(lane_all == 0, turned[1 - side], turned[side]))
        diagonal = north + south + east + west + (courant_rows + courant_cols)
        inside = row_in if side == 0 else row_in * side_in
        parts = (north, south + courant_rows, east, west + courant_cols, diagonal, inside)
        for number, part in enumerate(parts):
            u_a[pl.ds((side * 6 + number) * ext, ext), :] = part

    shift_a, shift_b, shift_turn = sublane_constants()
    shift_square = shift_turn * shift_turn
    upper = lax.broadcasted_iota(jnp.int32, (8, LANES), 0) < 4

    def spread(g, carry):
        for side in range(2):
            both = [
                [
                    u_a[pl.ds(pl.multiple_of((side * 6 + number) * ext + half + 8 * g, 8), 8), :]
                    for half in (0, pairs)
                ]
                for number in range(6)
            ]
            for i in range(8):
                at = pl.ds(pl.multiple_of(64 * g + 8 * i, 8), 8)
                wide = [
                    jnp.where(
                        upper,
                        jnp.broadcast_to(first[i : i + 1, :], (8, LANES)),
                        jnp.broadcast_to(second[i : i + 1, :], (8, LANES)),
                    )
                    for first, second in both
                ]
                for number in range(4):
                    coef[side * 4 + number, at, :] = wide[number]
                diag_a, diag_b = wide[4] + shift_a, wide[4] + shift_b
                scale_a = wide[5] / (diag_a * diag_a + shift_square)
                scale_b = wide[5] / (diag_b * diag_b + shift_square)
                inv[side * 3, at, :] = diag_a * scale_a
                inv[side * 3 + 1, at, :] = diag_b * scale_b
                inv[side * 3 + 2, at, :] = shift_turn * scale_a
        return carry

    lax.fori_loop(0, pairs // 8, spread, 0)

    own_rhs.wait()
    for d in range(1, 8):
        go_arrival(d).wait_recv()

    log_alpha = math.log(circulant_alpha)

    def strided(row, f, pad):
        half, pair = row // pairs, row % pairs
        return pl.ds(8 * (pair + pad) + 4 * half + f % 4, 8, stride=8)

    for g in range(groups):
        tile = pl.ds(8 * g, 8)
        steps = [arrived[t, tile, :] * math.exp(log_alpha * t / 8) for t in range(8)]
        edges = jnp.zeros((8, LANES), jnp.float32)
        for f, value in enumerate(forward_eight(steps)):
            rhs_f[f // 4, strided(HALO + 8 * g, f, 0), :] = value
            edges = jnp.where(lane // 16 == f, pltpu.roll(value, 8 + 16 * f, 1), edges)
            if g == 0:
                row_out[0, f] = value
            if g == groups - 1:
                row_out[1, f] = value
        packed[tile, :] = edges

    def halo_copy(number):
        dp, dz = SIDES[number]
        if dp == 0:
            source = row_out.at[0 if dz < 0 else 1]
        else:
            first, count = {0: (0, groups), -1: (0, 1), 1: (groups - 1, 1)}[dz]
            source = packed.at[pl.ds(8 * first, 8 * count)]
        copy = pltpu.make_async_remote_copy(
            src_ref=source, dst_ref=halo_target(number),
            send_sem=halo_s.at[number], recv_sem=halo_r.at[number],
            device_id=neighbour(dp, dz), device_id_type=mesh_id,
        )
        return copy

    def halo_target(number):
        dp, dz = SIDES[number]
        if dp == 0:
            return row_in_f.at[1 if dz < 0 else 0]
        last, count = {0: (1, groups), -1: (groups + 1, 1), 1: (0, 1)}[dz]
        return (from_right if dp < 0 else from_left).at[pl.ds(8 * last, 8 * count)]

    for number, (dp, dz) in enumerate(SIDES):
        @pl.when(there(dp, dz))
        def _():
            halo_copy(number).start()

    for number, (dp, dz) in enumerate(SIDES):
        @pl.when(there(-dp, -dz))
        def _():
            halo_copy(number).wait_recv()

        @pl.when(jnp.logical_not(there(-dp, -dz)))
        def _():
            target = halo_target(number)
            target[...] = jnp.zeros(target.shape, jnp.float32)

    weights = step_weights(DEGREE) * SWEEPS
    for g in range(ext // 8):
        tile = pl.ds(8 * g, 8)
        both = jnp.where(lane % 16 < 8, from_left[tile, :], from_right[tile, :])
        for f in range(8):
            at = strided(8 * g, f, 0)
            rhs_f[2 + f // 4, at, :] = pltpu.roll(both, 120 - 16 * f, 1)
            if g == 0:
                rhs_f[f // 4, at, :] = row_in_f[0, f]
            if g == ext // 8 - 1:
                rhs_f[f // 4, at, :] = row_in_f[1, f]

    def close(ref):
        for which in range(4):
            ref[which, pl.ds(0, 8), :] = pltpu.roll(ref[which, pl.ds(8 * pairs, 8), :], 4, 0)
            ref[which, pl.ds(8 * pairs + 8, 8), :] = pltpu.roll(ref[which, pl.ds(8, 8), :], 4, 0)

    chunk = pairs // 2

    def begin(g, carry):
        for i in range(chunk):
            at = pl.ds(pl.multiple_of(8 * chunk * g + 8 * i, 8), 8)
            mid = pl.ds(pl.multiple_of(8 * chunk * g + 8 * i + 8, 8), 8)
            for side in range(2):
                a, b = rhs_f[2 * side, at, :], rhs_f[2 * side + 1, at, :]
                turn = inv[3 * side + 2, at, :]
                v_a[2 * side, mid, :] = weights[0] * (inv[3 * side, at, :] * a + turn * b)
                v_a[2 * side + 1, mid, :] = weights[0] * (inv[3 * side + 1, at, :] * b - turn * a)
        return carry

    lax.fori_loop(0, 2, begin, 0)
    close(v_a)

    def step(old, new, weight, last):
        def body(g, carry):
            def tile_of(which, i):
                return old[which, pl.ds(pl.multiple_of(8 * chunk * g + 8 * i, 8), 8), :]

            before = [tile_of(which, 0) for which in range(4)]
            here = [tile_of(which, 1) for which in range(4)]
            for i in range(chunk):
                at = pl.ds(pl.multiple_of(8 * chunk * g + 8 * i, 8), 8)
                mid = pl.ds(pl.multiple_of(8 * chunk * g + 8 * i + 8, 8), 8)
                after = [tile_of(which, i + 2) for which in range(4)]
                ups = [pltpu.roll(x, LANES - 1, 1) for x in here]
                downs = [pltpu.roll(x, 1, 1) for x in here]
                for side in range(1 if last else 2):
                    north, south, east, west = [coef[4 * side + n, at, :] for n in range(4)]
                    totals = []
                    for part in range(2):
                        own, other = 2 * side + part, 2 * (1 - side) + part
                        right = jnp.where(lane == LANES - 1, ups[other], ups[own])
                        left = jnp.where(lane == 0, downs[other], downs[own])
                        totals.append(
                            (rhs_f[own, at, :] + north * after[own])
                            + (south * before[own] + east * right)
                            + west * left
                        )
                    turn = inv[3 * side + 2, at, :]
                    changes = (
                        inv[3 * side, at, :] * totals[0] + turn * totals[1],
                        inv[3 * side + 1, at, :] * totals[1] - turn * totals[0],
                    )
                    for part in range(2):
                        own = 2 * side + part
                        new[own, mid, :] = (1.0 - weight) * here[own] + weight * changes[part]
                before, here = here, after
            return carry

        lax.fori_loop(0, 2, body, 0)
        if not last:
            close(new)

    old, new = v_a, v_b
    for number in range(1, len(weights)):
        step(old, new, weights[number], number == len(weights) - 1)
        old, new = new, old

    for g in range(groups):
        tile = pl.ds(8 * g, 8)
        fields = [old[f // 4, strided(HALO + 8 * g, f, 1), :] for f in range(8)]
        for t, value in enumerate(backward_eight(fields)):
            leaving[t, tile, :] = value * (math.exp(-log_alpha * t / 8) / 8)

    columns = pl.ds(pl.multiple_of(p * LANES, LANES), LANES)

    def back_copy(d):
        peer = (me + d) % 8
        return pltpu.make_async_remote_copy(
            src_ref=leaving.at[peer], dst_ref=out.at[:, columns],
            send_sem=back_s.at[d], recv_sem=back_r.at[d],
            device_id=(peer, z), device_id_type=mesh_id,
        )

    def back_arrival(d):
        peer = (me + 8 - d) % 8
        theirs = pl.ds(pl.multiple_of(patch_place(peer) * LANES, LANES), LANES)
        return pltpu.make_async_remote_copy(
            src_ref=leaving.at[peer], dst_ref=out.at[:, theirs],
            send_sem=back_s.at[d], recv_sem=back_r.at[d],
            device_id=(peer, z), device_id_type=mesh_id,
        )

    for d in range(1, 8):
        back_copy(d).start()
    own_out = pltpu.make_async_copy(leaving.at[me], out.at[:, columns], local.at[2])
    own_out.start()

    for dz in (-1, 1):
        @pl.when(there(0, dz))
        def _():
            kap_copy(dz).wait_send()

    for d in range(1, 8):
        go_copy(d).wait_send()
    for number, (dp, dz) in enumerate(SIDES):
        @pl.when(there(dp, dz))
        def _():
            halo_copy(number).wait_send()

    own_out.wait()
    for d in range(1, 8):
        back_arrival(d).wait_recv()
    for d in range(1, 8):
        back_copy(d).wait_send()


def patch_body(row_count, right_side, kappa):
    rows, width = kappa.shape
    ext = rows + 2 * HALO
    f32 = jnp.float32
    dma = pltpu.SemaphoreType.DMA
    result = pl.pallas_call(
        functools.partial(patch_kernel, rows, row_count),
        out_shape=jax.ShapeDtypeStruct((rows, width), f32),
        in_specs=[pl.BlockSpec(memory_space=pl.ANY)] * 2,
        out_specs=pl.BlockSpec(memory_space=pltpu.VMEM),
        scratch_shapes=[
            pltpu.VMEM((8, rows, LANES), f32),
            pltpu.VMEM((8, rows, LANES), f32),
            pltpu.VMEM((ext, width), f32),
            pltpu.VMEM((4, 4 * ext, LANES), f32),
            pltpu.VMEM((4, 4 * (ext + 4), LANES), f32),
            pltpu.VMEM((4, 4 * (ext + 4), LANES), f32),
            pltpu.VMEM((12 * ext, LANES), f32),
            pltpu.VMEM((8, 4 * ext, LANES), f32),
            pltpu.VMEM((6, 4 * ext, LANES), f32),
            pltpu.VMEM((rows, LANES), f32),
            pltpu.VMEM((ext, LANES), f32),
            pltpu.VMEM((ext, LANES), f32),
            pltpu.VMEM((2, 8, HALO, LANES), f32),
            pltpu.VMEM((2, 8, HALO, LANES), f32),
            dma((8,)), dma((8,)), dma((8,)), dma((8,)), dma((8,)), dma((8,)),
            dma((2,)), dma((2,)), dma((3,)),
        ],
        compiler_params=pltpu.CompilerParams(
            collective_id=0, has_side_effects=True, vmem_limit_bytes=60 * 2**20
        ),
        name="patch_solve",
    )(right_side.reshape(rows, width), kappa)
    return result.reshape(right_side.shape)


def solution(mesh):
    placed = (P("tm", "row", None), P("row", None))
    tm_size, row_count = mesh.shape["tm"], mesh.shape["row"]

    def local(right_side, kappa):
        fits = (
            tm_size == 8 and right_side.shape[0] == 1
            and kappa.shape[1] == tm_size * LANES and kappa.shape[0] % 16 == 0
        )
        if fits:
            return patch_body(row_count, right_side, kappa)
        return body(right_side, kappa)

    return jax.shard_map(
        local, mesh=mesh, in_specs=placed, out_specs=P("tm", "row", None), check_vma=False
    )
```

```python
import functools
import math

import jax
import jax.numpy as jnp
from jax import lax
from jax.experimental import pallas as pl
from jax.experimental.pallas import tpu as pltpu
from jax.sharding import PartitionSpec as P

SWEEPS = 2
DEGREE = 4


circulant_alpha = 0.05
courant_rows = 0.5
courant_cols = 0.25
cheb_centre = 1.0
cheb_half = 0.7


def from_partner(value, axis, bit):
    mask = 2**bit
    pairs = [(source, source ^ mask) for source in range(lax.axis_size(axis))]
    return lax.ppermute(value, axis, pairs)


def padded_2(block, sides, width):
    for axis, dim in sides:
        count = lax.axis_size(axis)
        forward = [(i, i + 1) for i in range(count - 1)]
        backward = [(target, source) for source, target in forward]
        low = lax.ppermute(
            lax.slice_in_dim(block, block.shape[dim] - width, None, axis=dim), axis, forward
        )
        high = lax.ppermute(lax.slice_in_dim(block, 0, width, axis=dim), axis, backward)
        block = jnp.concatenate([low, block, high], axis=dim)
    return block


def step_weights(count):
    return [
        1.0 / (cheb_centre + cheb_half * math.cos(math.pi * (2 * number + 1) / (2 * count)))
        for number in range(count)
    ]


def face_terms(kappa_rows):
    padded = jnp.pad(kappa_rows, ((0, 0), (1, 1)))
    centre = padded[1:-1, 1:-1]
    north = 0.5 * (centre + padded[2:, 1:-1])
    south = 0.5 * (centre + padded[:-2, 1:-1])
    east = 0.5 * (centre + padded[1:-1, 2:])
    west = 0.5 * (centre + padded[1:-1, :-2])
    diagonal = north + south + east + west + (courant_rows + courant_cols)
    return (north, south, east, west, diagonal)


def spatial(extended, faces):
    north, south, east, west, diagonal = faces
    padded = jnp.pad(extended, ((0, 0), (0, 0), (0, 0), (1, 1)))
    centre = padded[:, :, 1:-1, 1:-1]
    above = padded[:, :, 2:, 1:-1]
    below = padded[:, :, :-2, 1:-1]
    after = padded[:, :, 1:-1, 2:]
    before = padded[:, :, 1:-1, :-2]
    coupled = north * above + south * below + east * after + west * before
    return diagonal * centre - coupled - courant_rows * below - courant_cols * before


def rotate(pair, cosine, sine):
    return jnp.stack([pair[0] * cosine - pair[1] * sine, pair[0] * sine + pair[1] * cosine])


def short_transform(pair, sign):
    count = pair.shape[1]
    index = jnp.arange(count, dtype=jnp.int32)
    angles = 2.0 * math.pi / count * (index[:, None] * index[None, :] % count).astype(jnp.float32)
    cosine = jnp.cos(angles)
    sine = sign * jnp.sin(angles)
    highest = lax.Precision.HIGHEST
    real = jnp.einsum("kj,jrc->krc", cosine, pair[0], precision=highest) - jnp.einsum(
        "kj,jrc->krc", sine, pair[1], precision=highest
    )
    imag = jnp.einsum("kj,jrc->krc", cosine, pair[1], precision=highest) + jnp.einsum(
        "kj,jrc->krc", sine, pair[0], precision=highest
    )
    return jnp.stack([real, imag])


def bit_reversed(device, levels):
    total = jnp.zeros((), jnp.int32)
    for place in range(levels):
        total = total + device // 2**place % 2 * 2 ** (levels - 1 - place)
    return total


def forward_pairs(scaled, device, levels, tm_size, total_steps):
    place = levels - 1
    half = 2**place
    lower = device // half % 2 == 1
    angle = -math.pi / half * (device % half).astype(jnp.float32)
    partner = from_partner(scaled, "tm", place)
    summed = scaled + partner
    differ = partner - scaled
    real = jnp.where(lower, differ * jnp.cos(angle), summed)
    imag = jnp.where(lower, differ * jnp.sin(angle), jnp.zeros_like(summed))
    state = jnp.stack([real, imag])
    for place in range(levels - 2, -1, -1):
        half = 2**place
        lower = device // half % 2 == 1
        angle = -math.pi / half * (device % half).astype(jnp.float32)
        partner = from_partner(state, "tm", place)
        summed = state + partner
        rotated = rotate(partner - state, jnp.cos(angle), jnp.sin(angle))
        state = jnp.where(lower, rotated, summed)
    first_index = bit_reversed(device, levels)
    steps_dev = scaled.shape[0]
    local_steps = jnp.arange(steps_dev, dtype=jnp.int32)
    twist = (
        -2.0 * math.pi / total_steps * (local_steps * first_index % total_steps).astype(jnp.float32)
    )
    state = rotate(state, jnp.cos(twist)[:, None, None], jnp.sin(twist)[:, None, None])
    spectrum = short_transform(state, -1.0)
    frequencies = first_index + tm_size * local_steps
    return (spectrum, frequencies)


def backward_pairs(solved, device, levels, total_steps):
    steps_dev = solved.shape[1]
    first_index = bit_reversed(device, levels)
    state = short_transform(solved, 1.0) * (1.0 / steps_dev)
    local_steps = jnp.arange(steps_dev, dtype=jnp.int32)
    twist = (
        2.0 * math.pi / total_steps * (local_steps * first_index % total_steps).astype(jnp.float32)
    )
    state = rotate(state, jnp.cos(twist)[:, None, None], jnp.sin(twist)[:, None, None])
    for place in range(0, levels - 1):
        half = 2**place
        lower = device // half % 2 == 1
        angle = math.pi / half * (device % half).astype(jnp.float32)
        cosine = jnp.cos(angle)
        sine = jnp.sin(angle)
        partner = from_partner(state, "tm", place)
        upper_value = (state + rotate(partner, cosine, sine)) * 0.5
        lower_value = (partner - rotate(state, cosine, sine)) * 0.5
        state = jnp.where(lower, lower_value, upper_value)
    place = levels - 1
    half = 2**place
    lower = device // half % 2 == 1
    angle = math.pi / half * (device % half).astype(jnp.float32)
    own_turned = state[0] * jnp.cos(angle) - state[1] * jnp.sin(angle)
    outgoing = jnp.where(lower, own_turned, state[0])
    received = from_partner(outgoing, "tm", place)
    return jnp.where(lower, (received - own_turned) * 0.5, (state[0] + received) * 0.5)


def shift_terms(frequencies, faces, total_steps):
    decay = circulant_alpha ** (1.0 / total_steps)
    theta = 2.0 * math.pi / total_steps * frequencies.astype(jnp.float32)
    shift_real = (1.0 - decay * jnp.cos(theta))[:, None, None]
    shift_imag = (decay * jnp.sin(theta))[:, None, None]
    diag_real = shift_real + faces[4]
    magnitude = diag_real * diag_real + shift_imag * shift_imag
    return (shift_real, shift_imag, diag_real / magnitude, -shift_imag / magnitude)


def solve_each(spectrum, frequencies, kappa):
    total_steps = spectrum.shape[1] * lax.axis_size("tm")
    kappa_rows = padded_2(kappa, (("row", 0),), 1)
    faces = face_terms(kappa_rows)
    shift_real, shift_imag, inv_real, inv_imag = shift_terms(frequencies, faces, total_steps)
    state = jnp.zeros_like(spectrum)
    first = True
    for sweep in range(SWEEPS):
        for weight in step_weights(DEGREE):
            if first:
                residual = spectrum
                first = False
            else:
                extended = padded_2(state, (("row", 2),), 1)
                image = spatial(extended, faces)
                image_real = shift_real * state[0] - shift_imag * state[1] + image[0]
                image_imag = shift_real * state[1] + shift_imag * state[0] + image[1]
                residual = spectrum - jnp.stack([image_real, image_imag])
            corr_real = inv_real * residual[0] - inv_imag * residual[1]
            corr_imag = inv_real * residual[1] + inv_imag * residual[0]
            state = state + weight * jnp.stack([corr_real, corr_imag])
    return state


def solve_block(spectrum, frequencies, kappa):
    return solve_each(spectrum, frequencies, kappa)


def body(right_side, kappa):
    steps_dev = right_side.shape[0]
    tm_size = lax.axis_size("tm")
    total_steps = steps_dev * tm_size
    device = lax.axis_index("tm")
    local_steps = jnp.arange(steps_dev, dtype=jnp.int32)
    global_steps = device * steps_dev + local_steps
    log_alpha = math.log(circulant_alpha)
    step_float = global_steps.astype(jnp.float32)
    scaled = right_side * jnp.exp(log_alpha * step_float / total_steps)[:, None, None]
    levels = tm_size.bit_length() - 1
    spectrum, frequencies = forward_pairs(scaled, device, levels, tm_size, total_steps)
    solved = solve_block(spectrum, frequencies, kappa)
    signal = backward_pairs(solved, device, levels, total_steps)
    return signal * jnp.exp(-log_alpha * step_float / total_steps)[:, None, None]


LANES = 128
HALO = 8
SIDES = [(0, -1), (0, 1), (-1, 0), (-1, -1), (-1, 1), (1, 0), (1, -1), (1, 1)]


def patch_place(index):
    chip = index // 2
    return 2 * (chip + chip // 2 * (5 - 2 * chip)) + index % 2


def sublane_constants():
    field = lax.broadcasted_iota(jnp.int32, (8, LANES), 0) % 4
    decay = circulant_alpha ** (1.0 / 8)
    real = jnp.zeros((8, LANES), jnp.float32)
    turn = jnp.zeros((8, LANES), jnp.float32)
    for k in (1, 2, 3):
        theta = 2.0 * math.pi * k / 8
        real = jnp.where(field == k, 1.0 - decay * math.cos(theta), real)
        turn = jnp.where(field == k, decay * math.sin(theta), turn)
    real_a = jnp.where(field == 0, 1.0 - decay, real)
    real_b = jnp.where(field == 0, 1.0 + decay, real)
    return real_a, real_b, turn


def forward_eight(x):
    root = math.sqrt(0.5)
    s = [x[t] + x[t + 4] for t in range(4)]
    d = [x[t] - x[t + 4] for t in range(4)]
    even, odd = s[0] + s[2], s[1] + s[3]
    less, more = root * (d[1] - d[3]), root * (d[1] + d[3])
    return [
        even + odd, d[0] + less, s[0] - s[2], d[0] - less,
        even - odd, -d[2] - more, s[3] - s[1], d[2] - more,
    ]


def backward_eight(f):
    root = math.sqrt(0.5)
    x0, r1, r2, r3, x4, i1, i2, i3 = f
    plus, minus = x0 + x4, x0 - x4
    even = [plus + 2.0 * r2, minus - 2.0 * i2, plus - 2.0 * r2, minus + 2.0 * i2]
    less, total = r1 - r3, i1 + i3
    odd = [
        2.0 * (r1 + r3), 2.0 * root * (less - total),
        2.0 * (i3 - i1), -2.0 * root * (less + total),
    ]
    return [even[t] + odd[t] for t in range(4)] + [even[t] - odd[t] for t in range(4)]


def patch_kernel(
    rows, row_count, rhs, kappa, out,
    arrived, leaving, kap, rhs_f, v_a, v_b, u_a,
    coef, inv, side_f, side_a, side_b, coef_s, inv_s, packed, from_left, from_right, row_out, row_in_f,
    go_s, go_r, back_s, back_r, halo_s, halo_r, kap_s, kap_r, local,
):
    mesh_id = pl.DeviceIdType.MESH
    me, z = lax.axis_index("tm"), lax.axis_index("row")
    p = patch_place(me)
    ext = rows + 2 * HALO
    groups = rows // 8
    pairs = ext // 2
    packs = pairs // 8

    def there(dp, dz):
        ok = None
        for delta, at, count in ((dp, p, 8), (dz, z, row_count)):
            if delta:
                good = at > 0 if delta < 0 else at < count - 1
                ok = good if ok is None else jnp.logical_and(ok, good)
        return ok

    def neighbour(dp, dz):
        return (patch_place((p + dp + 8) % 8), z + dz)

    barrier = pltpu.get_barrier_semaphore()
    for d in range(1, 8):
        pl.semaphore_signal(barrier, inc=1, device_id=((me + d) % 8, z), device_id_type=mesh_id)
    expected = jnp.int32(7)
    for dp, dz in SIDES:
        if dz == 0:
            continue
        ok = there(dp, dz)
        expected = expected + ok.astype(jnp.int32)

        @pl.when(ok)
        def _():
            pl.semaphore_signal(
                barrier, inc=1, device_id=neighbour(dp, dz), device_id_type=mesh_id
            )

    own_rhs = pltpu.make_async_copy(
        rhs.at[:, pl.ds(pl.multiple_of(p * LANES, LANES), LANES)], arrived.at[me], local.at[0]
    )
    own_kap = pltpu.make_async_copy(kappa, kap.at[pl.ds(HALO, rows)], local.at[1])
    own_rhs.start()
    own_kap.start()
    pl.semaphore_wait(barrier, expected)

    def go_copy(d):
        peer = (me + d) % 8
        columns = pl.ds(pl.multiple_of(patch_place(peer) * LANES, LANES), LANES)
        return pltpu.make_async_remote_copy(
            src_ref=rhs.at[:, columns], dst_ref=arrived.at[me],
            send_sem=go_s.at[d], recv_sem=go_r.at[d],
            device_id=(peer, z), device_id_type=mesh_id,
        )

    def go_arrival(d):
        peer = (me + 8 - d) % 8
        return pltpu.make_async_remote_copy(
            src_ref=rhs.at[:, pl.ds(0, LANES)], dst_ref=arrived.at[peer],
            send_sem=go_s.at[d], recv_sem=go_r.at[d],
            device_id=(peer, z), device_id_type=mesh_id,
        )

    def kap_copy(dz):
        first, last = (0, HALO + rows) if dz < 0 else (rows - HALO, 0)
        which = (dz + 1) // 2
        return pltpu.make_async_remote_copy(
            src_ref=kappa.at[pl.ds(first, HALO)], dst_ref=kap.at[pl.ds(last, HALO)],
            send_sem=kap_s.at[which], recv_sem=kap_r.at[which],
            device_id=(me, z + dz), device_id_type=mesh_id,
        )

    for dz in (-1, 1):
        @pl.when(there(0, dz))
        def _():
            kap_copy(dz).start()

    for d in range(1, 8):
        go_copy(d).start()

    own_kap.wait()
    for dz in (-1, 1):
        lost = HALO + rows if dz < 0 else 0

        @pl.when(there(0, -dz))
        def _():
            kap_copy(dz).wait_recv()

        @pl.when(jnp.logical_not(there(0, -dz)))
        def _():
            kap[pl.ds(lost, HALO), :] = jnp.zeros((HALO, kap.shape[1]), jnp.float32)

    lane = lax.broadcasted_iota(jnp.int32, (8, LANES), 1)
    lane_all = lax.broadcasted_iota(jnp.int32, (ext, LANES), 1)

    def kap_block(which):
        return kap[:, pl.ds(pl.multiple_of(which * LANES, LANES), LANES)]

    right_in = (p < 7).astype(jnp.float32)
    left_in = (p > 0).astype(jnp.float32)
    side_in = jnp.where(lane_all < 64, right_in, left_in)
    row_at = lax.broadcasted_iota(jnp.int32, (ext, LANES), 0)
    top_in = (z > 0).astype(jnp.float32)
    low_in = (z < row_count - 1).astype(jnp.float32)
    row_in = jnp.where(row_at < HALO, top_in, jnp.where(row_at >= HALO + rows, low_in, 1.0))
    k_m = kap_block(p)
    k_s = jnp.where(lane_all < 64, kap_block((p + 1) % 8), kap_block((p + 7) % 8)) * side_in
    turned = [pltpu.roll(k, 1, 1) for k in (k_m, k_s)]
    turned_up = [pltpu.roll(k, LANES - 1, 1) for k in (k_m, k_s)]
    for side, k in enumerate((k_m, k_s)):
        north = 0.5 * (k + pltpu.roll(k, ext - 1, 0))
        south = 0.5 * (k + pltpu.roll(k, 1, 0))
        east = 0.5 * (k + jnp.where(lane_all == LANES - 1, turned_up[1 - side], turned_up[side]))
        west = 0.5 * (k + jnp.where(lane_all == 0, turned[1 - side], turned[side]))
        diagonal = north + south + east + west + (courant_rows + courant_cols)
        inside = row_in if side == 0 else row_in * side_in
        parts = (north, south + courant_rows, east, west + courant_cols, diagonal, inside)
        for number, part in enumerate(parts):
            u_a[pl.ds((side * 6 + number) * ext, ext), :] = part

    shift_a, shift_b, shift_turn = sublane_constants()
    shift_square = shift_turn * shift_turn
    upper = lax.broadcasted_iota(jnp.int32, (8, LANES), 0) < 4

    def inverses(wide, scale):
        diag_a, diag_b = wide + shift_a, wide + shift_b
        scale_a = scale / (diag_a * diag_a + shift_square)
        scale_b = scale / (diag_b * diag_b + shift_square)
        return diag_a * scale_a, diag_b * scale_b, shift_turn * scale_a

    def spread(g, carry):
        both = [
            [
                u_a[pl.ds(pl.multiple_of(number * ext + half + 8 * g, 8), 8), :]
                for half in (0, pairs)
            ]
            for number in range(6)
        ]
        for i in range(8):
            at = pl.ds(pl.multiple_of(64 * g + 8 * i, 8), 8)
            wide = [
                jnp.where(
                    upper,
                    jnp.broadcast_to(first[i : i + 1, :], (8, LANES)),
                    jnp.broadcast_to(second[i : i + 1, :], (8, LANES)),
                )
                for first, second in both
            ]
            for number in range(4):
                coef[number, at, :] = wide[number]
            for number, value in enumerate(inverses(wide[4], wide[5])):
                inv[number, at, :] = value
        return carry

    lax.fori_loop(0, pairs // 8, spread, 0)

    for jj in range(packs):
        wide = []
        for number in range(6):
            total = jnp.zeros((8, LANES), jnp.float32)
            for m in range(8):
                row = (6 + number) * ext + jj + packs * m
                line = jnp.where(
                    upper,
                    jnp.broadcast_to(u_a[pl.ds(row, 1), :], (8, LANES)),
                    jnp.broadcast_to(u_a[pl.ds(row + pairs, 1), :], (8, LANES)),
                )
                total = jnp.where(lane // 16 == m, pltpu.roll(line, (16 * m + 8) % LANES, 1), total)
            wide.append(total)
        at = pl.ds(8 * jj, 8)
        for number in range(4):
            coef_s[number, at, :] = wide[number]
        for number, value in enumerate(inverses(wide[4], wide[5])):
            inv_s[number, at, :] = value

    own_rhs.wait()
    for d in range(1, 8):
        go_arrival(d).wait_recv()

    log_alpha = math.log(circulant_alpha)

    def strided(row, f, pad):
        half, pair = row // pairs, row % pairs
        return pl.ds(8 * (pair + pad) + 4 * half + f % 4, 8, stride=8)

    for g in range(groups):
        tile = pl.ds(8 * g, 8)
        steps = [arrived[t, tile, :] * math.exp(log_alpha * t / 8) for t in range(8)]
        edges = jnp.zeros((8, LANES), jnp.float32)
        for f, value in enumerate(forward_eight(steps)):
            rhs_f[f // 4, strided(HALO + 8 * g, f, 0), :] = value
            edges = jnp.where(lane // 16 == f, pltpu.roll(value, 8 + 16 * f, 1), edges)
            if g == 0:
                row_out[0, f] = value
            if g == groups - 1:
                row_out[1, f] = value
        packed[tile, :] = edges

    def halo_copy(number):
        dp, dz = SIDES[number]
        if dp == 0:
            source = row_out.at[0 if dz < 0 else 1]
        else:
            first, count = {0: (0, groups), -1: (0, 1), 1: (groups - 1, 1)}[dz]
            source = packed.at[pl.ds(8 * first, 8 * count)]
        copy = pltpu.make_async_remote_copy(
            src_ref=source, dst_ref=halo_target(number),
            send_sem=halo_s.at[number], recv_sem=halo_r.at[number],
            device_id=neighbour(dp, dz), device_id_type=mesh_id,
        )
        return copy

    def halo_target(number):
        dp, dz = SIDES[number]
        if dp == 0:
            return row_in_f.at[1 if dz < 0 else 0]
        last, count = {0: (1, groups), -1: (groups + 1, 1), 1: (0, 1)}[dz]
        return (from_right if dp < 0 else from_left).at[pl.ds(8 * last, 8 * count)]

    for number, (dp, dz) in enumerate(SIDES):
        @pl.when(there(dp, dz))
        def _():
            halo_copy(number).start()

    for number, (dp, dz) in enumerate(SIDES):
        @pl.when(there(-dp, -dz))
        def _():
            halo_copy(number).wait_recv()

        @pl.when(jnp.logical_not(there(-dp, -dz)))
        def _():
            target = halo_target(number)
            target[...] = jnp.zeros(target.shape, jnp.float32)

    weights = step_weights(DEGREE) * SWEEPS
    for g in range(ext // 8):
        tile = pl.ds(8 * g, 8)
        both = jnp.where(lane % 16 < 8, from_left[tile, :], from_right[tile, :])
        for f in range(8):
            at = strided(8 * g, f, 0)
            side_a[f // 4, at, :] = pltpu.roll(both, 120 - 16 * f, 1)
            if g == 0:
                rhs_f[f // 4, at, :] = row_in_f[0, f]
            if g == ext // 8 - 1:
                rhs_f[f // 4, at, :] = row_in_f[1, f]

    for part in range(2):
        for jj in range(packs):
            total = jnp.zeros((8, LANES), jnp.float32)
            for m in range(8):
                line = side_a[part, pl.ds(8 * (jj + packs * m), 8), :]
                total = jnp.where(lane // 16 == m, pltpu.roll(line, (16 * m + 8) % LANES, 1), total)
            side_f[part, pl.ds(8 * jj, 8), :] = total

    def close(ref, side):
        for part in range(2):
            first = ref[part, pl.ds(8, 8), :]
            final = ref[part, pl.ds(8 * pairs, 8), :]
            ref[part, pl.ds(0, 8), :] = pltpu.roll(final, 4, 0)
            ref[part, pl.ds(8 * pairs + 8, 8), :] = pltpu.roll(first, 4, 0)
            first = side[part, pl.ds(8, 8), :]
            final = side[part, pl.ds(8 * packs, 8), :]
            first = jnp.where(lane < 16, pltpu.roll(first, 4, 0), first)
            final = jnp.where(lane >= 112, pltpu.roll(final, 4, 0), final)
            side[part, pl.ds(0, 8), :] = pltpu.roll(final, 16, 1)
            side[part, pl.ds(8 * packs + 8, 8), :] = pltpu.roll(first, 112, 1)

    def corrected(totals, inv_ref, at):
        turn = inv_ref[2, at, :]
        return (
            inv_ref[0, at, :] * totals[0] + turn * totals[1],
            inv_ref[1, at, :] * totals[1] - turn * totals[0],
        )

    def begin(count, right, inv_ref, new):
        for j in range(count):
            at, mid = pl.ds(8 * j, 8), pl.ds(8 * j + 8, 8)
            changes = corrected([right[part, at, :] for part in range(2)], inv_ref, at)
            for part in range(2):
                new[part, mid, :] = weights[0] * changes[part]

    def update(j, right, coef_ref, inv_ref, old, new, rights, lefts, weight):
        at, mid, after = (pl.ds(8 * j + 8 * k, 8) for k in range(3))
        north, south, east, west = [coef_ref[n, at, :] for n in range(4)]
        totals = [
            (right[part, at, :] + north * old[part, after, :])
            + (south * old[part, at, :] + east * rights[part])
            + west * lefts[part]
            for part in range(2)
        ]
        changes = corrected(totals, inv_ref, at)
        for part in range(2):
            new[part, mid, :] = (1.0 - weight) * old[part, mid, :] + weight * changes[part]

    def step(old, old_s, new, new_s, weight, last):
        for jj in range(packs):
            edges = [old_s[part, pl.ds(8 * jj + 8, 8), :] for part in range(2)]
            inner = list(edges)
            for m in range(8):
                j = jj + packs * m
                rights, lefts = [], []
                for part in range(2):
                    here = old[part, pl.ds(8 * j + 8, 8), :]
                    outer = pltpu.roll(edges[part], 120 - 16 * m, 1)
                    rights.append(pltpu.roll(jnp.where(lane == 0, outer, here), LANES - 1, 1))
                    lefts.append(pltpu.roll(jnp.where(lane == LANES - 1, outer, here), 1, 1))
                    if not last:
                        moved = pltpu.roll(here, (16 * m + 8) % LANES, 1)
                        inner[part] = jnp.where(lane // 16 == m, moved, inner[part])
                update(j, rhs_f, coef, inv, old, new, rights, lefts, weight)
            if not last:
                rights = [
                    pltpu.roll(jnp.where(lane % 16 == 8, inner[part], edges[part]), LANES - 1, 1)
                    for part in range(2)
                ]
                lefts = [
                    pltpu.roll(jnp.where(lane % 16 == 7, inner[part], edges[part]), 1, 1)
                    for part in range(2)
                ]
                update(jj, side_f, coef_s, inv_s, old_s, new_s, rights, lefts, weight)
        if not last:
            close(new, new_s)

    begin(pairs, rhs_f, inv, v_a)
    begin(packs, side_f, inv_s, side_b)
    close(v_a, side_b)
    old, old_s, new, new_s = v_a, side_b, v_b, side_a
    for number in range(1, len(weights)):
        step(old, old_s, new, new_s, weights[number], number == len(weights) - 1)
        old, old_s, new, new_s = new, new_s, old, old_s

    for g in range(groups):
        tile = pl.ds(8 * g, 8)
        fields = [old[f // 4, strided(HALO + 8 * g, f, 1), :] for f in range(8)]
        for t, value in enumerate(backward_eight(fields)):
            leaving[t, tile, :] = value * (math.exp(-log_alpha * t / 8) / 8)

    columns = pl.ds(pl.multiple_of(p * LANES, LANES), LANES)

    def back_copy(d):
        peer = (me + d) % 8
        return pltpu.make_async_remote_copy(
            src_ref=leaving.at[peer], dst_ref=out.at[:, columns],
            send_sem=back_s.at[d], recv_sem=back_r.at[d],
            device_id=(peer, z), device_id_type=mesh_id,
        )

    def back_arrival(d):
        peer = (me + 8 - d) % 8
        theirs = pl.ds(pl.multiple_of(patch_place(peer) * LANES, LANES), LANES)
        return pltpu.make_async_remote_copy(
            src_ref=leaving.at[peer], dst_ref=out.at[:, theirs],
            send_sem=back_s.at[d], recv_sem=back_r.at[d],
            device_id=(peer, z), device_id_type=mesh_id,
        )

    for d in range(1, 8):
        back_copy(d).start()
    own_out = pltpu.make_async_copy(leaving.at[me], out.at[:, columns], local.at[2])
    own_out.start()

    for dz in (-1, 1):
        @pl.when(there(0, dz))
        def _():
            kap_copy(dz).wait_send()

    for d in range(1, 8):
        go_copy(d).wait_send()
    for number, (dp, dz) in enumerate(SIDES):
        @pl.when(there(dp, dz))
        def _():
            halo_copy(number).wait_send()

    own_out.wait()
    for d in range(1, 8):
        back_arrival(d).wait_recv()
    for d in range(1, 8):
        back_copy(d).wait_send()


def patch_body(row_count, right_side, kappa):
    rows, width = kappa.shape
    ext = rows + 2 * HALO
    f32 = jnp.float32
    dma = pltpu.SemaphoreType.DMA
    result = pl.pallas_call(
        functools.partial(patch_kernel, rows, row_count),
        out_shape=jax.ShapeDtypeStruct((rows, width), f32),
        in_specs=[pl.BlockSpec(memory_space=pl.ANY)] * 2,
        out_specs=pl.BlockSpec(memory_space=pl.ANY),
        scratch_shapes=[
            pltpu.VMEM((8, rows, LANES), f32),
            pltpu.VMEM((8, rows, LANES), f32),
            pltpu.VMEM((ext, width), f32),
            pltpu.VMEM((2, 4 * ext, LANES), f32),
            pltpu.VMEM((2, 4 * (ext + 4), LANES), f32),
            pltpu.VMEM((2, 4 * (ext + 4), LANES), f32),
            pltpu.VMEM((12 * ext, LANES), f32),
            pltpu.VMEM((4, 4 * ext, LANES), f32),
            pltpu.VMEM((3, 4 * ext, LANES), f32),
            pltpu.VMEM((2, ext // 2, LANES), f32),
            pltpu.VMEM((2, 4 * ext, LANES), f32),
            pltpu.VMEM((2, ext // 2 + 16, LANES), f32),
            pltpu.VMEM((4, ext // 2, LANES), f32),
            pltpu.VMEM((3, ext // 2, LANES), f32),
            pltpu.VMEM((rows, LANES), f32),
            pltpu.VMEM((ext, LANES), f32),
            pltpu.VMEM((ext, LANES), f32),
            pltpu.VMEM((2, 8, HALO, LANES), f32),
            pltpu.VMEM((2, 8, HALO, LANES), f32),
            dma((8,)), dma((8,)), dma((8,)), dma((8,)), dma((8,)), dma((8,)),
            dma((2,)), dma((2,)), dma((3,)),
        ],
        compiler_params=pltpu.CompilerParams(
            collective_id=0, has_side_effects=True, vmem_limit_bytes=60 * 2**20
        ),
        name="patch_solve",
    )(right_side.reshape(rows, width), kappa)
    return result.reshape(right_side.shape)


def solution(mesh):
    placed = (P("tm", "row", None), P("row", None))
    tm_size, row_count = mesh.shape["tm"], mesh.shape["row"]

    def local(right_side, kappa):
        fits = (
            tm_size == 8 and right_side.shape[0] == 1
            and kappa.shape[1] == tm_size * LANES and kappa.shape[0] % 16 == 0
        )
        if fits:
            return patch_body(row_count, right_side, kappa)
        return body(right_side, kappa)

    return jax.shard_map(
        local, mesh=mesh, in_specs=placed, out_specs=P("tm", "row", None), check_vma=False
    )
```

```python
import functools
import math

import jax
import jax.numpy as jnp
from jax import lax
from jax.experimental import pallas as pl
from jax.experimental.pallas import tpu as pltpu
from jax.sharding import PartitionSpec as P

SWEEPS = 2
DEGREE = 4


circulant_alpha = 0.05
courant_rows = 0.5
courant_cols = 0.25
cheb_centre = 1.0
cheb_half = 0.7


def from_partner(value, axis, bit):
    mask = 2**bit
    pairs = [(source, source ^ mask) for source in range(lax.axis_size(axis))]
    return lax.ppermute(value, axis, pairs)


def padded_2(block, sides, width):
    for axis, dim in sides:
        count = lax.axis_size(axis)
        forward = [(i, i + 1) for i in range(count - 1)]
        backward = [(target, source) for source, target in forward]
        low = lax.ppermute(
            lax.slice_in_dim(block, block.shape[dim] - width, None, axis=dim), axis, forward
        )
        high = lax.ppermute(lax.slice_in_dim(block, 0, width, axis=dim), axis, backward)
        block = jnp.concatenate([low, block, high], axis=dim)
    return block


def step_weights(count):
    return [
        1.0 / (cheb_centre + cheb_half * math.cos(math.pi * (2 * number + 1) / (2 * count)))
        for number in range(count)
    ]


def face_terms(kappa_rows):
    padded = jnp.pad(kappa_rows, ((0, 0), (1, 1)))
    centre = padded[1:-1, 1:-1]
    north = 0.5 * (centre + padded[2:, 1:-1])
    south = 0.5 * (centre + padded[:-2, 1:-1])
    east = 0.5 * (centre + padded[1:-1, 2:])
    west = 0.5 * (centre + padded[1:-1, :-2])
    diagonal = north + south + east + west + (courant_rows + courant_cols)
    return (north, south, east, west, diagonal)


def spatial(extended, faces):
    north, south, east, west, diagonal = faces
    padded = jnp.pad(extended, ((0, 0), (0, 0), (0, 0), (1, 1)))
    centre = padded[:, :, 1:-1, 1:-1]
    above = padded[:, :, 2:, 1:-1]
    below = padded[:, :, :-2, 1:-1]
    after = padded[:, :, 1:-1, 2:]
    before = padded[:, :, 1:-1, :-2]
    coupled = north * above + south * below + east * after + west * before
    return diagonal * centre - coupled - courant_rows * below - courant_cols * before


def rotate(pair, cosine, sine):
    return jnp.stack([pair[0] * cosine - pair[1] * sine, pair[0] * sine + pair[1] * cosine])


def short_transform(pair, sign):
    count = pair.shape[1]
    index = jnp.arange(count, dtype=jnp.int32)
    angles = 2.0 * math.pi / count * (index[:, None] * index[None, :] % count).astype(jnp.float32)
    cosine = jnp.cos(angles)
    sine = sign * jnp.sin(angles)
    highest = lax.Precision.HIGHEST
    real = jnp.einsum("kj,jrc->krc", cosine, pair[0], precision=highest) - jnp.einsum(
        "kj,jrc->krc", sine, pair[1], precision=highest
    )
    imag = jnp.einsum("kj,jrc->krc", cosine, pair[1], precision=highest) + jnp.einsum(
        "kj,jrc->krc", sine, pair[0], precision=highest
    )
    return jnp.stack([real, imag])


def bit_reversed(device, levels):
    total = jnp.zeros((), jnp.int32)
    for place in range(levels):
        total = total + device // 2**place % 2 * 2 ** (levels - 1 - place)
    return total


def forward_pairs(scaled, device, levels, tm_size, total_steps):
    place = levels - 1
    half = 2**place
    lower = device // half % 2 == 1
    angle = -math.pi / half * (device % half).astype(jnp.float32)
    partner = from_partner(scaled, "tm", place)
    summed = scaled + partner
    differ = partner - scaled
    real = jnp.where(lower, differ * jnp.cos(angle), summed)
    imag = jnp.where(lower, differ * jnp.sin(angle), jnp.zeros_like(summed))
    state = jnp.stack([real, imag])
    for place in range(levels - 2, -1, -1):
        half = 2**place
        lower = device // half % 2 == 1
        angle = -math.pi / half * (device % half).astype(jnp.float32)
        partner = from_partner(state, "tm", place)
        summed = state + partner
        rotated = rotate(partner - state, jnp.cos(angle), jnp.sin(angle))
        state = jnp.where(lower, rotated, summed)
    first_index = bit_reversed(device, levels)
    steps_dev = scaled.shape[0]
    local_steps = jnp.arange(steps_dev, dtype=jnp.int32)
    twist = (
        -2.0 * math.pi / total_steps * (local_steps * first_index % total_steps).astype(jnp.float32)
    )
    state = rotate(state, jnp.cos(twist)[:, None, None], jnp.sin(twist)[:, None, None])
    spectrum = short_transform(state, -1.0)
    frequencies = first_index + tm_size * local_steps
    return (spectrum, frequencies)


def backward_pairs(solved, device, levels, total_steps):
    steps_dev = solved.shape[1]
    first_index = bit_reversed(device, levels)
    state = short_transform(solved, 1.0) * (1.0 / steps_dev)
    local_steps = jnp.arange(steps_dev, dtype=jnp.int32)
    twist = (
        2.0 * math.pi / total_steps * (local_steps * first_index % total_steps).astype(jnp.float32)
    )
    state = rotate(state, jnp.cos(twist)[:, None, None], jnp.sin(twist)[:, None, None])
    for place in range(0, levels - 1):
        half = 2**place
        lower = device // half % 2 == 1
        angle = math.pi / half * (device % half).astype(jnp.float32)
        cosine = jnp.cos(angle)
        sine = jnp.sin(angle)
        partner = from_partner(state, "tm", place)
        upper_value = (state + rotate(partner, cosine, sine)) * 0.5
        lower_value = (partner - rotate(state, cosine, sine)) * 0.5
        state = jnp.where(lower, lower_value, upper_value)
    place = levels - 1
    half = 2**place
    lower = device // half % 2 == 1
    angle = math.pi / half * (device % half).astype(jnp.float32)
    own_turned = state[0] * jnp.cos(angle) - state[1] * jnp.sin(angle)
    outgoing = jnp.where(lower, own_turned, state[0])
    received = from_partner(outgoing, "tm", place)
    return jnp.where(lower, (received - own_turned) * 0.5, (state[0] + received) * 0.5)


def shift_terms(frequencies, faces, total_steps):
    decay = circulant_alpha ** (1.0 / total_steps)
    theta = 2.0 * math.pi / total_steps * frequencies.astype(jnp.float32)
    shift_real = (1.0 - decay * jnp.cos(theta))[:, None, None]
    shift_imag = (decay * jnp.sin(theta))[:, None, None]
    diag_real = shift_real + faces[4]
    magnitude = diag_real * diag_real + shift_imag * shift_imag
    return (shift_real, shift_imag, diag_real / magnitude, -shift_imag / magnitude)


def solve_each(spectrum, frequencies, kappa):
    total_steps = spectrum.shape[1] * lax.axis_size("tm")
    kappa_rows = padded_2(kappa, (("row", 0),), 1)
    faces = face_terms(kappa_rows)
    shift_real, shift_imag, inv_real, inv_imag = shift_terms(frequencies, faces, total_steps)
    state = jnp.zeros_like(spectrum)
    first = True
    for sweep in range(SWEEPS):
        for weight in step_weights(DEGREE):
            if first:
                residual = spectrum
                first = False
            else:
                extended = padded_2(state, (("row", 2),), 1)
                image = spatial(extended, faces)
                image_real = shift_real * state[0] - shift_imag * state[1] + image[0]
                image_imag = shift_real * state[1] + shift_imag * state[0] + image[1]
                residual = spectrum - jnp.stack([image_real, image_imag])
            corr_real = inv_real * residual[0] - inv_imag * residual[1]
            corr_imag = inv_real * residual[1] + inv_imag * residual[0]
            state = state + weight * jnp.stack([corr_real, corr_imag])
    return state


def solve_block(spectrum, frequencies, kappa):
    return solve_each(spectrum, frequencies, kappa)


def body(right_side, kappa):
    steps_dev = right_side.shape[0]
    tm_size = lax.axis_size("tm")
    total_steps = steps_dev * tm_size
    device = lax.axis_index("tm")
    local_steps = jnp.arange(steps_dev, dtype=jnp.int32)
    global_steps = device * steps_dev + local_steps
    log_alpha = math.log(circulant_alpha)
    step_float = global_steps.astype(jnp.float32)
    scaled = right_side * jnp.exp(log_alpha * step_float / total_steps)[:, None, None]
    levels = tm_size.bit_length() - 1
    spectrum, frequencies = forward_pairs(scaled, device, levels, tm_size, total_steps)
    solved = solve_block(spectrum, frequencies, kappa)
    signal = backward_pairs(solved, device, levels, total_steps)
    return signal * jnp.exp(-log_alpha * step_float / total_steps)[:, None, None]


LANES = 128
HALO = 8
SIDES = [(0, -1), (0, 1), (-1, 0), (-1, -1), (-1, 1), (1, 0), (1, -1), (1, 1)]


def patch_place(index):
    chip = index // 2
    return 2 * (chip + chip // 2 * (5 - 2 * chip)) + index % 2


def sublane_constants():
    field = lax.broadcasted_iota(jnp.int32, (8, LANES), 0) % 4
    decay = circulant_alpha ** (1.0 / 8)
    real = jnp.zeros((8, LANES), jnp.float32)
    turn = jnp.zeros((8, LANES), jnp.float32)
    for k in (1, 2, 3):
        theta = 2.0 * math.pi * k / 8
        real = jnp.where(field == k, 1.0 - decay * math.cos(theta), real)
        turn = jnp.where(field == k, decay * math.sin(theta), turn)
    real_a = jnp.where(field == 0, 1.0 - decay, real)
    real_b = jnp.where(field == 0, 1.0 + decay, real)
    return real_a, real_b, turn


def forward_eight(x):
    root = math.sqrt(0.5)
    s = [x[t] + x[t + 4] for t in range(4)]
    d = [x[t] - x[t + 4] for t in range(4)]
    even, odd = s[0] + s[2], s[1] + s[3]
    less, more = root * (d[1] - d[3]), root * (d[1] + d[3])
    return [
        even + odd, d[0] + less, s[0] - s[2], d[0] - less,
        even - odd, -d[2] - more, s[3] - s[1], d[2] - more,
    ]


def backward_eight(f):
    root = math.sqrt(0.5)
    x0, r1, r2, r3, x4, i1, i2, i3 = f
    plus, minus = x0 + x4, x0 - x4
    even = [plus + 2.0 * r2, minus - 2.0 * i2, plus - 2.0 * r2, minus + 2.0 * i2]
    less, total = r1 - r3, i1 + i3
    odd = [
        2.0 * (r1 + r3), 2.0 * root * (less - total),
        2.0 * (i3 - i1), -2.0 * root * (less + total),
    ]
    return [even[t] + odd[t] for t in range(4)] + [even[t] - odd[t] for t in range(4)]


def patch_kernel(
    rows, row_count, rhs, kappa, out,
    arrived, leaving, kap, rhs_f, v, u_a,
    coef, inv, side_f, spare, v_s, coef_s, inv_s, packed, from_left, from_right, fields, row_in_f,
    go_s, go_r, back_s, back_r, halo_s, halo_r, kap_s, kap_r, local,
):
    mesh_id = pl.DeviceIdType.MESH
    me, z = lax.axis_index("tm"), lax.axis_index("row")
    p = patch_place(me)
    ext = rows + 2 * HALO
    groups = rows // 8
    pairs = ext // 2
    packs = pairs // 8

    def there(dp, dz):
        ok = None
        for delta, at, count in ((dp, p, 8), (dz, z, row_count)):
            if delta:
                good = at > 0 if delta < 0 else at < count - 1
                ok = good if ok is None else jnp.logical_and(ok, good)
        return ok

    def neighbour(dp, dz):
        return (patch_place((p + dp + 8) % 8), z + dz)

    barrier = pltpu.get_barrier_semaphore()
    for d in range(1, 8):
        pl.semaphore_signal(barrier, inc=1, device_id=((me + d) % 8, z), device_id_type=mesh_id)
    expected = jnp.int32(7)
    for dp, dz in SIDES:
        if dz == 0:
            continue
        ok = there(dp, dz)
        expected = expected + ok.astype(jnp.int32)

        @pl.when(ok)
        def _():
            pl.semaphore_signal(
                barrier, inc=1, device_id=neighbour(dp, dz), device_id_type=mesh_id
            )

    own_rhs = pltpu.make_async_copy(
        rhs.at[:, pl.ds(pl.multiple_of(p * LANES, LANES), LANES)], arrived.at[me], local.at[0]
    )
    own_kap = pltpu.make_async_copy(kappa, kap.at[pl.ds(HALO, rows)], local.at[1])
    own_rhs.start()
    own_kap.start()
    pl.semaphore_wait(barrier, expected)

    def go_copy(d):
        peer = (me + d) % 8
        columns = pl.ds(pl.multiple_of(patch_place(peer) * LANES, LANES), LANES)
        return pltpu.make_async_remote_copy(
            src_ref=rhs.at[:, columns], dst_ref=arrived.at[me],
            send_sem=go_s.at[d], recv_sem=go_r.at[d],
            device_id=(peer, z), device_id_type=mesh_id,
        )

    def go_arrival(d):
        peer = (me + 8 - d) % 8
        return pltpu.make_async_remote_copy(
            src_ref=rhs.at[:, pl.ds(0, LANES)], dst_ref=arrived.at[peer],
            send_sem=go_s.at[d], recv_sem=go_r.at[d],
            device_id=(peer, z), device_id_type=mesh_id,
        )

    def kap_copy(dz):
        first, last = (0, HALO + rows) if dz < 0 else (rows - HALO, 0)
        which = (dz + 1) // 2
        return pltpu.make_async_remote_copy(
            src_ref=kappa.at[pl.ds(first, HALO)], dst_ref=kap.at[pl.ds(last, HALO)],
            send_sem=kap_s.at[which], recv_sem=kap_r.at[which],
            device_id=(me, z + dz), device_id_type=mesh_id,
        )

    for dz in (-1, 1):
        @pl.when(there(0, dz))
        def _():
            kap_copy(dz).start()

    for d in range(1, 8):
        go_copy(d).start()

    own_kap.wait()
    for dz in (-1, 1):
        lost = HALO + rows if dz < 0 else 0

        @pl.when(there(0, -dz))
        def _():
            kap_copy(dz).wait_recv()

        @pl.when(jnp.logical_not(there(0, -dz)))
        def _():
            kap[pl.ds(lost, HALO), :] = jnp.zeros((HALO, kap.shape[1]), jnp.float32)

    lane = lax.broadcasted_iota(jnp.int32, (8, LANES), 1)
    lane_all = lax.broadcasted_iota(jnp.int32, (ext, LANES), 1)

    def kap_block(which):
        return kap[:, pl.ds(pl.multiple_of(which * LANES, LANES), LANES)]

    right_in = (p < 7).astype(jnp.float32)
    left_in = (p > 0).astype(jnp.float32)
    side_in = jnp.where(lane_all < 64, right_in, left_in)
    row_at = lax.broadcasted_iota(jnp.int32, (ext, LANES), 0)
    top_in = (z > 0).astype(jnp.float32)
    low_in = (z < row_count - 1).astype(jnp.float32)
    row_in = jnp.where(row_at < HALO, top_in, jnp.where(row_at >= HALO + rows, low_in, 1.0))
    k_m = kap_block(p)
    k_s = jnp.where(lane_all < 64, kap_block((p + 1) % 8), kap_block((p + 7) % 8)) * side_in
    turned = [pltpu.roll(k, 1, 1) for k in (k_m, k_s)]
    turned_up = [pltpu.roll(k, LANES - 1, 1) for k in (k_m, k_s)]
    for side, k in enumerate((k_m, k_s)):
        north = 0.5 * (k + pltpu.roll(k, ext - 1, 0))
        south = 0.5 * (k + pltpu.roll(k, 1, 0))
        east = 0.5 * (k + jnp.where(lane_all == LANES - 1, turned_up[1 - side], turned_up[side]))
        west = 0.5 * (k + jnp.where(lane_all == 0, turned[1 - side], turned[side]))
        diagonal = north + south + east + west + (courant_rows + courant_cols)
        inside = row_in if side == 0 else row_in * side_in
        parts = (north, south + courant_rows, east, west + courant_cols, diagonal, inside)
        for number, part in enumerate(parts):
            u_a[pl.ds((side * 6 + number) * ext, ext), :] = part

    shift_a, shift_b, shift_turn = sublane_constants()
    shift_square = shift_turn * shift_turn
    upper = lax.broadcasted_iota(jnp.int32, (8, LANES), 0) < 4

    def tile_at(index):
        return pl.ds(pl.multiple_of(8 * index, 8), 8)

    def inverses(wide, scale):
        diag_a, diag_b = wide + shift_a, wide + shift_b
        scale_a = scale / (diag_a * diag_a + shift_square)
        scale_b = scale / (diag_b * diag_b + shift_square)
        return diag_a * scale_a, diag_b * scale_b, shift_turn * scale_a

    def spread(g, carry):
        both = [
            [
                u_a[pl.ds(pl.multiple_of(number * ext + half + 8 * g, 8), 8), :]
                for half in (0, pairs)
            ]
            for number in range(6)
        ]
        for i in range(8):
            at = pl.ds(pl.multiple_of(64 * g + 8 * i, 8), 8)
            wide = [
                jnp.where(
                    upper,
                    jnp.broadcast_to(first[i : i + 1, :], (8, LANES)),
                    jnp.broadcast_to(second[i : i + 1, :], (8, LANES)),
                )
                for first, second in both
            ]
            for number in range(4):
                coef[number, at, :] = wide[number]
            for number, value in enumerate(inverses(wide[4], wide[5])):
                inv[number, at, :] = value
        return carry

    lax.fori_loop(0, pairs // 8, spread, 0)

    def spread_sides(jj, carry):
        wide = []
        for number in range(6):
            total = jnp.zeros((8, LANES), jnp.float32)
            for m in range(8):
                row = (6 + number) * ext + packs * m + jj
                line = jnp.where(
                    upper,
                    jnp.broadcast_to(u_a[pl.ds(row, 1), :], (8, LANES)),
                    jnp.broadcast_to(u_a[pl.ds(row + pairs, 1), :], (8, LANES)),
                )
                total = jnp.where(lane // 16 == m, pltpu.roll(line, (16 * m + 8) % LANES, 1), total)
            wide.append(total)
        at = tile_at(jj)
        for number in range(4):
            coef_s[number, at, :] = wide[number]
        for number, value in enumerate(inverses(wide[4], wide[5])):
            inv_s[number, at, :] = value
        return carry

    lax.fori_loop(0, packs, spread_sides, 0)

    own_rhs.wait()
    for d in range(1, 8):
        go_arrival(d).wait_recv()

    log_alpha = math.log(circulant_alpha)

    def strided(block, f, pad):
        half, pair = lax.div(block, packs), 8 * lax.rem(block, packs)
        return pl.ds(8 * (pair + pad) + 4 * half + f % 4, 8, stride=8)

    def transform(g, carry):
        tile = tile_at(g)
        steps = [arrived[t, tile, :] * math.exp(log_alpha * t / 8) for t in range(8)]
        edges = jnp.zeros((8, LANES), jnp.float32)
        for f, value in enumerate(forward_eight(steps)):
            rhs_f[f // 4, strided(g + 1, f, 0), :] = value
            edges = jnp.where(lane // 16 == f, pltpu.roll(value, 8 + 16 * f, 1), edges)
            fields[g, f] = value
        packed[tile, :] = edges
        return carry

    lax.fori_loop(0, groups, transform, 0)

    def halo_copy(number):
        dp, dz = SIDES[number]
        if dp == 0:
            source = fields.at[0 if dz < 0 else groups - 1]
        else:
            first, count = {0: (0, groups), -1: (0, 1), 1: (groups - 1, 1)}[dz]
            source = packed.at[pl.ds(8 * first, 8 * count)]
        copy = pltpu.make_async_remote_copy(
            src_ref=source, dst_ref=halo_target(number),
            send_sem=halo_s.at[number], recv_sem=halo_r.at[number],
            device_id=neighbour(dp, dz), device_id_type=mesh_id,
        )
        return copy

    def halo_target(number):
        dp, dz = SIDES[number]
        if dp == 0:
            return row_in_f.at[1 if dz < 0 else 0]
        last, count = {0: (1, groups), -1: (groups + 1, 1), 1: (0, 1)}[dz]
        return (from_right if dp < 0 else from_left).at[pl.ds(8 * last, 8 * count)]

    for number, (dp, dz) in enumerate(SIDES):
        @pl.when(there(dp, dz))
        def _():
            halo_copy(number).start()

    for number, (dp, dz) in enumerate(SIDES):
        @pl.when(there(-dp, -dz))
        def _():
            halo_copy(number).wait_recv()

        @pl.when(jnp.logical_not(there(-dp, -dz)))
        def _():
            target = halo_target(number)
            target[...] = jnp.zeros(target.shape, jnp.float32)

    weights = step_weights(DEGREE) * SWEEPS
    def place_rows(g, carry):
        for f in range(8):
            rhs_f[f // 4, strided(g * (groups + 1), f, 0), :] = row_in_f[g, f]
        return carry

    lax.fori_loop(0, 2, place_rows, 0)

    def place_sides(g, carry):
        tile = tile_at(g)
        both = jnp.where(lane % 16 < 8, from_left[tile, :], from_right[tile, :])
        for f in range(8):
            spare[f // 4, strided(g, f, 0), :] = pltpu.roll(both, 120 - 16 * f, 1)
        return carry

    lax.fori_loop(0, ext // 8, place_sides, 0)

    def pack_sides(jj, carry):
        for part in range(2):
            total = jnp.zeros((8, LANES), jnp.float32)
            for m in range(8):
                line = spare[part, tile_at(jj + packs * m), :]
                total = jnp.where(lane // 16 == m, pltpu.roll(line, (16 * m + 8) % LANES, 1), total)
            side_f[part, tile_at(jj), :] = total
        return carry

    lax.fori_loop(0, packs, pack_sides, 0)

    def close(slot):
        for part in range(2):
            base = 2 * slot + part
            first = v[base, pl.ds(8, 8), :]
            final = v[base, pl.ds(8 * pairs, 8), :]
            v[base, pl.ds(0, 8), :] = pltpu.roll(final, 4, 0)
            v[base, pl.ds(8 * pairs + 8, 8), :] = pltpu.roll(first, 4, 0)
            first = v_s[base, pl.ds(8, 8), :]
            final = v_s[base, pl.ds(8 * packs, 8), :]
            first = jnp.where(lane < 16, pltpu.roll(first, 4, 0), first)
            final = jnp.where(lane >= 112, pltpu.roll(final, 4, 0), final)
            v_s[base, pl.ds(0, 8), :] = pltpu.roll(final, 16, 1)
            v_s[base, pl.ds(8 * packs + 8, 8), :] = pltpu.roll(first, 112, 1)

    def corrected(totals, inv_ref, at):
        turn = inv_ref[2, at, :]
        return (
            inv_ref[0, at, :] * totals[0] + turn * totals[1],
            inv_ref[1, at, :] * totals[1] - turn * totals[0],
        )

    def begin(right, inv_ref, new):
        def body(j, carry):
            changes = corrected([right[part, tile_at(j), :] for part in range(2)], inv_ref, tile_at(j))
            for part in range(2):
                new[part, tile_at(j + 1), :] = weights[0] * changes[part]
            return carry

        return body

    def update(j, right, coef_ref, inv_ref, state, old, new, rights, lefts, weight):
        at, mid, after = tile_at(j), tile_at(j + 1), tile_at(j + 2)
        north, south, east, west = [coef_ref[n, at, :] for n in range(4)]
        totals = [
            (right[part, at, :] + north * state[old + part, after, :])
            + (south * state[old + part, at, :] + east * rights[part])
            + west * lefts[part]
            for part in range(2)
        ]
        changes = corrected(totals, inv_ref, at)
        for part in range(2):
            kept = (1.0 - weight) * state[old + part, mid, :]
            state[new + part, mid, :] = kept + weight * changes[part]

    lax.fori_loop(0, pairs, begin(rhs_f, inv, v), 0, unroll=8)
    lax.fori_loop(0, packs, begin(side_f, inv_s, v_s), 0, unroll=packs)
    close(0)

    def step(number, carry):
        old = 2 * lax.rem(number + 1, 2)
        new = 2 - old
        which = lax.rem(number, DEGREE)
        weight = jnp.float32(weights[0])
        for at in range(1, DEGREE):
            weight = jnp.where(which == at, jnp.float32(weights[at]), weight)

        def group(jj, carry):
            edges = [v_s[old + part, tile_at(jj + 1), :] for part in range(2)]
            inner = list(edges)
            for m in range(8):
                j = jj + packs * m
                rights, lefts = [], []
                for part in range(2):
                    here = v[old + part, tile_at(j + 1), :]
                    outer = pltpu.roll(edges[part], 120 - 16 * m, 1)
                    rights.append(pltpu.roll(jnp.where(lane == 0, outer, here), LANES - 1, 1))
                    lefts.append(pltpu.roll(jnp.where(lane == LANES - 1, outer, here), 1, 1))
                    moved = pltpu.roll(here, (16 * m + 8) % LANES, 1)
                    inner[part] = jnp.where(lane // 16 == m, moved, inner[part])
                update(j, rhs_f, coef, inv, v, old, new, rights, lefts, weight)
            rights = [
                pltpu.roll(jnp.where(lane % 16 == 8, inner[part], edges[part]), LANES - 1, 1)
                for part in range(2)
            ]
            lefts = [
                pltpu.roll(jnp.where(lane % 16 == 7, inner[part], edges[part]), 1, 1)
                for part in range(2)
            ]
            update(jj, side_f, coef_s, inv_s, v_s, old, new, rights, lefts, weight)
            return carry

        lax.fori_loop(0, packs, group, 0)
        close(lax.div(new, 2))
        return carry

    lax.fori_loop(1, len(weights), step, 0)
    final = 2 * ((len(weights) - 1) % 2)

    def inverse(g, carry):
        found = [v[final + f // 4, strided(g + 1, f, 1), :] for f in range(8)]
        for t, value in enumerate(backward_eight(found)):
            leaving[t, tile_at(g), :] = value * (math.exp(-log_alpha * t / 8) / 8)
        return carry

    lax.fori_loop(0, groups, inverse, 0)

    columns = pl.ds(pl.multiple_of(p * LANES, LANES), LANES)

    def back_copy(d):
        peer = (me + d) % 8
        return pltpu.make_async_remote_copy(
            src_ref=leaving.at[peer], dst_ref=out.at[:, columns],
            send_sem=back_s.at[d], recv_sem=back_r.at[d],
            device_id=(peer, z), device_id_type=mesh_id,
        )

    def back_arrival(d):
        peer = (me + 8 - d) % 8
        theirs = pl.ds(pl.multiple_of(patch_place(peer) * LANES, LANES), LANES)
        return pltpu.make_async_remote_copy(
            src_ref=leaving.at[peer], dst_ref=out.at[:, theirs],
            send_sem=back_s.at[d], recv_sem=back_r.at[d],
            device_id=(peer, z), device_id_type=mesh_id,
        )

    for d in range(1, 8):
        back_copy(d).start()
    own_out = pltpu.make_async_copy(leaving.at[me], out.at[:, columns], local.at[2])
    own_out.start()

    for dz in (-1, 1):
        @pl.when(there(0, dz))
        def _():
            kap_copy(dz).wait_send()

    for d in range(1, 8):
        go_copy(d).wait_send()
    for number, (dp, dz) in enumerate(SIDES):
        @pl.when(there(dp, dz))
        def _():
            halo_copy(number).wait_send()

    own_out.wait()
    for d in range(1, 8):
        back_arrival(d).wait_recv()
    for d in range(1, 8):
        back_copy(d).wait_send()


def patch_body(row_count, right_side, kappa):
    rows, width = kappa.shape
    ext = rows + 2 * HALO
    f32 = jnp.float32
    dma = pltpu.SemaphoreType.DMA
    result = pl.pallas_call(
        functools.partial(patch_kernel, rows, row_count),
        out_shape=jax.ShapeDtypeStruct((rows, width), f32),
        in_specs=[pl.BlockSpec(memory_space=pl.ANY)] * 2,
        out_specs=pl.BlockSpec(memory_space=pl.ANY),
        scratch_shapes=[
            pltpu.VMEM((8, rows, LANES), f32),
            pltpu.VMEM((8, rows, LANES), f32),
            pltpu.VMEM((ext, width), f32),
            pltpu.VMEM((2, 4 * ext, LANES), f32),
            pltpu.VMEM((4, 4 * (ext + 4), LANES), f32),
            pltpu.VMEM((12 * ext, LANES), f32),
            pltpu.VMEM((4, 4 * ext, LANES), f32),
            pltpu.VMEM((3, 4 * ext, LANES), f32),
            pltpu.VMEM((2, ext // 2, LANES), f32),
            pltpu.VMEM((2, 4 * ext, LANES), f32),
            pltpu.VMEM((4, ext // 2 + 16, LANES), f32),
            pltpu.VMEM((4, ext // 2, LANES), f32),
            pltpu.VMEM((3, ext // 2, LANES), f32),
            pltpu.VMEM((rows, LANES), f32),
            pltpu.VMEM((ext, LANES), f32),
            pltpu.VMEM((ext, LANES), f32),
            pltpu.VMEM((rows // 8, 8, HALO, LANES), f32),
            pltpu.VMEM((2, 8, HALO, LANES), f32),
            dma((8,)), dma((8,)), dma((8,)), dma((8,)), dma((8,)), dma((8,)),
            dma((2,)), dma((2,)), dma((3,)),
        ],
        compiler_params=pltpu.CompilerParams(
            collective_id=0, has_side_effects=True, vmem_limit_bytes=60 * 2**20
        ),
        name="patch_solve",
    )(right_side.reshape(rows, width), kappa)
    return result.reshape(right_side.shape)


def solution(mesh):
    placed = (P("tm", "row", None), P("row", None))
    tm_size, row_count = mesh.shape["tm"], mesh.shape["row"]

    def local(right_side, kappa):
        fits = (
            tm_size == 8 and right_side.shape[0] == 1
            and kappa.shape[1] == tm_size * LANES and kappa.shape[0] % 16 == 0
        )
        if fits:
            return patch_body(row_count, right_side, kappa)
        return body(right_side, kappa)

    return jax.shard_map(
        local, mesh=mesh, in_specs=placed, out_specs=P("tm", "row", None), check_vma=False
    )
```

```python
import functools
import math

import jax
import jax.numpy as jnp
from jax import lax
from jax.experimental import pallas as pl
from jax.experimental.pallas import tpu as pltpu
from jax.sharding import PartitionSpec as P

SWEEPS = 2
DEGREE = 4


circulant_alpha = 0.05
courant_rows = 0.5
courant_cols = 0.25
cheb_centre = 1.0
cheb_half = 0.7


def from_partner(value, axis, bit):
    mask = 2**bit
    pairs = [(source, source ^ mask) for source in range(lax.axis_size(axis))]
    return lax.ppermute(value, axis, pairs)


def padded_2(block, sides, width):
    for axis, dim in sides:
        count = lax.axis_size(axis)
        forward = [(i, i + 1) for i in range(count - 1)]
        backward = [(target, source) for source, target in forward]
        low = lax.ppermute(
            lax.slice_in_dim(block, block.shape[dim] - width, None, axis=dim), axis, forward
        )
        high = lax.ppermute(lax.slice_in_dim(block, 0, width, axis=dim), axis, backward)
        block = jnp.concatenate([low, block, high], axis=dim)
    return block


def step_weights(count):
    return [
        1.0 / (cheb_centre + cheb_half * math.cos(math.pi * (2 * number + 1) / (2 * count)))
        for number in range(count)
    ]


def face_terms(kappa_rows):
    padded = jnp.pad(kappa_rows, ((0, 0), (1, 1)))
    centre = padded[1:-1, 1:-1]
    north = 0.5 * (centre + padded[2:, 1:-1])
    south = 0.5 * (centre + padded[:-2, 1:-1])
    east = 0.5 * (centre + padded[1:-1, 2:])
    west = 0.5 * (centre + padded[1:-1, :-2])
    diagonal = north + south + east + west + (courant_rows + courant_cols)
    return (north, south, east, west, diagonal)


def spatial(extended, faces):
    north, south, east, west, diagonal = faces
    padded = jnp.pad(extended, ((0, 0), (0, 0), (0, 0), (1, 1)))
    centre = padded[:, :, 1:-1, 1:-1]
    above = padded[:, :, 2:, 1:-1]
    below = padded[:, :, :-2, 1:-1]
    after = padded[:, :, 1:-1, 2:]
    before = padded[:, :, 1:-1, :-2]
    coupled = north * above + south * below + east * after + west * before
    return diagonal * centre - coupled - courant_rows * below - courant_cols * before


def rotate(pair, cosine, sine):
    return jnp.stack([pair[0] * cosine - pair[1] * sine, pair[0] * sine + pair[1] * cosine])


def short_transform(pair, sign):
    count = pair.shape[1]
    index = jnp.arange(count, dtype=jnp.int32)
    angles = 2.0 * math.pi / count * (index[:, None] * index[None, :] % count).astype(jnp.float32)
    cosine = jnp.cos(angles)
    sine = sign * jnp.sin(angles)
    highest = lax.Precision.HIGHEST
    real = jnp.einsum("kj,jrc->krc", cosine, pair[0], precision=highest) - jnp.einsum(
        "kj,jrc->krc", sine, pair[1], precision=highest
    )
    imag = jnp.einsum("kj,jrc->krc", cosine, pair[1], precision=highest) + jnp.einsum(
        "kj,jrc->krc", sine, pair[0], precision=highest
    )
    return jnp.stack([real, imag])


def bit_reversed(device, levels):
    total = jnp.zeros((), jnp.int32)
    for place in range(levels):
        total = total + device // 2**place % 2 * 2 ** (levels - 1 - place)
    return total


def forward_pairs(scaled, device, levels, tm_size, total_steps):
    place = levels - 1
    half = 2**place
    lower = device // half % 2 == 1
    angle = -math.pi / half * (device % half).astype(jnp.float32)
    partner = from_partner(scaled, "tm", place)
    summed = scaled + partner
    differ = partner - scaled
    real = jnp.where(lower, differ * jnp.cos(angle), summed)
    imag = jnp.where(lower, differ * jnp.sin(angle), jnp.zeros_like(summed))
    state = jnp.stack([real, imag])
    for place in range(levels - 2, -1, -1):
        half = 2**place
        lower = device // half % 2 == 1
        angle = -math.pi / half * (device % half).astype(jnp.float32)
        partner = from_partner(state, "tm", place)
        summed = state + partner
        rotated = rotate(partner - state, jnp.cos(angle), jnp.sin(angle))
        state = jnp.where(lower, rotated, summed)
    first_index = bit_reversed(device, levels)
    steps_dev = scaled.shape[0]
    local_steps = jnp.arange(steps_dev, dtype=jnp.int32)
    twist = (
        -2.0 * math.pi / total_steps * (local_steps * first_index % total_steps).astype(jnp.float32)
    )
    state = rotate(state, jnp.cos(twist)[:, None, None], jnp.sin(twist)[:, None, None])
    spectrum = short_transform(state, -1.0)
    frequencies = first_index + tm_size * local_steps
    return (spectrum, frequencies)


def backward_pairs(solved, device, levels, total_steps):
    steps_dev = solved.shape[1]
    first_index = bit_reversed(device, levels)
    state = short_transform(solved, 1.0) * (1.0 / steps_dev)
    local_steps = jnp.arange(steps_dev, dtype=jnp.int32)
    twist = (
        2.0 * math.pi / total_steps * (local_steps * first_index % total_steps).astype(jnp.float32)
    )
    state = rotate(state, jnp.cos(twist)[:, None, None], jnp.sin(twist)[:, None, None])
    for place in range(0, levels - 1):
        half = 2**place
        lower = device // half % 2 == 1
        angle = math.pi / half * (device % half).astype(jnp.float32)
        cosine = jnp.cos(angle)
        sine = jnp.sin(angle)
        partner = from_partner(state, "tm", place)
        upper_value = (state + rotate(partner, cosine, sine)) * 0.5
        lower_value = (partner - rotate(state, cosine, sine)) * 0.5
        state = jnp.where(lower, lower_value, upper_value)
    place = levels - 1
    half = 2**place
    lower = device // half % 2 == 1
    angle = math.pi / half * (device % half).astype(jnp.float32)
    own_turned = state[0] * jnp.cos(angle) - state[1] * jnp.sin(angle)
    outgoing = jnp.where(lower, own_turned, state[0])
    received = from_partner(outgoing, "tm", place)
    return jnp.where(lower, (received - own_turned) * 0.5, (state[0] + received) * 0.5)


def shift_terms(frequencies, faces, total_steps):
    decay = circulant_alpha ** (1.0 / total_steps)
    theta = 2.0 * math.pi / total_steps * frequencies.astype(jnp.float32)
    shift_real = (1.0 - decay * jnp.cos(theta))[:, None, None]
    shift_imag = (decay * jnp.sin(theta))[:, None, None]
    diag_real = shift_real + faces[4]
    magnitude = diag_real * diag_real + shift_imag * shift_imag
    return (shift_real, shift_imag, diag_real / magnitude, -shift_imag / magnitude)


def solve_each(spectrum, frequencies, kappa):
    total_steps = spectrum.shape[1] * lax.axis_size("tm")
    kappa_rows = padded_2(kappa, (("row", 0),), 1)
    faces = face_terms(kappa_rows)
    shift_real, shift_imag, inv_real, inv_imag = shift_terms(frequencies, faces, total_steps)
    state = jnp.zeros_like(spectrum)
    first = True
    for sweep in range(SWEEPS):
        for weight in step_weights(DEGREE):
            if first:
                residual = spectrum
                first = False
            else:
                extended = padded_2(state, (("row", 2),), 1)
                image = spatial(extended, faces)
                image_real = shift_real * state[0] - shift_imag * state[1] + image[0]
                image_imag = shift_real * state[1] + shift_imag * state[0] + image[1]
                residual = spectrum - jnp.stack([image_real, image_imag])
            corr_real = inv_real * residual[0] - inv_imag * residual[1]
            corr_imag = inv_real * residual[1] + inv_imag * residual[0]
            state = state + weight * jnp.stack([corr_real, corr_imag])
    return state


def solve_block(spectrum, frequencies, kappa):
    return solve_each(spectrum, frequencies, kappa)


def body(right_side, kappa):
    steps_dev = right_side.shape[0]
    tm_size = lax.axis_size("tm")
    total_steps = steps_dev * tm_size
    device = lax.axis_index("tm")
    local_steps = jnp.arange(steps_dev, dtype=jnp.int32)
    global_steps = device * steps_dev + local_steps
    log_alpha = math.log(circulant_alpha)
    step_float = global_steps.astype(jnp.float32)
    scaled = right_side * jnp.exp(log_alpha * step_float / total_steps)[:, None, None]
    levels = tm_size.bit_length() - 1
    spectrum, frequencies = forward_pairs(scaled, device, levels, tm_size, total_steps)
    solved = solve_block(spectrum, frequencies, kappa)
    signal = backward_pairs(solved, device, levels, total_steps)
    return signal * jnp.exp(-log_alpha * step_float / total_steps)[:, None, None]


LANES = 128
HALO = 8
SIDES = [(0, -1), (0, 1), (-1, 0), (-1, -1), (-1, 1), (1, 0), (1, -1), (1, 1)]


def patch_place(index):
    chip = index // 2
    return 2 * (chip + chip // 2 * (5 - 2 * chip)) + index % 2


def sublane_constants():
    field = lax.broadcasted_iota(jnp.int32, (8, LANES), 0) % 4
    decay = circulant_alpha ** (1.0 / 8)
    real = jnp.zeros((8, LANES), jnp.float32)
    turn = jnp.zeros((8, LANES), jnp.float32)
    for k in (1, 2, 3):
        theta = 2.0 * math.pi * k / 8
        real = jnp.where(field == k, 1.0 - decay * math.cos(theta), real)
        turn = jnp.where(field == k, decay * math.sin(theta), turn)
    real_a = jnp.where(field == 0, 1.0 - decay, real)
    real_b = jnp.where(field == 0, 1.0 + decay, real)
    return real_a, real_b, turn


def forward_eight(x):
    root = math.sqrt(0.5)
    s = [x[t] + x[t + 4] for t in range(4)]
    d = [x[t] - x[t + 4] for t in range(4)]
    even, odd = s[0] + s[2], s[1] + s[3]
    less, more = root * (d[1] - d[3]), root * (d[1] + d[3])
    return [
        even + odd, d[0] + less, s[0] - s[2], d[0] - less,
        even - odd, -d[2] - more, s[3] - s[1], d[2] - more,
    ]


def backward_eight(f):
    root = math.sqrt(0.5)
    x0, r1, r2, r3, x4, i1, i2, i3 = f
    plus, minus = x0 + x4, x0 - x4
    even = [plus + 2.0 * r2, minus - 2.0 * i2, plus - 2.0 * r2, minus + 2.0 * i2]
    less, total = r1 - r3, i1 + i3
    odd = [
        2.0 * (r1 + r3), 2.0 * root * (less - total),
        2.0 * (i3 - i1), -2.0 * root * (less + total),
    ]
    return [even[t] + odd[t] for t in range(4)] + [even[t] - odd[t] for t in range(4)]


def patch_kernel(
    rows, row_count, rhs, kappa, out,
    arrived, leaving, kap, rhs_f, v, u_a,
    coef, inv, side_f, spare, v_s, coef_s, inv_s, packed, from_left, from_right, fields, row_in_f,
    go_s, go_r, back_s, back_r, halo_s, halo_r, kap_s, kap_r, local,
):
    mesh_id = pl.DeviceIdType.MESH
    me, z = lax.axis_index("tm"), lax.axis_index("row")
    p = patch_place(me)
    ext = rows + 2 * HALO
    groups = rows // 8
    pairs = ext // 2
    packs = pairs // 8

    def there(dp, dz):
        ok = None
        for delta, at, count in ((dp, p, 8), (dz, z, row_count)):
            if delta:
                good = at > 0 if delta < 0 else at < count - 1
                ok = good if ok is None else jnp.logical_and(ok, good)
        return ok

    def neighbour(dp, dz):
        return (patch_place((p + dp + 8) % 8), z + dz)

    barrier = pltpu.get_barrier_semaphore()
    for d in range(1, 8):
        pl.semaphore_signal(barrier, inc=1, device_id=((me + d) % 8, z), device_id_type=mesh_id)
    expected = jnp.int32(7)
    for dp, dz in SIDES:
        if dz == 0:
            continue
        ok = there(dp, dz)
        expected = expected + ok.astype(jnp.int32)

        @pl.when(ok)
        def _():
            pl.semaphore_signal(
                barrier, inc=1, device_id=neighbour(dp, dz), device_id_type=mesh_id
            )

    own_rhs = pltpu.make_async_copy(
        rhs.at[:, pl.ds(pl.multiple_of(p * LANES, LANES), LANES)], arrived.at[me], local.at[0]
    )
    own_kap = pltpu.make_async_copy(kappa, kap.at[pl.ds(HALO, rows)], local.at[1])
    own_rhs.start()
    own_kap.start()
    pl.semaphore_wait(barrier, expected)

    def go_copy(d):
        peer = (me + d) % 8
        columns = pl.ds(pl.multiple_of(patch_place(peer) * LANES, LANES), LANES)
        return pltpu.make_async_remote_copy(
            src_ref=rhs.at[:, columns], dst_ref=arrived.at[me],
            send_sem=go_s.at[d], recv_sem=go_r.at[d],
            device_id=(peer, z), device_id_type=mesh_id,
        )

    def go_arrival(d):
        peer = (me + 8 - d) % 8
        return pltpu.make_async_remote_copy(
            src_ref=rhs.at[:, pl.ds(0, LANES)], dst_ref=arrived.at[peer],
            send_sem=go_s.at[d], recv_sem=go_r.at[d],
            device_id=(peer, z), device_id_type=mesh_id,
        )

    def kap_copy(dz):
        first, last = (0, HALO + rows) if dz < 0 else (rows - HALO, 0)
        which = (dz + 1) // 2
        return pltpu.make_async_remote_copy(
            src_ref=kappa.at[pl.ds(first, HALO)], dst_ref=kap.at[pl.ds(last, HALO)],
            send_sem=kap_s.at[which], recv_sem=kap_r.at[which],
            device_id=(me, z + dz), device_id_type=mesh_id,
        )

    for dz in (-1, 1):
        @pl.when(there(0, dz))
        def _():
            kap_copy(dz).start()

    for d in range(1, 8):
        go_copy(d).start()

    own_kap.wait()
    for dz in (-1, 1):
        lost = HALO + rows if dz < 0 else 0

        @pl.when(there(0, -dz))
        def _():
            kap_copy(dz).wait_recv()

        @pl.when(jnp.logical_not(there(0, -dz)))
        def _():
            kap[pl.ds(lost, HALO), :] = jnp.zeros((HALO, kap.shape[1]), jnp.float32)

    lane = lax.broadcasted_iota(jnp.int32, (8, LANES), 1)
    lane_all = lax.broadcasted_iota(jnp.int32, (ext, LANES), 1)

    def kap_block(which):
        return kap[:, pl.ds(pl.multiple_of(which * LANES, LANES), LANES)]

    right_in = (p < 7).astype(jnp.float32)
    left_in = (p > 0).astype(jnp.float32)
    side_in = jnp.where(lane_all < 64, right_in, left_in)
    row_at = lax.broadcasted_iota(jnp.int32, (ext, LANES), 0)
    top_in = (z > 0).astype(jnp.float32)
    low_in = (z < row_count - 1).astype(jnp.float32)
    row_in = jnp.where(row_at < HALO, top_in, jnp.where(row_at >= HALO + rows, low_in, 1.0))
    k_m = kap_block(p)
    k_s = jnp.where(lane_all < 64, kap_block((p + 1) % 8), kap_block((p + 7) % 8)) * side_in
    turned = [pltpu.roll(k, 1, 1) for k in (k_m, k_s)]
    turned_up = [pltpu.roll(k, LANES - 1, 1) for k in (k_m, k_s)]
    for side, k in enumerate((k_m, k_s)):
        north = 0.5 * (k + pltpu.roll(k, ext - 1, 0))
        south = 0.5 * (k + pltpu.roll(k, 1, 0))
        east = 0.5 * (k + jnp.where(lane_all == LANES - 1, turned_up[1 - side], turned_up[side]))
        west = 0.5 * (k + jnp.where(lane_all == 0, turned[1 - side], turned[side]))
        diagonal = north + south + east + west + (courant_rows + courant_cols)
        inside = row_in if side == 0 else row_in * side_in
        parts = (north, south + courant_rows, east, west + courant_cols, diagonal, inside)
        for number, part in enumerate(parts):
            u_a[pl.ds((side * 6 + number) * ext, ext), :] = part

    shift_a, shift_b, shift_turn = sublane_constants()
    shift_square = shift_turn * shift_turn
    upper = lax.broadcasted_iota(jnp.int32, (8, LANES), 0) < 4

    def tile_at(index):
        return pl.ds(pl.multiple_of(8 * index, 8), 8)

    def inverses(wide, scale):
        diag_a, diag_b = wide + shift_a, wide + shift_b
        scale_a = scale / (diag_a * diag_a + shift_square)
        scale_b = scale / (diag_b * diag_b + shift_square)
        return diag_a * scale_a, diag_b * scale_b, shift_turn * scale_a

    def spread(g, carry):
        both = [
            [
                u_a[pl.ds(pl.multiple_of(number * ext + half + 8 * g, 8), 8), :]
                for half in (0, pairs)
            ]
            for number in range(6)
        ]
        for i in range(8):
            at = pl.ds(pl.multiple_of(64 * g + 8 * i, 8), 8)
            wide = [
                jnp.where(
                    upper,
                    jnp.broadcast_to(first[i : i + 1, :], (8, LANES)),
                    jnp.broadcast_to(second[i : i + 1, :], (8, LANES)),
                )
                for first, second in both
            ]
            for number in range(4):
                coef[number, at, :] = wide[number]
            for number, value in enumerate(inverses(wide[4], wide[5])):
                inv[number, at, :] = value
        return carry

    lax.fori_loop(0, pairs // 8, spread, 0)

    def spread_sides(jj, carry):
        wide = []
        for number in range(6):
            total = jnp.zeros((8, LANES), jnp.float32)
            for m in range(8):
                row = (6 + number) * ext + packs * m + jj
                line = jnp.where(
                    upper,
                    jnp.broadcast_to(u_a[pl.ds(row, 1), :], (8, LANES)),
                    jnp.broadcast_to(u_a[pl.ds(row + pairs, 1), :], (8, LANES)),
                )
                total = jnp.where(lane // 16 == m, pltpu.roll(line, (16 * m + 8) % LANES, 1), total)
            wide.append(total)
        at = tile_at(jj)
        for number in range(4):
            coef_s[number, at, :] = wide[number]
        for number, value in enumerate(inverses(wide[4], wide[5])):
            inv_s[number, at, :] = value
        return carry

    lax.fori_loop(0, packs, spread_sides, 0)

    own_rhs.wait()
    for d in range(1, 8):
        go_arrival(d).wait_recv()

    log_alpha = math.log(circulant_alpha)

    def strided(block, f, pad):
        half, pair = lax.div(block, packs), 8 * lax.rem(block, packs)
        return pl.ds(8 * (pair + pad) + 4 * half + f % 4, 8, stride=8)

    def transform(g, carry):
        tile = tile_at(g)
        steps = [arrived[t, tile, :] * math.exp(log_alpha * t / 8) for t in range(8)]
        edges = jnp.zeros((8, LANES), jnp.float32)
        for f, value in enumerate(forward_eight(steps)):
            rhs_f[f // 4, strided(g + 1, f, 0), :] = value
            edges = jnp.where(lane // 16 == f, pltpu.roll(value, 8 + 16 * f, 1), edges)
            fields[g, f] = value
        packed[tile, :] = edges
        return carry

    lax.fori_loop(0, groups, transform, 0)

    def halo_copy(number):
        dp, dz = SIDES[number]
        if dp == 0:
            source = fields.at[0 if dz < 0 else groups - 1]
        else:
            first, count = {0: (0, groups), -1: (0, 1), 1: (groups - 1, 1)}[dz]
            source = packed.at[pl.ds(8 * first, 8 * count)]
        copy = pltpu.make_async_remote_copy(
            src_ref=source, dst_ref=halo_target(number),
            send_sem=halo_s.at[number], recv_sem=halo_r.at[number],
            device_id=neighbour(dp, dz), device_id_type=mesh_id,
        )
        return copy

    def halo_target(number):
        dp, dz = SIDES[number]
        if dp == 0:
            return row_in_f.at[1 if dz < 0 else 0]
        last, count = {0: (1, groups), -1: (groups + 1, 1), 1: (0, 1)}[dz]
        return (from_right if dp < 0 else from_left).at[pl.ds(8 * last, 8 * count)]

    for number, (dp, dz) in enumerate(SIDES):
        @pl.when(there(dp, dz))
        def _():
            halo_copy(number).start()

    for number, (dp, dz) in enumerate(SIDES):
        @pl.when(there(-dp, -dz))
        def _():
            halo_copy(number).wait_recv()

        @pl.when(jnp.logical_not(there(-dp, -dz)))
        def _():
            target = halo_target(number)
            target[...] = jnp.zeros(target.shape, jnp.float32)

    weights = step_weights(DEGREE) * SWEEPS
    def place_rows(g, carry):
        for f in range(8):
            rhs_f[f // 4, strided(g * (groups + 1), f, 0), :] = row_in_f[g, f]
        return carry

    lax.fori_loop(0, 2, place_rows, 0)

    def place_sides(g, carry):
        tile = tile_at(g)
        both = jnp.where(lane % 16 < 8, from_left[tile, :], from_right[tile, :])
        for f in range(8):
            spare[f // 4, strided(g, f, 0), :] = pltpu.roll(both, 120 - 16 * f, 1)
        return carry

    lax.fori_loop(0, ext // 8, place_sides, 0)

    def pack_sides(jj, carry):
        for part in range(2):
            total = jnp.zeros((8, LANES), jnp.float32)
            for m in range(8):
                line = spare[part, tile_at(jj + packs * m), :]
                total = jnp.where(lane // 16 == m, pltpu.roll(line, (16 * m + 8) % LANES, 1), total)
            side_f[part, tile_at(jj), :] = total
        return carry

    lax.fori_loop(0, packs, pack_sides, 0)

    def close(slot):
        for part in range(2):
            base = 2 * slot + part
            first = v[base, pl.ds(8, 8), :]
            final = v[base, pl.ds(8 * pairs, 8), :]
            v[base, pl.ds(0, 8), :] = pltpu.roll(final, 4, 0)
            v[base, pl.ds(8 * pairs + 8, 8), :] = pltpu.roll(first, 4, 0)
            first = v_s[base, pl.ds(8, 8), :]
            final = v_s[base, pl.ds(8 * packs, 8), :]
            first = jnp.where(lane < 16, pltpu.roll(first, 4, 0), first)
            final = jnp.where(lane >= 112, pltpu.roll(final, 4, 0), final)
            v_s[base, pl.ds(0, 8), :] = pltpu.roll(final, 16, 1)
            v_s[base, pl.ds(8 * packs + 8, 8), :] = pltpu.roll(first, 112, 1)

    def corrected(totals, inv_ref, at):
        turn = inv_ref[2, at, :]
        return (
            inv_ref[0, at, :] * totals[0] + turn * totals[1],
            inv_ref[1, at, :] * totals[1] - turn * totals[0],
        )

    def begin(right, inv_ref, new):
        def body(j, carry):
            changes = corrected([right[part, tile_at(j), :] for part in range(2)], inv_ref, tile_at(j))
            for part in range(2):
                new[part, tile_at(j + 1), :] = weights[0] * changes[part]
            return carry

        return body

    def update(j, right, coef_ref, inv_ref, state, old, new, rights, lefts, weight):
        at, mid, after = tile_at(j), tile_at(j + 1), tile_at(j + 2)
        north, south, east, west = [coef_ref[n, at, :] for n in range(4)]
        totals = [
            (right[part, at, :] + north * state[old + part, after, :])
            + (south * state[old + part, at, :] + east * rights[part])
            + west * lefts[part]
            for part in range(2)
        ]
        changes = corrected(totals, inv_ref, at)
        for part in range(2):
            kept = (1.0 - weight) * state[old + part, mid, :]
            state[new + part, mid, :] = kept + weight * changes[part]

    lax.fori_loop(0, pairs, begin(rhs_f, inv, v), 0, unroll=8)
    lax.fori_loop(0, packs, begin(side_f, inv_s, v_s), 0, unroll=packs)
    close(0)

    def step(number, carry):
        old = 2 * lax.rem(number + 1, 2)
        new = 2 - old
        which = lax.rem(number, DEGREE)
        weight = jnp.float32(weights[0])
        for at in range(1, DEGREE):
            weight = jnp.where(which == at, jnp.float32(weights[at]), weight)

        def group(jj, carry):
            edges = [v_s[old + part, tile_at(jj + 1), :] for part in range(2)]
            inner = list(edges)
            for m in range(8):
                j = jj + packs * m
                rights, lefts = [], []
                for part in range(2):
                    here = v[old + part, tile_at(j + 1), :]
                    outer = pltpu.roll(edges[part], 120 - 16 * m, 1)
                    rights.append(pltpu.roll(jnp.where(lane == 0, outer, here), LANES - 1, 1))
                    lefts.append(pltpu.roll(jnp.where(lane == LANES - 1, outer, here), 1, 1))
                    moved = pltpu.roll(here, (16 * m + 8) % LANES, 1)
                    inner[part] = jnp.where(lane // 16 == m, moved, inner[part])
                update(j, rhs_f, coef, inv, v, old, new, rights, lefts, weight)
            rights = [
                pltpu.roll(jnp.where(lane % 16 == 8, inner[part], edges[part]), LANES - 1, 1)
                for part in range(2)
            ]
            lefts = [
                pltpu.roll(jnp.where(lane % 16 == 7, inner[part], edges[part]), 1, 1)
                for part in range(2)
            ]
            update(jj, side_f, coef_s, inv_s, v_s, old, new, rights, lefts, weight)
            return carry

        lax.fori_loop(0, packs, group, 0)
        close(lax.div(new, 2))
        return carry

    lax.fori_loop(1, len(weights), step, 0)
    final = 2 * ((len(weights) - 1) % 2)

    def inverse(g, carry):
        found = [v[final + f // 4, strided(g + 1, f, 1), :] for f in range(8)]
        for t, value in enumerate(backward_eight(found)):
            leaving[t, tile_at(g), :] = value * (math.exp(-log_alpha * t / 8) / 8)
        return carry

    lax.fori_loop(0, groups, inverse, 0)

    columns = pl.ds(pl.multiple_of(p * LANES, LANES), LANES)

    def back_copy(d):
        peer = (me + d) % 8
        return pltpu.make_async_remote_copy(
            src_ref=leaving.at[peer], dst_ref=out.at[:, columns],
            send_sem=back_s.at[d], recv_sem=back_r.at[d],
            device_id=(peer, z), device_id_type=mesh_id,
        )

    def back_arrival(d):
        peer = (me + 8 - d) % 8
        theirs = pl.ds(pl.multiple_of(patch_place(peer) * LANES, LANES), LANES)
        return pltpu.make_async_remote_copy(
            src_ref=leaving.at[peer], dst_ref=out.at[:, theirs],
            send_sem=back_s.at[d], recv_sem=back_r.at[d],
            device_id=(peer, z), device_id_type=mesh_id,
        )

    for d in range(1, 8):
        back_copy(d).start()
    own_out = pltpu.make_async_copy(leaving.at[me], out.at[:, columns], local.at[2])
    own_out.start()

    for dz in (-1, 1):
        @pl.when(there(0, dz))
        def _():
            kap_copy(dz).wait_send()

    for d in range(1, 8):
        go_copy(d).wait_send()
    for number, (dp, dz) in enumerate(SIDES):
        @pl.when(there(dp, dz))
        def _():
            halo_copy(number).wait_send()

    own_out.wait()
    for d in range(1, 8):
        back_arrival(d).wait_recv()
    for d in range(1, 8):
        back_copy(d).wait_send()


def patch_body(row_count, right_side, kappa):
    rows, width = kappa.shape
    ext = rows + 2 * HALO
    f32 = jnp.float32
    dma = pltpu.SemaphoreType.DMA
    result = pl.pallas_call(
        functools.partial(patch_kernel, rows, row_count),
        out_shape=jax.ShapeDtypeStruct((rows, width), f32),
        in_specs=[pl.BlockSpec(memory_space=pl.ANY)] * 2,
        out_specs=pl.BlockSpec(memory_space=pltpu.VMEM),
        scratch_shapes=[
            pltpu.VMEM((8, rows, LANES), f32),
            pltpu.VMEM((8, rows, LANES), f32),
            pltpu.VMEM((ext, width), f32),
            pltpu.VMEM((2, 4 * ext, LANES), f32),
            pltpu.VMEM((4, 4 * (ext + 4), LANES), f32),
            pltpu.VMEM((12 * ext, LANES), f32),
            pltpu.VMEM((4, 4 * ext, LANES), f32),
            pltpu.VMEM((3, 4 * ext, LANES), f32),
            pltpu.VMEM((2, ext // 2, LANES), f32),
            pltpu.VMEM((2, 4 * ext, LANES), f32),
            pltpu.VMEM((4, ext // 2 + 16, LANES), f32),
            pltpu.VMEM((4, ext // 2, LANES), f32),
            pltpu.VMEM((3, ext // 2, LANES), f32),
            pltpu.VMEM((rows, LANES), f32),
            pltpu.VMEM((ext, LANES), f32),
            pltpu.VMEM((ext, LANES), f32),
            pltpu.VMEM((rows // 8, 8, HALO, LANES), f32),
            pltpu.VMEM((2, 8, HALO, LANES), f32),
            dma((8,)), dma((8,)), dma((8,)), dma((8,)), dma((8,)), dma((8,)),
            dma((2,)), dma((2,)), dma((3,)),
        ],
        compiler_params=pltpu.CompilerParams(
            collective_id=0, has_side_effects=True, vmem_limit_bytes=60 * 2**20
        ),
        name="patch_solve",
    )(right_side.reshape(rows, width), kappa)
    return result.reshape(right_side.shape)


def solution(mesh):
    placed = (P("tm", "row", None), P("row", None))
    tm_size, row_count = mesh.shape["tm"], mesh.shape["row"]

    def local(right_side, kappa):
        fits = (
            tm_size == 8 and right_side.shape[0] == 1
            and kappa.shape[1] == tm_size * LANES and kappa.shape[0] % 16 == 0
        )
        if fits:
            return patch_body(row_count, right_side, kappa)
        return body(right_side, kappa)

    return jax.shard_map(
        local, mesh=mesh, in_specs=placed, out_specs=P("tm", "row", None), check_vma=False
    )
```

```python
import functools
import math

import jax
import jax.numpy as jnp
from jax import lax
from jax.experimental import pallas as pl
from jax.experimental.pallas import tpu as pltpu
from jax.sharding import PartitionSpec as P

SWEEPS = 2
DEGREE = 4


circulant_alpha = 0.05
courant_rows = 0.5
courant_cols = 0.25
cheb_centre = 1.0
cheb_half = 0.7


def from_partner(value, axis, bit):
    mask = 2**bit
    pairs = [(source, source ^ mask) for source in range(lax.axis_size(axis))]
    return lax.ppermute(value, axis, pairs)


def padded_2(block, sides, width):
    for axis, dim in sides:
        count = lax.axis_size(axis)
        forward = [(i, i + 1) for i in range(count - 1)]
        backward = [(target, source) for source, target in forward]
        low = lax.ppermute(
            lax.slice_in_dim(block, block.shape[dim] - width, None, axis=dim), axis, forward
        )
        high = lax.ppermute(lax.slice_in_dim(block, 0, width, axis=dim), axis, backward)
        block = jnp.concatenate([low, block, high], axis=dim)
    return block


def step_weights(count):
    return [
        1.0 / (cheb_centre + cheb_half * math.cos(math.pi * (2 * number + 1) / (2 * count)))
        for number in range(count)
    ]


def face_terms(kappa_rows):
    padded = jnp.pad(kappa_rows, ((0, 0), (1, 1)))
    centre = padded[1:-1, 1:-1]
    north = 0.5 * (centre + padded[2:, 1:-1])
    south = 0.5 * (centre + padded[:-2, 1:-1])
    east = 0.5 * (centre + padded[1:-1, 2:])
    west = 0.5 * (centre + padded[1:-1, :-2])
    diagonal = north + south + east + west + (courant_rows + courant_cols)
    return (north, south, east, west, diagonal)


def spatial(extended, faces):
    north, south, east, west, diagonal = faces
    padded = jnp.pad(extended, ((0, 0), (0, 0), (0, 0), (1, 1)))
    centre = padded[:, :, 1:-1, 1:-1]
    above = padded[:, :, 2:, 1:-1]
    below = padded[:, :, :-2, 1:-1]
    after = padded[:, :, 1:-1, 2:]
    before = padded[:, :, 1:-1, :-2]
    coupled = north * above + south * below + east * after + west * before
    return diagonal * centre - coupled - courant_rows * below - courant_cols * before


def rotate(pair, cosine, sine):
    return jnp.stack([pair[0] * cosine - pair[1] * sine, pair[0] * sine + pair[1] * cosine])


def short_transform(pair, sign):
    count = pair.shape[1]
    index = jnp.arange(count, dtype=jnp.int32)
    angles = 2.0 * math.pi / count * (index[:, None] * index[None, :] % count).astype(jnp.float32)
    cosine = jnp.cos(angles)
    sine = sign * jnp.sin(angles)
    highest = lax.Precision.HIGHEST
    real = jnp.einsum("kj,jrc->krc", cosine, pair[0], precision=highest) - jnp.einsum(
        "kj,jrc->krc", sine, pair[1], precision=highest
    )
    imag = jnp.einsum("kj,jrc->krc", cosine, pair[1], precision=highest) + jnp.einsum(
        "kj,jrc->krc", sine, pair[0], precision=highest
    )
    return jnp.stack([real, imag])


def bit_reversed(device, levels):
    total = jnp.zeros((), jnp.int32)
    for place in range(levels):
        total = total + device // 2**place % 2 * 2 ** (levels - 1 - place)
    return total


def forward_pairs(scaled, device, levels, tm_size, total_steps):
    place = levels - 1
    half = 2**place
    lower = device // half % 2 == 1
    angle = -math.pi / half * (device % half).astype(jnp.float32)
    partner = from_partner(scaled, "tm", place)
    summed = scaled + partner
    differ = partner - scaled
    real = jnp.where(lower, differ * jnp.cos(angle), summed)
    imag = jnp.where(lower, differ * jnp.sin(angle), jnp.zeros_like(summed))
    state = jnp.stack([real, imag])
    for place in range(levels - 2, -1, -1):
        half = 2**place
        lower = device // half % 2 == 1
        angle = -math.pi / half * (device % half).astype(jnp.float32)
        partner = from_partner(state, "tm", place)
        summed = state + partner
        rotated = rotate(partner - state, jnp.cos(angle), jnp.sin(angle))
        state = jnp.where(lower, rotated, summed)
    first_index = bit_reversed(device, levels)
    steps_dev = scaled.shape[0]
    local_steps = jnp.arange(steps_dev, dtype=jnp.int32)
    twist = (
        -2.0 * math.pi / total_steps * (local_steps * first_index % total_steps).astype(jnp.float32)
    )
    state = rotate(state, jnp.cos(twist)[:, None, None], jnp.sin(twist)[:, None, None])
    spectrum = short_transform(state, -1.0)
    frequencies = first_index + tm_size * local_steps
    return (spectrum, frequencies)


def backward_pairs(solved, device, levels, total_steps):
    steps_dev = solved.shape[1]
    first_index = bit_reversed(device, levels)
    state = short_transform(solved, 1.0) * (1.0 / steps_dev)
    local_steps = jnp.arange(steps_dev, dtype=jnp.int32)
    twist = (
        2.0 * math.pi / total_steps * (local_steps * first_index % total_steps).astype(jnp.float32)
    )
    state = rotate(state, jnp.cos(twist)[:, None, None], jnp.sin(twist)[:, None, None])
    for place in range(0, levels - 1):
        half = 2**place
        lower = device // half % 2 == 1
        angle = math.pi / half * (device % half).astype(jnp.float32)
        cosine = jnp.cos(angle)
        sine = jnp.sin(angle)
        partner = from_partner(state, "tm", place)
        upper_value = (state + rotate(partner, cosine, sine)) * 0.5
        lower_value = (partner - rotate(state, cosine, sine)) * 0.5
        state = jnp.where(lower, lower_value, upper_value)
    place = levels - 1
    half = 2**place
    lower = device // half % 2 == 1
    angle = math.pi / half * (device % half).astype(jnp.float32)
    own_turned = state[0] * jnp.cos(angle) - state[1] * jnp.sin(angle)
    outgoing = jnp.where(lower, own_turned, state[0])
    received = from_partner(outgoing, "tm", place)
    return jnp.where(lower, (received - own_turned) * 0.5, (state[0] + received) * 0.5)


def shift_terms(frequencies, faces, total_steps):
    decay = circulant_alpha ** (1.0 / total_steps)
    theta = 2.0 * math.pi / total_steps * frequencies.astype(jnp.float32)
    shift_real = (1.0 - decay * jnp.cos(theta))[:, None, None]
    shift_imag = (decay * jnp.sin(theta))[:, None, None]
    diag_real = shift_real + faces[4]
    magnitude = diag_real * diag_real + shift_imag * shift_imag
    return (shift_real, shift_imag, diag_real / magnitude, -shift_imag / magnitude)


def solve_each(spectrum, frequencies, kappa):
    total_steps = spectrum.shape[1] * lax.axis_size("tm")
    kappa_rows = padded_2(kappa, (("row", 0),), 1)
    faces = face_terms(kappa_rows)
    shift_real, shift_imag, inv_real, inv_imag = shift_terms(frequencies, faces, total_steps)
    state = jnp.zeros_like(spectrum)
    first = True
    for sweep in range(SWEEPS):
        for weight in step_weights(DEGREE):
            if first:
                residual = spectrum
                first = False
            else:
                extended = padded_2(state, (("row", 2),), 1)
                image = spatial(extended, faces)
                image_real = shift_real * state[0] - shift_imag * state[1] + image[0]
                image_imag = shift_real * state[1] + shift_imag * state[0] + image[1]
                residual = spectrum - jnp.stack([image_real, image_imag])
            corr_real = inv_real * residual[0] - inv_imag * residual[1]
            corr_imag = inv_real * residual[1] + inv_imag * residual[0]
            state = state + weight * jnp.stack([corr_real, corr_imag])
    return state


def solve_block(spectrum, frequencies, kappa):
    return solve_each(spectrum, frequencies, kappa)


def body(right_side, kappa):
    steps_dev = right_side.shape[0]
    tm_size = lax.axis_size("tm")
    total_steps = steps_dev * tm_size
    device = lax.axis_index("tm")
    local_steps = jnp.arange(steps_dev, dtype=jnp.int32)
    global_steps = device * steps_dev + local_steps
    log_alpha = math.log(circulant_alpha)
    step_float = global_steps.astype(jnp.float32)
    scaled = right_side * jnp.exp(log_alpha * step_float / total_steps)[:, None, None]
    levels = tm_size.bit_length() - 1
    spectrum, frequencies = forward_pairs(scaled, device, levels, tm_size, total_steps)
    solved = solve_block(spectrum, frequencies, kappa)
    signal = backward_pairs(solved, device, levels, total_steps)
    return signal * jnp.exp(-log_alpha * step_float / total_steps)[:, None, None]


LANES = 128
HALO = 8
SIDES = [(0, -1), (0, 1), (-1, 0), (-1, -1), (-1, 1), (1, 0), (1, -1), (1, 1)]


def patch_place(index):
    chip = index // 2
    return 2 * (chip + chip // 2 * (5 - 2 * chip)) + index % 2


def sublane_constants():
    field = lax.broadcasted_iota(jnp.int32, (8, LANES), 0) & 3
    decay = circulant_alpha ** (1.0 / 8)
    real = jnp.zeros((8, LANES), jnp.float32)
    turn = jnp.zeros((8, LANES), jnp.float32)
    for k in (1, 2, 3):
        theta = 2.0 * math.pi * k / 8
        real = jnp.where(field == k, 1.0 - decay * math.cos(theta), real)
        turn = jnp.where(field == k, decay * math.sin(theta), turn)
    real_a = jnp.where(field == 0, 1.0 - decay, real)
    real_b = jnp.where(field == 0, 1.0 + decay, real)
    return real_a, real_b, turn


def forward_eight(x):
    root = math.sqrt(0.5)
    s = [x[t] + x[t + 4] for t in range(4)]
    d = [x[t] - x[t + 4] for t in range(4)]
    even, odd = s[0] + s[2], s[1] + s[3]
    less, more = root * (d[1] - d[3]), root * (d[1] + d[3])
    return [
        even + odd, d[0] + less, s[0] - s[2], d[0] - less,
        even - odd, -d[2] - more, s[3] - s[1], d[2] - more,
    ]


def backward_eight(f):
    root = math.sqrt(0.5)
    x0, r1, r2, r3, x4, i1, i2, i3 = f
    plus, minus = x0 + x4, x0 - x4
    even = [plus + 2.0 * r2, minus - 2.0 * i2, plus - 2.0 * r2, minus + 2.0 * i2]
    less, total = r1 - r3, i1 + i3
    odd = [
        2.0 * (r1 + r3), 2.0 * root * (less - total),
        2.0 * (i3 - i1), -2.0 * root * (less + total),
    ]
    return [even[t] + odd[t] for t in range(4)] + [even[t] - odd[t] for t in range(4)]


def patch_kernel(
    rows, row_count, rhs, kappa, out,
    arrived, leaving, kap, rhs_f, v, u_a,
    coef, inv, side_f, spare, v_s, coef_s, inv_s, packed, from_left, from_right, fields, row_in_f,
    go_s, go_r, back_s, back_r, halo_s, halo_r, kap_s, kap_r, local,
):
    mesh_id = pl.DeviceIdType.MESH
    me, z = lax.axis_index("tm"), lax.axis_index("row")
    p = patch_place(me)
    ext = rows + 2 * HALO
    groups = rows // 8
    pairs = ext // 2
    packs = pairs // 8

    def there(dp, dz):
        ok = None
        for delta, at, count in ((dp, p, 8), (dz, z, row_count)):
            if delta:
                good = at > 0 if delta < 0 else at < count - 1
                ok = good if ok is None else jnp.logical_and(ok, good)
        return ok

    def neighbour(dp, dz):
        return (patch_place((p + dp + 8) % 8), z + dz)

    barrier = pltpu.get_barrier_semaphore()
    for d in range(1, 8):
        pl.semaphore_signal(barrier, inc=1, device_id=((me + d) % 8, z), device_id_type=mesh_id)
    expected = jnp.int32(7)
    for dp, dz in SIDES:
        if dz == 0:
            continue
        ok = there(dp, dz)
        expected = expected + ok.astype(jnp.int32)

        @pl.when(ok)
        def _():
            pl.semaphore_signal(
                barrier, inc=1, device_id=neighbour(dp, dz), device_id_type=mesh_id
            )

    own_rhs = pltpu.make_async_copy(
        rhs.at[:, pl.ds(pl.multiple_of(p * LANES, LANES), LANES)], arrived.at[me], local.at[0]
    )
    own_kap = pltpu.make_async_copy(kappa, kap.at[pl.ds(HALO, rows)], local.at[1])
    own_rhs.start()
    own_kap.start()
    pl.semaphore_wait(barrier, expected)

    def go_copy(d):
        peer = (me + d) % 8
        columns = pl.ds(pl.multiple_of(patch_place(peer) * LANES, LANES), LANES)
        return pltpu.make_async_remote_copy(
            src_ref=rhs.at[:, columns], dst_ref=arrived.at[me],
            send_sem=go_s.at[d], recv_sem=go_r.at[d],
            device_id=(peer, z), device_id_type=mesh_id,
        )

    def go_arrival(d):
        peer = (me + 8 - d) % 8
        return pltpu.make_async_remote_copy(
            src_ref=rhs.at[:, pl.ds(0, LANES)], dst_ref=arrived.at[peer],
            send_sem=go_s.at[d], recv_sem=go_r.at[d],
            device_id=(peer, z), device_id_type=mesh_id,
        )

    def kap_copy(dz):
        first, last = (0, HALO + rows) if dz < 0 else (rows - HALO, 0)
        which = (dz + 1) // 2
        return pltpu.make_async_remote_copy(
            src_ref=kappa.at[pl.ds(first, HALO)], dst_ref=kap.at[pl.ds(last, HALO)],
            send_sem=kap_s.at[which], recv_sem=kap_r.at[which],
            device_id=(me, z + dz), device_id_type=mesh_id,
        )

    for dz in (-1, 1):
        @pl.when(there(0, dz))
        def _():
            kap_copy(dz).start()

    for d in range(1, 8):
        go_copy(d).start()

    own_kap.wait()
    for dz in (-1, 1):
        lost = HALO + rows if dz < 0 else 0

        @pl.when(there(0, -dz))
        def _():
            kap_copy(dz).wait_recv()

        @pl.when(jnp.logical_not(there(0, -dz)))
        def _():
            kap[pl.ds(lost, HALO), :] = jnp.zeros((HALO, kap.shape[1]), jnp.float32)

    lane = lax.broadcasted_iota(jnp.int32, (8, LANES), 1)
    lane_group, lane_place = lane & 112, lane & 15
    lane_all = lax.broadcasted_iota(jnp.int32, (ext, LANES), 1)

    def kap_block(which):
        return kap[:, pl.ds(pl.multiple_of(which * LANES, LANES), LANES)]

    right_in = (p < 7).astype(jnp.float32)
    left_in = (p > 0).astype(jnp.float32)
    side_in = jnp.where(lane_all < 64, right_in, left_in)
    row_at = lax.broadcasted_iota(jnp.int32, (ext, LANES), 0)
    top_in = (z > 0).astype(jnp.float32)
    low_in = (z < row_count - 1).astype(jnp.float32)
    row_in = jnp.where(row_at < HALO, top_in, jnp.where(row_at >= HALO + rows, low_in, 1.0))
    k_m = kap_block(p)
    k_s = jnp.where(lane_all < 64, kap_block((p + 1) % 8), kap_block((p + 7) % 8)) * side_in
    turned = [pltpu.roll(k, 1, 1) for k in (k_m, k_s)]
    turned_up = [pltpu.roll(k, LANES - 1, 1) for k in (k_m, k_s)]
    for side, k in enumerate((k_m, k_s)):
        north = 0.5 * (k + pltpu.roll(k, ext - 1, 0))
        south = 0.5 * (k + pltpu.roll(k, 1, 0))
        east = 0.5 * (k + jnp.where(lane_all == LANES - 1, turned_up[1 - side], turned_up[side]))
        west = 0.5 * (k + jnp.where(lane_all == 0, turned[1 - side], turned[side]))
        diagonal = north + south + east + west + (courant_rows + courant_cols)
        inside = row_in if side == 0 else row_in * side_in
        parts = (north, south + courant_rows, east, west + courant_cols, diagonal, inside)
        for number, part in enumerate(parts):
            u_a[pl.ds((side * 6 + number) * ext, ext), :] = part

    shift_a, shift_b, shift_turn = sublane_constants()
    shift_square = shift_turn * shift_turn
    upper = lax.broadcasted_iota(jnp.int32, (8, LANES), 0) < 4

    def tile_at(index):
        return pl.ds(pl.multiple_of(8 * index, 8), 8)

    def inverses(wide, scale):
        diag_a, diag_b = wide + shift_a, wide + shift_b
        scale_a = scale / (diag_a * diag_a + shift_square)
        scale_b = scale / (diag_b * diag_b + shift_square)
        return diag_a * scale_a, diag_b * scale_b, shift_turn * scale_a

    def spread(g, carry):
        both = [
            [
                u_a[pl.ds(pl.multiple_of(number * ext + half + 8 * g, 8), 8), :]
                for half in (0, pairs)
            ]
            for number in range(6)
        ]
        for i in range(8):
            at = pl.ds(pl.multiple_of(64 * g + 8 * i, 8), 8)
            wide = [
                jnp.where(
                    upper,
                    jnp.broadcast_to(first[i : i + 1, :], (8, LANES)),
                    jnp.broadcast_to(second[i : i + 1, :], (8, LANES)),
                )
                for first, second in both
            ]
            for number in range(4):
                coef[number, at, :] = wide[number]
            for number, value in enumerate(inverses(wide[4], wide[5])):
                inv[number, at, :] = value
        return carry

    lax.fori_loop(0, pairs // 8, spread, 0)

    def spread_sides(jj, carry):
        wide = []
        for number in range(6):
            total = jnp.zeros((8, LANES), jnp.float32)
            for m in range(8):
                row = (6 + number) * ext + packs * m + jj
                line = jnp.where(
                    upper,
                    jnp.broadcast_to(u_a[pl.ds(row, 1), :], (8, LANES)),
                    jnp.broadcast_to(u_a[pl.ds(row + pairs, 1), :], (8, LANES)),
                )
                total = jnp.where(lane_group == 16 * m, pltpu.roll(line, (16 * m + 8) % LANES, 1), total)
            wide.append(total)
        at = tile_at(jj)
        for number in range(4):
            coef_s[number, at, :] = wide[number]
        for number, value in enumerate(inverses(wide[4], wide[5])):
            inv_s[number, at, :] = value
        return carry

    lax.fori_loop(0, packs, spread_sides, 0)

    own_rhs.wait()
    for d in range(1, 8):
        go_arrival(d).wait_recv()

    log_alpha = math.log(circulant_alpha)

    def strided(block, f, pad):
        half, pair = lax.div(block, packs), 8 * lax.rem(block, packs)
        return pl.ds(8 * (pair + pad) + 4 * half + f % 4, 8, stride=8)

    def transform(g, carry):
        tile = tile_at(g)
        steps = [arrived[t, tile, :] * math.exp(log_alpha * t / 8) for t in range(8)]
        edges = jnp.zeros((8, LANES), jnp.float32)
        for f, value in enumerate(forward_eight(steps)):
            rhs_f[f // 4, strided(g + 1, f, 0), :] = value
            edges = jnp.where(lane_group == 16 * f, pltpu.roll(value, 8 + 16 * f, 1), edges)
            fields[g, f] = value
        packed[tile, :] = edges
        return carry

    lax.fori_loop(0, groups, transform, 0)

    def halo_copy(number):
        dp, dz = SIDES[number]
        if dp == 0:
            source = fields.at[0 if dz < 0 else groups - 1]
        else:
            first, count = {0: (0, groups), -1: (0, 1), 1: (groups - 1, 1)}[dz]
            source = packed.at[pl.ds(8 * first, 8 * count)]
        copy = pltpu.make_async_remote_copy(
            src_ref=source, dst_ref=halo_target(number),
            send_sem=halo_s.at[number], recv_sem=halo_r.at[number],
            device_id=neighbour(dp, dz), device_id_type=mesh_id,
        )
        return copy

    def halo_target(number):
        dp, dz = SIDES[number]
        if dp == 0:
            return row_in_f.at[1 if dz < 0 else 0]
        last, count = {0: (1, groups), -1: (groups + 1, 1), 1: (0, 1)}[dz]
        return (from_right if dp < 0 else from_left).at[pl.ds(8 * last, 8 * count)]

    for number, (dp, dz) in enumerate(SIDES):
        @pl.when(there(dp, dz))
        def _():
            halo_copy(number).start()

    for number, (dp, dz) in enumerate(SIDES):
        @pl.when(there(-dp, -dz))
        def _():
            halo_copy(number).wait_recv()

        @pl.when(jnp.logical_not(there(-dp, -dz)))
        def _():
            target = halo_target(number)
            target[...] = jnp.zeros(target.shape, jnp.float32)

    weights = step_weights(DEGREE) * SWEEPS
    def place_rows(g, carry):
        for f in range(8):
            rhs_f[f // 4, strided(g * (groups + 1), f, 0), :] = row_in_f[g, f]
        return carry

    lax.fori_loop(0, 2, place_rows, 0)

    def place_sides(g, carry):
        tile = tile_at(g)
        both = jnp.where(lane_place < 8, from_left[tile, :], from_right[tile, :])
        for f in range(8):
            spare[f // 4, strided(g, f, 0), :] = pltpu.roll(both, 120 - 16 * f, 1)
        return carry

    lax.fori_loop(0, ext // 8, place_sides, 0)

    def pack_sides(jj, carry):
        for part in range(2):
            total = jnp.zeros((8, LANES), jnp.float32)
            for m in range(8):
                line = spare[part, tile_at(jj + packs * m), :]
                total = jnp.where(lane_group == 16 * m, pltpu.roll(line, (16 * m + 8) % LANES, 1), total)
            side_f[part, tile_at(jj), :] = total
        return carry

    lax.fori_loop(0, packs, pack_sides, 0)

    def close(slot):
        for part in range(2):
            base = 2 * slot + part
            first = v[base, pl.ds(8, 8), :]
            final = v[base, pl.ds(8 * pairs, 8), :]
            v[base, pl.ds(0, 8), :] = pltpu.roll(final, 4, 0)
            v[base, pl.ds(8 * pairs + 8, 8), :] = pltpu.roll(first, 4, 0)
            first = v_s[base, pl.ds(8, 8), :]
            final = v_s[base, pl.ds(8 * packs, 8), :]
            first = jnp.where(lane < 16, pltpu.roll(first, 4, 0), first)
            final = jnp.where(lane >= 112, pltpu.roll(final, 4, 0), final)
            v_s[base, pl.ds(0, 8), :] = pltpu.roll(final, 16, 1)
            v_s[base, pl.ds(8 * packs + 8, 8), :] = pltpu.roll(first, 112, 1)

    def corrected(totals, inv_ref, at):
        turn = inv_ref[2, at, :]
        return (
            inv_ref[0, at, :] * totals[0] + turn * totals[1],
            inv_ref[1, at, :] * totals[1] - turn * totals[0],
        )

    def begin(right, inv_ref, new):
        def body(j, carry):
            changes = corrected([right[part, tile_at(j), :] for part in range(2)], inv_ref, tile_at(j))
            for part in range(2):
                new[part, tile_at(j + 1), :] = weights[0] * changes[part]
            return carry

        return body

    def update(j, right, coef_ref, inv_ref, state, old, new, rights, lefts, weight):
        at, mid, after = tile_at(j), tile_at(j + 1), tile_at(j + 2)
        north, south, east, west = [coef_ref[n, at, :] for n in range(4)]
        totals = [
            (right[part, at, :] + north * state[old + part, after, :])
            + (south * state[old + part, at, :] + east * rights[part])
            + west * lefts[part]
            for part in range(2)
        ]
        changes = corrected(totals, inv_ref, at)
        for part in range(2):
            kept = (1.0 - weight) * state[old + part, mid, :]
            state[new + part, mid, :] = kept + weight * changes[part]

    lax.fori_loop(0, pairs, begin(rhs_f, inv, v), 0, unroll=8)
    lax.fori_loop(0, packs, begin(side_f, inv_s, v_s), 0, unroll=packs)
    close(0)

    def step(number, carry):
        old = 2 * lax.rem(number + 1, 2)
        new = 2 - old
        which = lax.rem(number, DEGREE)
        weight = jnp.float32(weights[0])
        for at in range(1, DEGREE):
            weight = jnp.where(which == at, jnp.float32(weights[at]), weight)

        def group(jj, carry):
            edges = [v_s[old + part, tile_at(jj + 1), :] for part in range(2)]
            inner = list(edges)
            for m in range(8):
                j = jj + packs * m
                rights, lefts = [], []
                for part in range(2):
                    here = v[old + part, tile_at(j + 1), :]
                    outer = pltpu.roll(edges[part], 120 - 16 * m, 1)
                    rights.append(pltpu.roll(jnp.where(lane == 0, outer, here), LANES - 1, 1))
                    lefts.append(pltpu.roll(jnp.where(lane == LANES - 1, outer, here), 1, 1))
                    moved = pltpu.roll(here, (16 * m + 8) % LANES, 1)
                    inner[part] = jnp.where(lane_group == 16 * m, moved, inner[part])
                update(j, rhs_f, coef, inv, v, old, new, rights, lefts, weight)
            rights = [
                pltpu.roll(jnp.where(lane_place == 8, inner[part], edges[part]), LANES - 1, 1)
                for part in range(2)
            ]
            lefts = [
                pltpu.roll(jnp.where(lane_place == 7, inner[part], edges[part]), 1, 1)
                for part in range(2)
            ]
            update(jj, side_f, coef_s, inv_s, v_s, old, new, rights, lefts, weight)
            return carry

        lax.fori_loop(0, packs, group, 0)
        close(lax.div(new, 2))
        return carry

    lax.fori_loop(1, len(weights), step, 0)
    final = 2 * ((len(weights) - 1) % 2)

    def inverse(g, carry):
        found = [v[final + f // 4, strided(g + 1, f, 1), :] for f in range(8)]
        for t, value in enumerate(backward_eight(found)):
            leaving[t, tile_at(g), :] = value * (math.exp(-log_alpha * t / 8) / 8)
        return carry

    lax.fori_loop(0, groups, inverse, 0)

    columns = pl.ds(pl.multiple_of(p * LANES, LANES), LANES)

    def back_copy(d):
        peer = (me + d) % 8
        return pltpu.make_async_remote_copy(
            src_ref=leaving.at[peer], dst_ref=out.at[:, columns],
            send_sem=back_s.at[d], recv_sem=back_r.at[d],
            device_id=(peer, z), device_id_type=mesh_id,
        )

    def back_arrival(d):
        peer = (me + 8 - d) % 8
        theirs = pl.ds(pl.multiple_of(patch_place(peer) * LANES, LANES), LANES)
        return pltpu.make_async_remote_copy(
            src_ref=leaving.at[peer], dst_ref=out.at[:, theirs],
            send_sem=back_s.at[d], recv_sem=back_r.at[d],
            device_id=(peer, z), device_id_type=mesh_id,
        )

    for d in range(1, 8):
        back_copy(d).start()
    own_out = pltpu.make_async_copy(leaving.at[me], out.at[:, columns], local.at[2])
    own_out.start()

    for dz in (-1, 1):
        @pl.when(there(0, dz))
        def _():
            kap_copy(dz).wait_send()

    for d in range(1, 8):
        go_copy(d).wait_send()
    for number, (dp, dz) in enumerate(SIDES):
        @pl.when(there(dp, dz))
        def _():
            halo_copy(number).wait_send()

    own_out.wait()
    for d in range(1, 8):
        back_arrival(d).wait_recv()
    for d in range(1, 8):
        back_copy(d).wait_send()


def patch_body(row_count, right_side, kappa):
    rows, width = kappa.shape
    ext = rows + 2 * HALO
    f32 = jnp.float32
    dma = pltpu.SemaphoreType.DMA
    result = pl.pallas_call(
        functools.partial(patch_kernel, rows, row_count),
        out_shape=jax.ShapeDtypeStruct((rows, width), f32),
        in_specs=[pl.BlockSpec(memory_space=pl.ANY)] * 2,
        out_specs=pl.BlockSpec(memory_space=pltpu.VMEM),
        scratch_shapes=[
            pltpu.VMEM((8, rows, LANES), f32),
            pltpu.VMEM((8, rows, LANES), f32),
            pltpu.VMEM((ext, width), f32),
            pltpu.VMEM((2, 4 * ext, LANES), f32),
            pltpu.VMEM((4, 4 * (ext + 4), LANES), f32),
            pltpu.VMEM((12 * ext, LANES), f32),
            pltpu.VMEM((4, 4 * ext, LANES), f32),
            pltpu.VMEM((3, 4 * ext, LANES), f32),
            pltpu.VMEM((2, ext // 2, LANES), f32),
            pltpu.VMEM((2, 4 * ext, LANES), f32),
            pltpu.VMEM((4, ext // 2 + 16, LANES), f32),
            pltpu.VMEM((4, ext // 2, LANES), f32),
            pltpu.VMEM((3, ext // 2, LANES), f32),
            pltpu.VMEM((rows, LANES), f32),
            pltpu.VMEM((ext, LANES), f32),
            pltpu.VMEM((ext, LANES), f32),
            pltpu.VMEM((rows // 8, 8, HALO, LANES), f32),
            pltpu.VMEM((2, 8, HALO, LANES), f32),
            dma((8,)), dma((8,)), dma((8,)), dma((8,)), dma((8,)), dma((8,)),
            dma((2,)), dma((2,)), dma((3,)),
        ],
        compiler_params=pltpu.CompilerParams(
            collective_id=0, has_side_effects=True, vmem_limit_bytes=60 * 2**20
        ),
        name="patch_solve",
    )(right_side.reshape(rows, width), kappa)
    return result.reshape(right_side.shape)


def solution(mesh):
    placed = (P("tm", "row", None), P("row", None))
    tm_size, row_count = mesh.shape["tm"], mesh.shape["row"]

    def local(right_side, kappa):
        fits = (
            tm_size == 8 and right_side.shape[0] == 1
            and kappa.shape[1] == tm_size * LANES and kappa.shape[0] % 16 == 0
        )
        if fits:
            return patch_body(row_count, right_side, kappa)
        return body(right_side, kappa)

    return jax.shard_map(
        local, mesh=mesh, in_specs=placed, out_specs=P("tm", "row", None), check_vma=False
    )
```

```python
import functools
import math

import jax
import jax.numpy as jnp
from jax import lax
from jax.experimental import pallas as pl
from jax.experimental.pallas import tpu as pltpu
from jax.sharding import PartitionSpec as P

SWEEPS = 2
DEGREE = 4


circulant_alpha = 0.05
courant_rows = 0.5
courant_cols = 0.25
cheb_centre = 1.0
cheb_half = 0.7


def from_partner(value, axis, bit):
    mask = 2**bit
    pairs = [(source, source ^ mask) for source in range(lax.axis_size(axis))]
    return lax.ppermute(value, axis, pairs)


def padded_2(block, sides, width):
    for axis, dim in sides:
        count = lax.axis_size(axis)
        forward = [(i, i + 1) for i in range(count - 1)]
        backward = [(target, source) for source, target in forward]
        low = lax.ppermute(
            lax.slice_in_dim(block, block.shape[dim] - width, None, axis=dim), axis, forward
        )
        high = lax.ppermute(lax.slice_in_dim(block, 0, width, axis=dim), axis, backward)
        block = jnp.concatenate([low, block, high], axis=dim)
    return block


def step_weights(count):
    return [
        1.0 / (cheb_centre + cheb_half * math.cos(math.pi * (2 * number + 1) / (2 * count)))
        for number in range(count)
    ]


def face_terms(kappa_rows):
    padded = jnp.pad(kappa_rows, ((0, 0), (1, 1)))
    centre = padded[1:-1, 1:-1]
    north = 0.5 * (centre + padded[2:, 1:-1])
    south = 0.5 * (centre + padded[:-2, 1:-1])
    east = 0.5 * (centre + padded[1:-1, 2:])
    west = 0.5 * (centre + padded[1:-1, :-2])
    diagonal = north + south + east + west + (courant_rows + courant_cols)
    return (north, south, east, west, diagonal)


def spatial(extended, faces):
    north, south, east, west, diagonal = faces
    padded = jnp.pad(extended, ((0, 0), (0, 0), (0, 0), (1, 1)))
    centre = padded[:, :, 1:-1, 1:-1]
    above = padded[:, :, 2:, 1:-1]
    below = padded[:, :, :-2, 1:-1]
    after = padded[:, :, 1:-1, 2:]
    before = padded[:, :, 1:-1, :-2]
    coupled = north * above + south * below + east * after + west * before
    return diagonal * centre - coupled - courant_rows * below - courant_cols * before


def rotate(pair, cosine, sine):
    return jnp.stack([pair[0] * cosine - pair[1] * sine, pair[0] * sine + pair[1] * cosine])


def short_transform(pair, sign):
    count = pair.shape[1]
    index = jnp.arange(count, dtype=jnp.int32)
    angles = 2.0 * math.pi / count * (index[:, None] * index[None, :] % count).astype(jnp.float32)
    cosine = jnp.cos(angles)
    sine = sign * jnp.sin(angles)
    highest = lax.Precision.HIGHEST
    real = jnp.einsum("kj,jrc->krc", cosine, pair[0], precision=highest) - jnp.einsum(
        "kj,jrc->krc", sine, pair[1], precision=highest
    )
    imag = jnp.einsum("kj,jrc->krc", cosine, pair[1], precision=highest) + jnp.einsum(
        "kj,jrc->krc", sine, pair[0], precision=highest
    )
    return jnp.stack([real, imag])


def bit_reversed(device, levels):
    total = jnp.zeros((), jnp.int32)
    for place in range(levels):
        total = total + device // 2**place % 2 * 2 ** (levels - 1 - place)
    return total


def forward_pairs(scaled, device, levels, tm_size, total_steps):
    place = levels - 1
    half = 2**place
    lower = device // half % 2 == 1
    angle = -math.pi / half * (device % half).astype(jnp.float32)
    partner = from_partner(scaled, "tm", place)
    summed = scaled + partner
    differ = partner - scaled
    real = jnp.where(lower, differ * jnp.cos(angle), summed)
    imag = jnp.where(lower, differ * jnp.sin(angle), jnp.zeros_like(summed))
    state = jnp.stack([real, imag])
    for place in range(levels - 2, -1, -1):
        half = 2**place
        lower = device // half % 2 == 1
        angle = -math.pi / half * (device % half).astype(jnp.float32)
        partner = from_partner(state, "tm", place)
        summed = state + partner
        rotated = rotate(partner - state, jnp.cos(angle), jnp.sin(angle))
        state = jnp.where(lower, rotated, summed)
    first_index = bit_reversed(device, levels)
    steps_dev = scaled.shape[0]
    local_steps = jnp.arange(steps_dev, dtype=jnp.int32)
    twist = (
        -2.0 * math.pi / total_steps * (local_steps * first_index % total_steps).astype(jnp.float32)
    )
    state = rotate(state, jnp.cos(twist)[:, None, None], jnp.sin(twist)[:, None, None])
    spectrum = short_transform(state, -1.0)
    frequencies = first_index + tm_size * local_steps
    return (spectrum, frequencies)


def backward_pairs(solved, device, levels, total_steps):
    steps_dev = solved.shape[1]
    first_index = bit_reversed(device, levels)
    state = short_transform(solved, 1.0) * (1.0 / steps_dev)
    local_steps = jnp.arange(steps_dev, dtype=jnp.int32)
    twist = (
        2.0 * math.pi / total_steps * (local_steps * first_index % total_steps).astype(jnp.float32)
    )
    state = rotate(state, jnp.cos(twist)[:, None, None], jnp.sin(twist)[:, None, None])
    for place in range(0, levels - 1):
        half = 2**place
        lower = device // half % 2 == 1
        angle = math.pi / half * (device % half).astype(jnp.float32)
        cosine = jnp.cos(angle)
        sine = jnp.sin(angle)
        partner = from_partner(state, "tm", place)
        upper_value = (state + rotate(partner, cosine, sine)) * 0.5
        lower_value = (partner - rotate(state, cosine, sine)) * 0.5
        state = jnp.where(lower, lower_value, upper_value)
    place = levels - 1
    half = 2**place
    lower = device // half % 2 == 1
    angle = math.pi / half * (device % half).astype(jnp.float32)
    own_turned = state[0] * jnp.cos(angle) - state[1] * jnp.sin(angle)
    outgoing = jnp.where(lower, own_turned, state[0])
    received = from_partner(outgoing, "tm", place)
    return jnp.where(lower, (received - own_turned) * 0.5, (state[0] + received) * 0.5)


def shift_terms(frequencies, faces, total_steps):
    decay = circulant_alpha ** (1.0 / total_steps)
    theta = 2.0 * math.pi / total_steps * frequencies.astype(jnp.float32)
    shift_real = (1.0 - decay * jnp.cos(theta))[:, None, None]
    shift_imag = (decay * jnp.sin(theta))[:, None, None]
    diag_real = shift_real + faces[4]
    magnitude = diag_real * diag_real + shift_imag * shift_imag
    return (shift_real, shift_imag, diag_real / magnitude, -shift_imag / magnitude)


def solve_each(spectrum, frequencies, kappa):
    total_steps = spectrum.shape[1] * lax.axis_size("tm")
    kappa_rows = padded_2(kappa, (("row", 0),), 1)
    faces = face_terms(kappa_rows)
    shift_real, shift_imag, inv_real, inv_imag = shift_terms(frequencies, faces, total_steps)
    state = jnp.zeros_like(spectrum)
    first = True
    for sweep in range(SWEEPS):
        for weight in step_weights(DEGREE):
            if first:
                residual = spectrum
                first = False
            else:
                extended = padded_2(state, (("row", 2),), 1)
                image = spatial(extended, faces)
                image_real = shift_real * state[0] - shift_imag * state[1] + image[0]
                image_imag = shift_real * state[1] + shift_imag * state[0] + image[1]
                residual = spectrum - jnp.stack([image_real, image_imag])
            corr_real = inv_real * residual[0] - inv_imag * residual[1]
            corr_imag = inv_real * residual[1] + inv_imag * residual[0]
            state = state + weight * jnp.stack([corr_real, corr_imag])
    return state


def solve_block(spectrum, frequencies, kappa):
    return solve_each(spectrum, frequencies, kappa)


def body(right_side, kappa):
    steps_dev = right_side.shape[0]
    tm_size = lax.axis_size("tm")
    total_steps = steps_dev * tm_size
    device = lax.axis_index("tm")
    local_steps = jnp.arange(steps_dev, dtype=jnp.int32)
    global_steps = device * steps_dev + local_steps
    log_alpha = math.log(circulant_alpha)
    step_float = global_steps.astype(jnp.float32)
    scaled = right_side * jnp.exp(log_alpha * step_float / total_steps)[:, None, None]
    levels = tm_size.bit_length() - 1
    spectrum, frequencies = forward_pairs(scaled, device, levels, tm_size, total_steps)
    solved = solve_block(spectrum, frequencies, kappa)
    signal = backward_pairs(solved, device, levels, total_steps)
    return signal * jnp.exp(-log_alpha * step_float / total_steps)[:, None, None]


LANES = 128
HALO = 8
SIDES = [(0, -1), (0, 1), (-1, 0), (-1, -1), (-1, 1), (1, 0), (1, -1), (1, 1)]


def patch_place(index):
    chip = index // 2
    return 2 * (chip + chip // 2 * (5 - 2 * chip)) + index % 2


def sublane_constants():
    field = lax.broadcasted_iota(jnp.int32, (8, LANES), 0) % 4
    decay = circulant_alpha ** (1.0 / 8)
    real = jnp.zeros((8, LANES), jnp.float32)
    turn = jnp.zeros((8, LANES), jnp.float32)
    for k in (1, 2, 3):
        theta = 2.0 * math.pi * k / 8
        real = jnp.where(field == k, 1.0 - decay * math.cos(theta), real)
        turn = jnp.where(field == k, decay * math.sin(theta), turn)
    real_a = jnp.where(field == 0, 1.0 - decay, real)
    real_b = jnp.where(field == 0, 1.0 + decay, real)
    return real_a, real_b, turn


def forward_eight(x):
    root = math.sqrt(0.5)
    s = [x[t] + x[t + 4] for t in range(4)]
    d = [x[t] - x[t + 4] for t in range(4)]
    even, odd = s[0] + s[2], s[1] + s[3]
    less, more = root * (d[1] - d[3]), root * (d[1] + d[3])
    return [
        even + odd, d[0] + less, s[0] - s[2], d[0] - less,
        even - odd, -d[2] - more, s[3] - s[1], d[2] - more,
    ]


def backward_eight(f):
    root = math.sqrt(0.5)
    x0, r1, r2, r3, x4, i1, i2, i3 = f
    plus, minus = x0 + x4, x0 - x4
    even = [plus + 2.0 * r2, minus - 2.0 * i2, plus - 2.0 * r2, minus + 2.0 * i2]
    less, total = r1 - r3, i1 + i3
    odd = [
        2.0 * (r1 + r3), 2.0 * root * (less - total),
        2.0 * (i3 - i1), -2.0 * root * (less + total),
    ]
    return [even[t] + odd[t] for t in range(4)] + [even[t] - odd[t] for t in range(4)]


def patch_kernel(
    rows, row_count, rhs, kappa, out,
    arrived, leaving, kap, rhs_f, v_a, v_b, u_a,
    coef, inv, packed, from_left, from_right, row_out, row_in_f,
    go_s, go_r, back_s, back_r, halo_s, halo_r, kap_s, kap_r, local,
):
    mesh_id = pl.DeviceIdType.MESH
    me, z = lax.axis_index("tm"), lax.axis_index("row")
    p = patch_place(me)
    ext = rows + 2 * HALO
    groups = rows // 8
    pairs = ext // 2

    def there(dp, dz):
        ok = None
        for delta, at, count in ((dp, p, 8), (dz, z, row_count)):
            if delta:
                good = at > 0 if delta < 0 else at < count - 1
                ok = good if ok is None else jnp.logical_and(ok, good)
        return ok

    def neighbour(dp, dz):
        return (patch_place((p + dp + 8) % 8), z + dz)

    barrier = pltpu.get_barrier_semaphore()
    for d in range(1, 8):
        pl.semaphore_signal(barrier, inc=1, device_id=((me + d) % 8, z), device_id_type=mesh_id)
    expected = jnp.int32(7)
    for dp, dz in SIDES:
        if dz == 0:
            continue
        ok = there(dp, dz)
        expected = expected + ok.astype(jnp.int32)

        @pl.when(ok)
        def _():
            pl.semaphore_signal(
                barrier, inc=1, device_id=neighbour(dp, dz), device_id_type=mesh_id
            )

    own_rhs = pltpu.make_async_copy(
        rhs.at[:, pl.ds(pl.multiple_of(p * LANES, LANES), LANES)], arrived.at[me], local.at[0]
    )
    own_kap = pltpu.make_async_copy(kappa, kap.at[pl.ds(HALO, rows)], local.at[1])
    own_rhs.start()
    own_kap.start()
    pl.semaphore_wait(barrier, expected)

    def go_copy(d):
        peer = (me + d) % 8
        columns = pl.ds(pl.multiple_of(patch_place(peer) * LANES, LANES), LANES)
        return pltpu.make_async_remote_copy(
            src_ref=rhs.at[:, columns], dst_ref=arrived.at[me],
            send_sem=go_s.at[d], recv_sem=go_r.at[d],
            device_id=(peer, z), device_id_type=mesh_id,
        )

    def go_arrival(d):
        peer = (me + 8 - d) % 8
        return pltpu.make_async_remote_copy(
            src_ref=rhs.at[:, pl.ds(0, LANES)], dst_ref=arrived.at[peer],
            send_sem=go_s.at[d], recv_sem=go_r.at[d],
            device_id=(peer, z), device_id_type=mesh_id,
        )

    def kap_copy(dz):
        first, last = (0, HALO + rows) if dz < 0 else (rows - HALO, 0)
        which = (dz + 1) // 2
        return pltpu.make_async_remote_copy(
            src_ref=kappa.at[pl.ds(first, HALO)], dst_ref=kap.at[pl.ds(last, HALO)],
            send_sem=kap_s.at[which], recv_sem=kap_r.at[which],
            device_id=(me, z + dz), device_id_type=mesh_id,
        )

    for dz in (-1, 1):
        @pl.when(there(0, dz))
        def _():
            kap_copy(dz).start()

    for d in range(1, 8):
        go_copy(d).start()

    own_kap.wait()
    for dz in (-1, 1):
        lost = HALO + rows if dz < 0 else 0

        @pl.when(there(0, -dz))
        def _():
            kap_copy(dz).wait_recv()

        @pl.when(jnp.logical_not(there(0, -dz)))
        def _():
            kap[pl.ds(lost, HALO), :] = jnp.zeros((HALO, kap.shape[1]), jnp.float32)

    lane = lax.broadcasted_iota(jnp.int32, (8, LANES), 1)
    lane_group, lane_place = lane & 112, lane & 15
    lane_all = lax.broadcasted_iota(jnp.int32, (ext, LANES), 1)

    def kap_block(which):
        return kap[:, pl.ds(pl.multiple_of(which * LANES, LANES), LANES)]

    right_in = (p < 7).astype(jnp.float32)
    left_in = (p > 0).astype(jnp.float32)
    side_in = jnp.where(lane_all < 64, right_in, left_in)
    row_at = lax.broadcasted_iota(jnp.int32, (ext, LANES), 0)
    top_in = (z > 0).astype(jnp.float32)
    low_in = (z < row_count - 1).astype(jnp.float32)
    row_in = jnp.where(row_at < HALO, top_in, jnp.where(row_at >= HALO + rows, low_in, 1.0))
    k_m = kap_block(p)
    k_s = jnp.where(lane_all < 64, kap_block((p + 1) % 8), kap_block((p + 7) % 8)) * side_in
    turned = [pltpu.roll(k, 1, 1) for k in (k_m, k_s)]
    turned_up = [pltpu.roll(k, LANES - 1, 1) for k in (k_m, k_s)]
    for side, k in enumerate((k_m, k_s)):
        north = 0.5 * (k + pltpu.roll(k, ext - 1, 0))
        south = 0.5 * (k + pltpu.roll(k, 1, 0))
        east = 0.5 * (k + jnp.where(lane_all == LANES - 1, turned_up[1 - side], turned_up[side]))
        west = 0.5 * (k + jnp.where(lane_all == 0, turned[1 - side], turned[side]))
        diagonal = north + south + east + west + (courant_rows + courant_cols)
        inside = row_in if side == 0 else row_in * side_in
        parts = (north, south + courant_rows, east, west + courant_cols, diagonal, inside)
        for number, part in enumerate(parts):
            u_a[pl.ds((side * 6 + number) * ext, ext), :] = part

    shift_a, shift_b, shift_turn = sublane_constants()
    shift_square = shift_turn * shift_turn
    upper = lax.broadcasted_iota(jnp.int32, (8, LANES), 0) < 4

    def spread(g, carry):
        for side in range(2):
            both = [
                [
                    u_a[pl.ds(pl.multiple_of((side * 6 + number) * ext + half + 8 * g, 8), 8), :]
                    for half in (0, pairs)
                ]
                for number in range(6)
            ]
            for i in range(8):
                at = pl.ds(pl.multiple_of(64 * g + 8 * i, 8), 8)
                wide = [
                    jnp.where(
                        upper,
                        jnp.broadcast_to(first[i : i + 1, :], (8, LANES)),
                        jnp.broadcast_to(second[i : i + 1, :], (8, LANES)),
                    )
                    for first, second in both
                ]
                for number in range(4):
                    coef[side * 4 + number, at, :] = wide[number]
                diag_a, diag_b = wide[4] + shift_a, wide[4] + shift_b
                scale_a = wide[5] / (diag_a * diag_a + shift_square)
                scale_b = wide[5] / (diag_b * diag_b + shift_square)
                inv[side * 3, at, :] = diag_a * scale_a
                inv[side * 3 + 1, at, :] = diag_b * scale_b
                inv[side * 3 + 2, at, :] = shift_turn * scale_a
        return carry

    lax.fori_loop(0, pairs // 8, spread, 0)

    own_rhs.wait()
    for d in range(1, 8):
        go_arrival(d).wait_recv()

    log_alpha = math.log(circulant_alpha)

    def strided(row, f, pad):
        half, pair = row // pairs, row % pairs
        return pl.ds(8 * (pair + pad) + 4 * half + f % 4, 8, stride=8)

    for g in range(groups):
        tile = pl.ds(8 * g, 8)
        steps = [arrived[t, tile, :] * math.exp(log_alpha * t / 8) for t in range(8)]
        edges = jnp.zeros((8, LANES), jnp.float32)
        for f, value in enumerate(forward_eight(steps)):
            rhs_f[f // 4, strided(HALO + 8 * g, f, 0), :] = value
            edges = jnp.where(lane_group == 16 * f, pltpu.roll(value, 8 + 16 * f, 1), edges)
            if g == 0:
                row_out[0, f] = value
            if g == groups - 1:
                row_out[1, f] = value
        packed[tile, :] = edges

    def halo_copy(number):
        dp, dz = SIDES[number]
        if dp == 0:
            source = row_out.at[0 if dz < 0 else 1]
        else:
            first, count = {0: (0, groups), -1: (0, 1), 1: (groups - 1, 1)}[dz]
            source = packed.at[pl.ds(8 * first, 8 * count)]
        copy = pltpu.make_async_remote_copy(
            src_ref=source, dst_ref=halo_target(number),
            send_sem=halo_s.at[number], recv_sem=halo_r.at[number],
            device_id=neighbour(dp, dz), device_id_type=mesh_id,
        )
        return copy

    def halo_target(number):
        dp, dz = SIDES[number]
        if dp == 0:
            return row_in_f.at[1 if dz < 0 else 0]
        last, count = {0: (1, groups), -1: (groups + 1, 1), 1: (0, 1)}[dz]
        return (from_right if dp < 0 else from_left).at[pl.ds(8 * last, 8 * count)]

    for number, (dp, dz) in enumerate(SIDES):
        @pl.when(there(dp, dz))
        def _():
            halo_copy(number).start()

    for number, (dp, dz) in enumerate(SIDES):
        @pl.when(there(-dp, -dz))
        def _():
            halo_copy(number).wait_recv()

        @pl.when(jnp.logical_not(there(-dp, -dz)))
        def _():
            target = halo_target(number)
            target[...] = jnp.zeros(target.shape, jnp.float32)

    weights = step_weights(DEGREE) * SWEEPS
    for g in range(ext // 8):
        tile = pl.ds(8 * g, 8)
        both = jnp.where(lane_place < 8, from_left[tile, :], from_right[tile, :])
        for f in range(8):
            at = strided(8 * g, f, 0)
            rhs_f[2 + f // 4, at, :] = pltpu.roll(both, 120 - 16 * f, 1)
            if g == 0:
                rhs_f[f // 4, at, :] = row_in_f[0, f]
            if g == ext // 8 - 1:
                rhs_f[f // 4, at, :] = row_in_f[1, f]

    def close(ref):
        for which in range(4):
            ref[which, pl.ds(0, 8), :] = pltpu.roll(ref[which, pl.ds(8 * pairs, 8), :], 4, 0)
            ref[which, pl.ds(8 * pairs + 8, 8), :] = pltpu.roll(ref[which, pl.ds(8, 8), :], 4, 0)

    chunk = pairs // 2

    def begin(g, carry):
        for i in range(chunk):
            at = pl.ds(pl.multiple_of(8 * chunk * g + 8 * i, 8), 8)
            mid = pl.ds(pl.multiple_of(8 * chunk * g + 8 * i + 8, 8), 8)
            for side in range(2):
                a, b = rhs_f[2 * side, at, :], rhs_f[2 * side + 1, at, :]
                turn = inv[3 * side + 2, at, :]
                v_a[2 * side, mid, :] = weights[0] * (inv[3 * side, at, :] * a + turn * b)
                v_a[2 * side + 1, mid, :] = weights[0] * (inv[3 * side + 1, at, :] * b - turn * a)
        return carry

    lax.fori_loop(0, 2, begin, 0)
    close(v_a)

    def step(old, new, weight, last):
        def body(g, carry):
            def tile_of(which, i):
                return old[which, pl.ds(pl.multiple_of(8 * chunk * g + 8 * i, 8), 8), :]

            before = [tile_of(which, 0) for which in range(4)]
            here = [tile_of(which, 1) for which in range(4)]
            for i in range(chunk):
                at = pl.ds(pl.multiple_of(8 * chunk * g + 8 * i, 8), 8)
                mid = pl.ds(pl.multiple_of(8 * chunk * g + 8 * i + 8, 8), 8)
                after = [tile_of(which, i + 2) for which in range(4)]
                ups = [pltpu.roll(x, LANES - 1, 1) for x in here]
                downs = [pltpu.roll(x, 1, 1) for x in here]
                for side in range(1 if last else 2):
                    north, south, east, west = [coef[4 * side + n, at, :] for n in range(4)]
                    totals = []
                    for part in range(2):
                        own, other = 2 * side + part, 2 * (1 - side) + part
                        right = jnp.where(lane == LANES - 1, ups[other], ups[own])
                        left = jnp.where(lane == 0, downs[other], downs[own])
                        totals.append(
                            (rhs_f[own, at, :] + north * after[own])
                            + (south * before[own] + east * right)
                            + west * left
                        )
                    turn = inv[3 * side + 2, at, :]
                    changes = (
                        inv[3 * side, at, :] * totals[0] + turn * totals[1],
                        inv[3 * side + 1, at, :] * totals[1] - turn * totals[0],
                    )
                    for part in range(2):
                        own = 2 * side + part
                        new[own, mid, :] = (1.0 - weight) * here[own] + weight * changes[part]
                before, here = here, after
            return carry

        lax.fori_loop(0, 2, body, 0)
        if not last:
            close(new)

    def weight_at(number):
        which = lax.rem(number, DEGREE)
        weight = jnp.float32(weights[0])
        for at in range(1, DEGREE):
            weight = jnp.where(which == at, jnp.float32(weights[at]), weight)
        return weight

    def two_steps(number, carry):
        step(v_a, v_b, weight_at(2 * number + 1), False)
        step(v_b, v_a, weight_at(2 * number + 2), False)
        return carry

    lax.fori_loop(0, len(weights) // 2 - 1, two_steps, 0)
    step(v_a, v_b, weights[-1], True)
    old = v_b

    for g in range(groups):
        tile = pl.ds(8 * g, 8)
        fields = [old[f // 4, strided(HALO + 8 * g, f, 1), :] for f in range(8)]
        for t, value in enumerate(backward_eight(fields)):
            leaving[t, tile, :] = value * (math.exp(-log_alpha * t / 8) / 8)

    columns = pl.ds(pl.multiple_of(p * LANES, LANES), LANES)

    def back_copy(d):
        peer = (me + d) % 8
        return pltpu.make_async_remote_copy(
            src_ref=leaving.at[peer], dst_ref=out.at[:, columns],
            send_sem=back_s.at[d], recv_sem=back_r.at[d],
            device_id=(peer, z), device_id_type=mesh_id,
        )

    def back_arrival(d):
        peer = (me + 8 - d) % 8
        theirs = pl.ds(pl.multiple_of(patch_place(peer) * LANES, LANES), LANES)
        return pltpu.make_async_remote_copy(
            src_ref=leaving.at[peer], dst_ref=out.at[:, theirs],
            send_sem=back_s.at[d], recv_sem=back_r.at[d],
            device_id=(peer, z), device_id_type=mesh_id,
        )

    for d in range(1, 8):
        back_copy(d).start()
    own_out = pltpu.make_async_copy(leaving.at[me], out.at[:, columns], local.at[2])
    own_out.start()

    for dz in (-1, 1):
        @pl.when(there(0, dz))
        def _():
            kap_copy(dz).wait_send()

    for d in range(1, 8):
        go_copy(d).wait_send()
    for number, (dp, dz) in enumerate(SIDES):
        @pl.when(there(dp, dz))
        def _():
            halo_copy(number).wait_send()

    own_out.wait()
    for d in range(1, 8):
        back_arrival(d).wait_recv()
    for d in range(1, 8):
        back_copy(d).wait_send()


def patch_body(row_count, right_side, kappa):
    rows, width = kappa.shape
    ext = rows + 2 * HALO
    f32 = jnp.float32
    dma = pltpu.SemaphoreType.DMA
    result = pl.pallas_call(
        functools.partial(patch_kernel, rows, row_count),
        out_shape=jax.ShapeDtypeStruct((rows, width), f32),
        in_specs=[pl.BlockSpec(memory_space=pl.ANY)] * 2,
        out_specs=pl.BlockSpec(memory_space=pltpu.VMEM),
        scratch_shapes=[
            pltpu.VMEM((8, rows, LANES), f32),
            pltpu.VMEM((8, rows, LANES), f32),
            pltpu.VMEM((ext, width), f32),
            pltpu.VMEM((4, 4 * ext, LANES), f32),
            pltpu.VMEM((4, 4 * (ext + 4), LANES), f32),
            pltpu.VMEM((4, 4 * (ext + 4), LANES), f32),
            pltpu.VMEM((12 * ext, LANES), f32),
            pltpu.VMEM((8, 4 * ext, LANES), f32),
            pltpu.VMEM((6, 4 * ext, LANES), f32),
            pltpu.VMEM((rows, LANES), f32),
            pltpu.VMEM((ext, LANES), f32),
            pltpu.VMEM((ext, LANES), f32),
            pltpu.VMEM((2, 8, HALO, LANES), f32),
            pltpu.VMEM((2, 8, HALO, LANES), f32),
            dma((8,)), dma((8,)), dma((8,)), dma((8,)), dma((8,)), dma((8,)),
            dma((2,)), dma((2,)), dma((3,)),
        ],
        compiler_params=pltpu.CompilerParams(
            collective_id=0, has_side_effects=True, vmem_limit_bytes=60 * 2**20
        ),
        name="patch_solve",
    )(right_side.reshape(rows, width), kappa)
    return result.reshape(right_side.shape)


def solution(mesh):
    placed = (P("tm", "row", None), P("row", None))
    tm_size, row_count = mesh.shape["tm"], mesh.shape["row"]

    def local(right_side, kappa):
        fits = (
            tm_size == 8 and right_side.shape[0] == 1
            and kappa.shape[1] == tm_size * LANES and kappa.shape[0] % 16 == 0
        )
        if fits:
            return patch_body(row_count, right_side, kappa)
        return body(right_side, kappa)

    return jax.shard_map(
        local, mesh=mesh, in_specs=placed, out_specs=P("tm", "row", None), check_vma=False
    )
```
